128 devices in a mesh: grp: 8 (over x, core), seq: 16 (over z, y).
Axes of the slice: x: 4, y: 4, z: 4, core: 2. Of those that a mesh axis runs over, the one named last changes fastest.
Arguments:
- image_queries: bfloat16 [98304, 768], P(('grp', 'seq')), may hold values from -6 to 6
- image_keys: bfloat16 [98304, 768], P(('grp', 'seq')), may hold values from -6 to 6
- image_values: bfloat16 [98304, 768], P(('grp', 'seq')), may hold values from -6 to 6
- cotangent: bfloat16 [98304, 768], P(('grp', 'seq')), may hold values from -6 to 6
- text_keys: bfloat16 [8, 128, 768], P('grp'), may hold values from -6 to 6
- text_values: bfloat16 [8, 128, 768], P('grp'), may hold values from -6 to 6
- text_lengths: int32 [8], P('grp'), may hold values from 32 to 128, as said below
- send_owner: int32 [128, 6], P(('grp', 'seq')), may hold values from 0 to 15, as said below
- recv_source: int32 [128, 6], P(('grp', 'seq')), may hold values from 0 to 15, as said below
- tile_counts: int32 [128, 3], P(('grp', 'seq')), may hold values from 1 to 3, 6 in all within a row
- caption_ids: int32 [128, 3], P(('grp', 'seq')), may hold values from 0 to 7
Outputs:
- attended: bfloat16 [98304, 768], P(('grp', 'seq'))
- grad_queries: bfloat16 [98304, 768], P(('grp', 'seq'))
- grad_keys: bfloat16 [98304, 768], P(('grp', 'seq'))
- grad_values: bfloat16 [98304, 768], P(('grp', 'seq'))
- grad_text_keys: bfloat16 [8, 128, 768], P('grp')
- grad_text_values: bfloat16 [8, 128, 768], P('grp')
The draws below stay inside these ranges and needn't reach their ends.
Inputs may be any that keep to these rules, and one draw needn't show every extreme that they name: `send_owner`: within one index of grp, each device sends at most one tile to each owner, and every owner receives exactly 6 tiles, one for each slot, consistent with recv_source. Consistent with send_owner: slot r of owner o is filled by the tile of device recv_source[o, r] whose send_owner entry is o. `text_lengths`: each caption has at least a quarter of its tokens live, and some caption has all 128.
All inputs are finite; a program needn't handle non-finite values.
Results may differ from the reference program's by a relative error of at most 0.008.
Values may be sent and summed in bfloat16 or wider, within the bound.
A program may use at most 192 MiB of HBM per device.

```python
import math
import jax
import jax.numpy as jnp
import numpy as np
from jax import lax

HEAD_DIM = 64
WIDTH = 768
TILE = 128
TILES_DEV = 6
TOKENS = 98304
MOST_TILES = 3
IMGS = 3
TXT = 128
NCAP = 8
N_GRP = 8
N_SEQ = 16
DEVICES = 128


def row_tables(key):
    offsets = jax.random.permutation(jax.random.fold_in(key, 1), N_SEQ)[:TILES_DEV]
    local_keys = jax.random.split(jax.random.fold_in(key, 2), N_SEQ)
    slot_keys = jax.random.split(jax.random.fold_in(key, 3), N_SEQ)
    local_order = jax.vmap(lambda given: jax.random.permutation(given, TILES_DEV))(local_keys)
    slot_order = jax.vmap(lambda given: jax.random.permutation(given, TILES_DEV))(slot_keys)
    places = jnp.arange(N_SEQ, dtype=jnp.int32)[:, None]
    owner_of_request = (places + offsets[None, :]) % N_SEQ
    source_of_request = (places - offsets[None, :]) % N_SEQ
    inverse_local = jnp.argsort(local_order, axis=1)
    inverse_slot = jnp.argsort(slot_order, axis=1)
    send_table = jnp.take_along_axis(owner_of_request, inverse_local, axis=1)
    recv_table = jnp.take_along_axis(source_of_request, inverse_slot, axis=1)
    return (send_table, recv_table)


def routing(key):

    def one_row(index):
        return row_tables(jax.random.fold_in(key, index))
    send_table, recv_table = jax.vmap(one_row)(jnp.arange(N_GRP, dtype=jnp.int32))
    return (send_table.reshape(N_GRP * N_SEQ, TILES_DEV).astype(jnp.int32), recv_table.reshape(N_GRP * N_SEQ, TILES_DEV).astype(jnp.int32))


def draw_send_owner(key, part):
    tables = routing(key)
    return tables[0]


def draw_recv_source(key, part):
    tables = routing(key)
    return tables[1]


def draw_image_queries(key, part):
    key = jax.random.fold_in(key, 21)
    return jnp.clip(jax.random.normal(key, (TOKENS, WIDTH), jnp.float32), -4.5, 4.5).astype(jnp.bfloat16)


def draw_image_keys(key, part):
    key = jax.random.fold_in(key, 22)
    return jnp.clip(jax.random.normal(key, (TOKENS, WIDTH), jnp.float32), -4.5, 4.5).astype(jnp.bfloat16)


def draw_text_lengths(key, part):
    key = jax.random.fold_in(key, 5)
    drawn = jax.random.randint(jax.random.fold_in(key, 1), (NCAP,), TXT // 4, TXT + 1)
    full_one = jax.random.randint(jax.random.fold_in(key, 2), (), 0, NCAP)
    return jnp.where(jnp.arange(NCAP) == full_one, TXT, drawn).astype(jnp.int32)


def plant(values, stream_key, low, top_value):
    extent = values.shape
    index_at = [jax.random.randint(jax.random.fold_in(stream_key, axis), (), 0, extent[axis]) for axis in range(len(extent))]
    values = values.at[tuple(index_at)].set(low)
    longest = extent.index(max(extent))
    index_at[longest] = (index_at[longest] + 1) % extent[longest]
    return values.at[tuple(index_at)].set(top_value)


def block_scale(stream_key, shape, shards, least, top_value):
    factor_of, own = 1.0, jax.random.fold_in(stream_key, 6)
    for dim, parts in shards:
        steps = jnp.exp(jax.random.uniform(jax.random.fold_in(own, dim), (parts,), jnp.float32, least / len(shards), top_value / len(shards)))
        factor_of = factor_of * jnp.repeat(steps, shape[dim] // parts).reshape([-1 if axis == dim else 1 for axis in range(len(shape))])
    return factor_of


def profile(amount, total, bound, skew):
    loads = [(1 << 20) // math.isqrt(rank ** skew) + 1 for rank in range(2, amount + 1)]
    spare, counts = total - bound - (amount - 1), [1] * (amount - 1)
    while spare > 0:
        movable = [i for i in range(amount - 1) if counts[i] < bound]
        whole, left = sum([loads[i] for i in movable]), spare
        for i in movable:
            extra = min(bound - counts[i], max(1, left * loads[i] // whole), spare)
            counts[i] = counts[i] + extra
            spare = spare - extra
    return np.array([bound] + counts)


def ragged(key, amount, total, limit, slope):
    if amount == 2:
        one = jax.random.randint(key, (), max(1, total - limit), min(limit, total - 1) + 1)
        return jnp.stack([one, total - one])
    sizes = jnp.asarray(profile(amount, total, limit, slope), jnp.int32)
    couples = (amount - 1) // 2
    giver, receiver = sizes[1:1 + 2 * couples:2], sizes[2:2 + 2 * couples:2]
    slack = jnp.minimum(giver - 1, limit - receiver)
    moved = jax.random.randint(jax.random.fold_in(key, 1), (couples,), 0, 1 << 20) % (slack + 1)
    sizes = sizes.at[1:1 + 2 * couples:2].set(giver - moved).at[2:2 + 2 * couples:2].set(receiver + moved)
    return sizes[jax.random.permutation(jax.random.fold_in(key, 2), amount)]


def gaussian(own_key, dims, spread, limit, pieces=(), kind=jnp.bfloat16):
    values = spread * jax.random.normal(own_key, dims, jnp.float32)
    if pieces:
        values = values * block_scale(own_key, dims, pieces, -0.22, 0.18)
    return jnp.clip(values, -limit, limit).astype(kind)


def setup_inputs(seed: int = 0) -> dict:
    seeds = jax.random.split(jax.random.key(seed), 12)
    image_queries = draw_image_queries(jax.random.fold_in(seeds[11], 71), 0)
    image_keys = draw_image_keys(jax.random.fold_in(seeds[11], 71), 0)
    image_values = gaussian(seeds[2], (TOKENS, WIDTH), 1.0, 6.0, ((0, 128),))
    cotangent = gaussian(seeds[3], (TOKENS, WIDTH), 1.0, 6.0, ((0, 128),))
    text_keys = gaussian(seeds[4], (NCAP, TXT, WIDTH), 1.0, 6.0, ((0, 8),))
    text_values = gaussian(seeds[5], (NCAP, TXT, WIDTH), 1.0, 6.0, ((0, 8),))
    text_lengths = draw_text_lengths(jax.random.fold_in(seeds[11], 71), 0)
    send_owner = draw_send_owner(jax.random.fold_in(seeds[11], 71), 0)
    recv_source = draw_recv_source(jax.random.fold_in(seeds[11], 71), 0)
    tile_counts = jax.vmap(lambda own: ragged(own, IMGS, TILES_DEV, MOST_TILES, 1))(jax.random.split(seeds[9], DEVICES)).reshape((DEVICES, IMGS)).astype(jnp.int32)
    caption_ids = plant(jax.random.randint(seeds[10], (DEVICES, IMGS), 0, NCAP), jax.random.fold_in(seeds[10], 1), 0, NCAP - 1).astype(jnp.int32)
    return {"image_queries": image_queries, "image_keys": image_keys, "image_values": image_values, "cotangent": cotangent, "text_keys": text_keys, "text_values": text_values, "text_lengths": text_lengths, "send_owner": send_owner, "recv_source": recv_source, "tile_counts": tile_counts, "caption_ids": caption_ids}


def owner_masks(image_tiles, image_captions, caption_lengths, row_count, tile_rows, text_rows):
    image_count = image_tiles.shape[0]
    image_ends = jnp.cumsum(image_tiles) * tile_rows
    position = jnp.arange(row_count, dtype=jnp.int32)
    segment = jnp.sum((position[:, None] >= image_ends[None, :-1]).astype(jnp.int32), axis=1)
    text_image = jnp.arange(image_count * text_rows, dtype=jnp.int32) // text_rows
    text_place = jnp.arange(image_count * text_rows, dtype=jnp.int32) % text_rows
    chosen = image_captions[:, None] == jnp.arange(caption_lengths.shape[0], dtype=jnp.int32)[None, :]
    caption_length = jnp.sum(jnp.where(chosen, caption_lengths[None, :], 0), axis=1)
    text_live = text_place < jnp.repeat(caption_length, text_rows)
    return segment, text_image, text_live, chosen


def owner_pass(owner_data, text_keys, text_values, text_lengths, score_scale):
    query_rows, key_rows, value_rows, grad_rows, image_tiles, image_captions = owner_data
    row_count, feature_width = query_rows.shape
    text_rows = text_keys.shape[1]
    image_count = image_tiles.shape[0]
    head_count = feature_width // HEAD_DIM
    segment, text_image, text_live, chosen = owner_masks(image_tiles, image_captions, text_lengths, row_count, TILE, text_rows)
    visible = jnp.concatenate([segment[:, None] == segment[None, :],
                               (segment[:, None] == text_image[None, :]) & text_live[None, :]], axis=1)
    key_all = jnp.concatenate([key_rows, text_keys[image_captions].reshape(image_count * text_rows, feature_width)], 0)
    value_all = jnp.concatenate([value_rows, text_values[image_captions].reshape(image_count * text_rows, feature_width)], 0)

    def heads_of(tensor):
        return tensor.astype(jnp.float32).reshape(tensor.shape[0], head_count, HEAD_DIM)

    query_f32 = heads_of(query_rows)
    key_f32 = heads_of(key_all)
    value_f32 = heads_of(value_all)
    grad_f32 = heads_of(grad_rows)
    best = lax.Precision.HIGHEST
    scores = jnp.einsum("qhd,khd->hqk", query_f32, key_f32, precision=best) * score_scale
    scores = jnp.where(visible[None], scores, -jnp.inf)
    weights = jnp.exp(scores - jnp.max(scores, axis=2, keepdims=True))
    prob_full = weights / jnp.sum(weights, axis=2, keepdims=True)
    prob_low = lax.optimization_barrier(prob_full.astype(jnp.bfloat16)).astype(jnp.float32)
    attended = jnp.einsum("hqk,khd->qhd", prob_low, value_f32, precision=best).reshape(row_count, feature_width).astype(jnp.bfloat16)
    grad_prob = jnp.einsum("qhd,khd->hqk", grad_f32, value_f32, precision=best)
    row_total = jnp.sum(prob_full * grad_prob, axis=2, keepdims=True)
    grad_score = lax.optimization_barrier((prob_full * (grad_prob - row_total)).astype(jnp.bfloat16)).astype(jnp.float32)
    grad_query = (jnp.einsum("hqk,khd->qhd", grad_score, key_f32, precision=best) * score_scale).reshape(row_count, feature_width).astype(jnp.bfloat16)
    grad_key_all = (jnp.einsum("hqk,qhd->khd", grad_score, query_f32, precision=best) * score_scale).reshape(-1, feature_width)
    grad_value_all = jnp.einsum("hqk,qhd->khd", prob_low, grad_f32, precision=best).reshape(-1, feature_width)
    return (attended, grad_query,
            grad_key_all[:row_count].astype(jnp.bfloat16), grad_value_all[:row_count].astype(jnp.bfloat16),
            grad_key_all[row_count:].reshape(image_count, text_rows, feature_width),
            grad_value_all[row_count:].reshape(image_count, text_rows, feature_width))


def reference(image_queries, image_keys, image_values, cotangent, text_keys, text_values, text_lengths,
              send_owner, recv_source, tile_counts, caption_ids):
    device_count, tile_count = send_owner.shape
    feature_width = image_queries.shape[1]
    text_rows = text_keys.shape[1]
    score_scale = HEAD_DIM ** -0.5
    owner_ids = jnp.arange(device_count, dtype=jnp.int32)
    source_ids = (owner_ids // N_SEQ * N_SEQ)[:, None] + recv_source
    matched = send_owner[source_ids] == (owner_ids % N_SEQ)[:, None, None]
    local_tile = jnp.sum(jnp.where(matched, jnp.arange(tile_count, dtype=jnp.int32)[None, None, :], 0), axis=2)
    flat_tile = (source_ids * tile_count + local_tile).reshape(-1).astype(jnp.int32)

    def to_owner(tensor):
        return tensor.reshape(device_count * tile_count, TILE, feature_width)[flat_tile].reshape(device_count, tile_count * TILE, feature_width)

    def one_owner(owner_data):
        return owner_pass(owner_data, text_keys, text_values, text_lengths, score_scale)

    results = lax.map(one_owner, (to_owner(image_queries), to_owner(image_keys), to_owner(image_values),
                                  to_owner(cotangent), tile_counts, caption_ids))

    def to_source(tensor):
        placed = jnp.zeros((device_count * tile_count, TILE, feature_width), tensor.dtype)
        placed = placed.at[flat_tile].set(tensor.reshape(device_count * tile_count, TILE, feature_width))
        return placed.reshape(-1, feature_width)

    caption_list = caption_ids.reshape(-1).astype(jnp.int32)
    caption_count = text_keys.shape[0]
    grad_text_keys = jax.ops.segment_sum(results[4].reshape(-1, text_rows, feature_width), caption_list,
                                         num_segments=caption_count).astype(jnp.bfloat16)
    grad_text_values = jax.ops.segment_sum(results[5].reshape(-1, text_rows, feature_width), caption_list,
                                           num_segments=caption_count).astype(jnp.bfloat16)
    return (to_source(results[0]), to_source(results[1]), to_source(results[2]), to_source(results[3]),
            grad_text_keys, grad_text_values)
```

```python
import functools

import jax
import jax.numpy as jnp
from jax import lax
from jax.experimental import pallas as pl
from jax.experimental.pallas import tpu as pltpu
from jax.sharding import PartitionSpec as P

HEAD_DIM = 64
LANES = 128
TILE = 128
MESH = pl.DeviceIdType.MESH

RING = 4
SLOTS = 4
RELAY = 2

OWN = 0
DIRECT = 9
FORWARD = 17
FINAL = 21
PASSING = 29
POOL = 33

P_SEND = 0
P_MID = 8
P_LATE = 16
P_IMAGE = 20
P_BACK = 32
P_BACK_MID = 40
P_BACK_LATE = 48
P_HOME = 52
P_SIZE = 64

T_RECV, T_COUNT, T_CAPTION, T_LENGTH = 6, 12, 15, 18

SEND, PASS, MID, LATE = range(4)


def plan_kernel(tab_ref, row_ref, out_ref):
    g = lax.axis_index("grp")
    me = lax.axis_index("seq")
    peers = 16
    tab = tab_ref[pl.ds(pl.multiple_of(g * peers, peers), peers), :]
    src = lax.broadcasted_iota(jnp.int32, (peers, LANES), 0)
    own = lax.broadcasted_iota(jnp.int32, (peers, LANES), 1)
    sends = jnp.zeros((peers, LANES), jnp.int32)
    place = jnp.zeros((peers, LANES), jnp.int32)
    for j in range(6):
        hit = (tab[:, j : j + 1] == own).astype(jnp.int32)
        sends += hit
        place += hit * j
    first = row_ref[0, T_COUNT]
    second = first + row_ref[0, T_COUNT + 1]
    result = jnp.zeros((peers, LANES), jnp.int32)
    padded = []
    for r in range(6):
        image = jnp.where(r >= first, 1, 0) + jnp.where(r >= second, 1, 0)
        begin = jnp.where(r >= second, second, jnp.where(r >= first, first, 0))
        where_r = image * 3 + r - begin
        padded.append(where_r)
        result += jnp.where(src == row_ref[0, T_RECV + r], where_r, 0)

    lower = (
        lax.broadcasted_iota(jnp.int32, (peers, peers), 1)
        < lax.broadcasted_iota(jnp.int32, (peers, peers), 0)
    ).astype(jnp.float32)
    upper = (
        lax.broadcasted_iota(jnp.int32, (LANES, LANES), 0)
        < lax.broadcasted_iota(jnp.int32, (LANES, LANES), 1)
    ).astype(jnp.float32)
    live = sends > 0
    coord = {"y": lambda t: lax.rem(t, RING), "z": lambda t: lax.div(t, RING) % RING}

    def slots(step, axis):
        count, rank = [], []
        for d in (1, 2, 3):
            picked = jnp.where(live & (step == d), 1.0, 0.0)
            if axis == 1:
                before = jnp.dot(picked, upper, preferred_element_type=jnp.float32)
            else:
                before = jnp.dot(lower, picked, preferred_element_type=jnp.float32)
            rank.append(before.astype(jnp.int32))
            count.append(jnp.sum(picked, axis=axis, keepdims=True).astype(jnp.int32))
        plus = jnp.minimum(jnp.minimum(RELAY, SLOTS - count[0]), count[1])
        code = jnp.where(
            step == 0,
            0,
            jnp.where(
                step == 1, 1, jnp.where(step == 3, 2, jnp.where(rank[1] < plus, 3, 4))
            ),
        )
        slot = jnp.where(
            code == 1,
            SLOTS - 1 - rank[0],
            jnp.where(
                code == 2,
                SLOTS - 1 - rank[2],
                jnp.where(code == 3, rank[1], rank[1] - plus),
            ),
        )
        return code, slot

    def arrived(code, slot, stay, flip):
        base = (DIRECT + SLOTS, DIRECT, FORWARD + RELAY, FORWARD) if flip else (
            DIRECT, DIRECT + SLOTS, FORWARD, FORWARD + RELAY)
        return jnp.where(
            code == 0,
            stay,
            slot
            + jnp.where(
                code == 1,
                base[0],
                jnp.where(code == 2, base[1], jnp.where(code == 3, base[2], base[3])),
            ),
        )

    def settled(code, slot, stay, flip):
        odd = (code == 1) | (code == 3)
        near, far = (FINAL + SLOTS, FINAL) if flip else (FINAL, FINAL + SLOTS)
        return jnp.where(code == 0, stay, slot + jnp.where(odd, near, far))

    zero_row = jnp.zeros((1, LANES), jnp.float32)
    rows = []
    for ring_a, ring_b in (("y", "z"), ("z", "y")):
        at_a, at_b = coord[ring_a], coord[ring_b]
        src_a, src_b, own_a, own_b = at_a(src), at_b(src), at_a(own), at_b(own)
        me_a, me_b = at_a(me), at_b(me)
        code_a, slot_a = slots(lax.rem(own_a - src_a + RING, RING), 1)
        code_b, slot_b = slots(lax.rem(own_b - src_b + RING, RING), 0)
        there = arrived(code_a, slot_a, place, False)
        there_end = settled(code_b, slot_b, there, False)
        back = arrived(code_b, slot_b, result, True)
        back_end = settled(code_a, slot_a, back, True)
        mine_src = live & (src == me)
        mine_own = live & (own == me)
        crossing = live & (own_a == me_a) & (src_b == me_b)
        part = {}

        def put(entry, condition, value):
            row = jnp.sum(
                jnp.where(condition, value, 0).astype(jnp.float32), axis=0, keepdims=True
            )
            part[entry] = part[entry] + row if entry in part else row

        def channel(code, sign, flip):
            sign = 1 - sign if flip else sign
            return (code == 1 + sign), (code == 3 + sign)

        for sign in (0, 1):
            ahead = 1 if sign == 0 else RING - 1
            near, far = channel(code_a, sign, False)
            for k in range(SLOTS):
                put(P_SEND + sign * SLOTS + k, mine_src & (near | far) & (slot_a == k), place)
            near, far = channel(code_b, sign, False)
            passing = live & (own_a == me_a) & far & (lax.rem(own_b - me_b + RING, RING) == ahead)
            for k in range(RELAY):
                put(P_MID + sign * SLOTS + k, crossing & far & (slot_b == k), there)
                put(P_LATE + sign * RELAY + k, crossing & near & (slot_b == k), there)
                put(P_LATE + sign * RELAY + k, passing & (slot_b == k), PASSING + sign * RELAY + k)
            for k in range(RELAY, SLOTS):
                put(P_MID + sign * SLOTS + k, crossing & near & (slot_b == k), there)
            near, far = channel(code_b, sign, True)
            for k in range(SLOTS):
                put(P_BACK + sign * SLOTS + k, mine_own & (near | far) & (slot_b == k), result)
            near, far = channel(code_a, sign, True)
            passing = live & (src_b == me_b) & far & (lax.rem(src_a - me_a + RING, RING) == ahead)
            for k in range(RELAY):
                put(P_BACK_MID + sign * SLOTS + k, crossing & far & (slot_a == k), back)
                put(P_BACK_LATE + sign * RELAY + k, crossing & near & (slot_a == k), back)
                put(P_BACK_LATE + sign * RELAY + k, passing & (slot_a == k), PASSING + sign * RELAY + k)
            for k in range(RELAY, SLOTS):
                put(P_BACK_MID + sign * SLOTS + k, crossing & near & (slot_a == k), back)
        begins = (0, first, second)
        for i in range(3):
            for j in range(3):
                r = jnp.minimum(begins[i] + j, 5)
                put(P_IMAGE + i * 3 + j, mine_own & (src == row_ref[0, T_RECV + r]), there_end)
        for j in range(6):
            put(P_HOME + j, mine_src & (place == j), back_end)
        rows.extend(part.get(entry, zero_row) for entry in range(P_SIZE))
    matrix = jnp.concatenate(rows, axis=0)
    ones = jnp.ones((8, LANES), jnp.float32)
    out = lax.dot_general(ones, matrix, (((1,), (1,)), ((), ())), preferred_element_type=jnp.float32)
    out_ref[...] = out.astype(jnp.int32)


def main_kernel(
    peers_grp,
    pairs,
    plan,
    tab,
    queries,
    keys,
    values,
    grads,
    cap_keys,
    cap_values,
    out_rows,
    out_queries,
    out_keys,
    out_values,
    out_text,
    inb,
    txt,
    send_a,
    recv_a,
    recv_p,
    send_m,
    recv_m,
    send_l,
    recv_l,
    pool,
    res,
    stage,
    tsend,
    trecv,
    ttot,
    ssem,
    rsem,
    tssem,
    trsem,
    insem,
    outsem,
):
    g = lax.axis_index("grp")
    s = lax.axis_index("seq")
    z, y = lax.div(s, RING), lax.rem(s, RING)
    row = g * (RING * RING) + s
    sources = (queries, keys, values, grads)
    outs = (out_rows, out_queries, out_keys, out_values)

    def neighbour(ring, sign):
        step = 1 if sign == 0 else RING - 1
        if ring == "y":
            return (g, z * RING + lax.rem(y + step, RING))
        return (g, lax.rem(z + step, RING) * RING + y)

    def group_peer(k):
        return lax.rem(g + k, peers_grp)

    barrier = pltpu.get_barrier_semaphore()
    for ring in ("y", "z"):
        for sign in (0, 1):
            pl.semaphore_signal(barrier, inc=1, device_id=neighbour(ring, sign), device_id_type=MESH)
    for k in range(1, peers_grp):
        pl.semaphore_signal(barrier, inc=1, device_id=(group_peer(k), s), device_id_type=MESH)

    def message(io, par, ty, sign, kind):
        ring = "y" if (ty + io + (1 if kind >= MID else 0)) % 2 == 0 else "z"
        if kind == SEND:
            src, dst = send_a.at[io, ty, sign], recv_a.at[io, par, ty, sign]
        elif kind == PASS:
            src, dst = recv_a.at[io, par, ty, sign, pl.ds(0, RELAY)], recv_p.at[io, par, ty, sign]
        elif kind == MID:
            src, dst = send_m.at[io, ty, sign], recv_m.at[io, par, ty, sign]
        else:
            src, dst = send_l.at[io, ty, sign], recv_l.at[io, par, ty, sign]
        index = (((io * 2 + par) * 2 + ty) * 2 + sign) * 4 + kind
        return pltpu.make_async_remote_copy(
            src_ref=src,
            dst_ref=dst,
            send_sem=ssem.at[index],
            recv_sem=rsem.at[index],
            device_id=neighbour(ring, sign),
            device_id_type=MESH,
        )

    def text_message(par, ty, k):
        index = (par * 2 + ty) * (peers_grp - 1) + k - 1
        target = group_peer(k)
        return pltpu.make_async_remote_copy(
            src_ref=tsend.at[ty, target],
            dst_ref=trecv.at[par, ty, k - 1],
            send_sem=tssem.at[index],
            recv_sem=trsem.at[index],
            device_id=(target, s),
            device_id_type=MESH,
        )

    def columns(pair, ty):
        return pl.ds(pl.multiple_of((pair * 2 + ty) * LANES, LANES), LANES)

    def loads(pair):
        par = lax.rem(pair, 2)
        copies = []
        for ty in range(2):
            for a in range(4):
                copies.append(
                    pltpu.make_async_copy(
                        sources[a].at[:, columns(pair, ty)], inb.at[par, ty, a], insem.at[ty * 6 + a]
                    )
                )
        return copies

    def caption_loads(pair):
        copies = []
        for ty in range(2):
            for a, cap in enumerate((cap_keys, cap_values)):
                copies.append(
                    pltpu.make_async_copy(
                        cap.at[:, :, columns(pair, ty)], txt.at[ty, a], insem.at[ty * 6 + 4 + a]
                    )
                )
        return copies

    def stores(pair):
        copies = []
        for ty in range(2):
            for a in range(4):
                copies.append(
                    pltpu.make_async_copy(
                        stage.at[ty, a], outs[a].at[:, columns(pair, ty)], outsem.at[ty * 5 + a]
                    )
                )
            copies.append(
                pltpu.make_async_copy(
                    ttot.at[ty], out_text.at[:, :, columns(pair, ty)], outsem.at[ty * 5 + 4]
                )
            )
        return copies

    def fill(base, count, read):
        def step(k, carry):
            pool[base + k] = read(k)
            return carry

        lax.fori_loop(0, count, step, 0)

    def fill_own(io, par, ty):
        if io == 0:
            def step(j, carry):
                at = pl.ds(pl.multiple_of(j * TILE, TILE), TILE)
                for a in range(4):
                    pool[OWN + j, a] = inb[par, ty, a, at, :]
                return carry

            lax.fori_loop(0, 6, step, 0)
        else:
            fill(OWN, 9, lambda k: res[ty, k])

    def fill_arrived(io, par, ty):
        for sign in range(2):
            fill(DIRECT + sign * SLOTS, SLOTS, lambda k: recv_a[io, par, ty, sign, k])
            fill(FORWARD + sign * RELAY, RELAY, lambda k: recv_p[io, par, ty, sign, k])

    def fill_passing(io, par, ty):
        for sign in range(2):
            fill(PASSING + sign * RELAY, RELAY, lambda k: recv_m[io, par, ty, sign, k])

    def fill_final(io, par, ty):
        for sign in range(2):
            fill(FINAL + sign * SLOTS, RELAY, lambda k: recv_l[io, par, ty, sign, k])
            fill(
                FINAL + sign * SLOTS + RELAY,
                SLOTS - RELAY,
                lambda k: recv_m[io, par, ty, sign, RELAY + k],
            )

    def choose(ref, io, ty, entry, count):
        for sign in range(2):
            def step(k, carry):
                ref[io, ty, sign, k] = pool[plan[0, ty * P_SIZE + entry + sign * count + k]]
                return carry

            lax.fori_loop(0, count, step, 0)

    def begin(io, par, ty, kind):
        for sign in range(2):
            message(io, par, ty, sign, kind).start()

    def finish(io, par, ty, kind):
        for sign in range(2):
            message(io, par, ty, sign, kind).wait()

    def first_send(io, par, ty):
        fill_own(io, par, ty)
        choose(send_a, io, ty, P_BACK if io else P_SEND, SLOTS)
        begin(io, par, ty, SEND)

    def pass_on(io, par):
        for ty in range(2):
            finish(io, par, ty, SEND)
            begin(io, par, ty, PASS)

    def turn(io, par):
        for ty in range(2):
            finish(io, par, ty, PASS)
            fill_own(io, par, ty)
            fill_arrived(io, par, ty)
            choose(send_m, io, ty, P_BACK_MID if io else P_MID, SLOTS)
            begin(io, par, ty, MID)

    def last_send(io, par):
        for ty in range(2):
            finish(io, par, ty, MID)
            fill_own(io, par, ty)
            fill_arrived(io, par, ty)
            fill_passing(io, par, ty)
            choose(send_l, io, ty, P_BACK_LATE if io else P_LATE, RELAY)
            begin(io, par, ty, LATE)

    def compute(ty):
        tsend[ty] = jnp.zeros(tsend.shape[1:], tsend.dtype)

        def image(i, carry):
            tiles = tab[row, T_COUNT + i]
            caption = tab[row, T_CAPTION + i]
            length = tab[caption * (RING * RING), T_LENGTH]
            at = [plan[0, ty * P_SIZE + P_IMAGE + i * 3 + j] for j in range(3)]
            q = jnp.concatenate([pool[p, 0] for p in at], axis=0)
            k = jnp.concatenate([pool[p, 1] for p in at] + [txt[ty, 0, caption]], axis=0)
            v = jnp.concatenate([pool[p, 2] for p in at] + [txt[ty, 1, caption]], axis=0)
            do = jnp.concatenate([pool[p, 3] for p in at], axis=0)
            rows_q, rows_k = q.shape[0], k.shape[0]
            q_row = lax.broadcasted_iota(jnp.int32, (rows_q, LANES), 0)
            do = jnp.where(q_row < tiles * TILE, do, jnp.zeros_like(do))
            q = q * jnp.asarray(HEAD_DIM**-0.5, q.dtype)
            k_row = lax.broadcasted_iota(jnp.int32, (rows_k, LANES), 0)
            seen = (k_row < tiles * TILE) | ((k_row >= rows_q) & (k_row < rows_q + length))
            bias = jnp.where(seen, 0.0, -1e30)
            bias = jnp.concatenate([bias] * (rows_q // LANES), axis=1)
            lane_q = lax.broadcasted_iota(jnp.int32, (rows_q, LANES), 1) < HEAD_DIM
            lane_k = lax.broadcasted_iota(jnp.int32, (rows_k, LANES), 1) < HEAD_DIM
            k_t = k.T
            v_t = v.T
            o_parts, dq_parts, dk_parts, dv_parts = [], [], [], []
            contract_lanes = (((1,), (1,)), ((), ()))
            f32 = jnp.float32
            for h in range(2):
                keep = lane_q if h == 0 else jnp.logical_not(lane_q)
                q_h = jnp.where(keep, q, jnp.zeros_like(q))
                do_h = jnp.where(keep, do, jnp.zeros_like(do))
                scores = lax.dot_general(k, q_h, contract_lanes, preferred_element_type=f32) + bias
                weights = jnp.exp(scores - jnp.max(scores, axis=0, keepdims=True))
                probs = weights * (1.0 / jnp.sum(weights, axis=0, keepdims=True))
                dprobs = lax.dot_general(v, do_h, contract_lanes, preferred_element_type=f32)
                total = jnp.sum(probs * dprobs, axis=0, keepdims=True)
                dscores = (probs * (dprobs - total)).astype(jnp.bfloat16)
                low = probs.astype(jnp.bfloat16)
                span = slice(h * HEAD_DIM, (h + 1) * HEAD_DIM)
                o_parts.append(jnp.dot(v_t[span], low, preferred_element_type=f32))
                dq_parts.append(jnp.dot(k_t[span], dscores, preferred_element_type=f32))
                dk_parts.append(jnp.dot(dscores, q, preferred_element_type=f32))
                dv_parts.append(jnp.dot(low, do, preferred_element_type=f32))
            o = jnp.concatenate(o_parts, axis=0).T.astype(jnp.bfloat16)
            dq = (jnp.concatenate(dq_parts, axis=0).T * HEAD_DIM**-0.5).astype(jnp.bfloat16)
            dk = jnp.where(lane_k, dk_parts[0], dk_parts[1])
            dv = jnp.where(lane_k, dv_parts[0], dv_parts[1])
            for j in range(3):
                rows = slice(j * TILE, (j + 1) * TILE)
                res[ty, i * 3 + j, 0] = o[rows]
                res[ty, i * 3 + j, 1] = dq[rows]
                res[ty, i * 3 + j, 2] = dk[rows].astype(jnp.bfloat16)
                res[ty, i * 3 + j, 3] = dv[rows].astype(jnp.bfloat16)
            dk_text, dv_text = dk[rows_q:], dv[rows_q:]

            def spread(c, inner):
                hit = jnp.where(caption == c, 1.0, 0.0)
                tsend[ty, c, 0] += dk_text * hit
                tsend[ty, c, 1] += dv_text * hit
                return inner

            lax.fori_loop(0, peers_grp, spread, 0)
            return carry

        lax.fori_loop(0, 3, image, 0)

    def work(pair):
        par = lax.rem(pair, 2)
        for copy in caption_loads(pair):
            copy.wait()
        for ty in range(2):
            finish(0, par, ty, LATE)
            fill_own(0, par, ty)
            fill_arrived(0, par, ty)
            fill_final(0, par, ty)
            compute(ty)
            first_send(1, par, ty)
            for k in range(1, peers_grp):
                text_message(par, ty, k).start()

    def home(pair):
        par = lax.rem(pair, 2)

        @pl.when(pair > 0)
        def _():
            for copy in stores(pair - 1):
                copy.wait()

        for ty in range(2):
            finish(1, par, ty, LATE)
            fill_own(1, par, ty)
            fill_arrived(1, par, ty)
            fill_final(1, par, ty)

            def place(j, carry):
                at = pl.ds(pl.multiple_of(j * TILE, TILE), TILE)
                for a in range(4):
                    stage[ty, a, at, :] = pool[plan[0, ty * P_SIZE + P_HOME + j], a]
                return carry

            lax.fori_loop(0, 6, place, 0)
            for k in range(1, peers_grp):
                text_message(par, ty, k).wait()
            total = tsend[ty, g]
            for k in range(1, peers_grp):
                total = total + trecv[par, ty, k - 1]
            ttot[ty] = total
        for copy in stores(pair):
            copy.start()

    for copy in loads(0):
        copy.start()
    pl.semaphore_wait(barrier, 4 + peers_grp - 1)

    def superstep(step, carry):
        entering = step < pairs
        working = (step >= 1) & (step <= pairs)
        par_in = lax.rem(step, 2)
        par_out = lax.rem(step + 1, 2)

        @pl.when(step >= 2)
        def _():
            home(step - 2)

        @pl.when(entering)
        def _():
            for copy in loads(step):
                copy.wait()
            for ty in range(2):
                first_send(0, par_in, ty)

        @pl.when(working)
        def _():
            work(step - 1)

        @pl.when(step + 1 < pairs)
        def _():
            for copy in loads(step + 1):
                copy.start()

        @pl.when(entering)
        def _():
            for copy in caption_loads(step):
                copy.start()

        @pl.when(working)
        def _():
            pass_on(1, par_out)

        @pl.when(entering)
        def _():
            pass_on(0, par_in)

        @pl.when(working)
        def _():
            turn(1, par_out)

        @pl.when(entering)
        def _():
            turn(0, par_in)

        @pl.when(working)
        def _():
            last_send(1, par_out)

        @pl.when(entering)
        def _():
            last_send(0, par_in)

        return carry

    lax.fori_loop(0, pairs + 2, superstep, 0)
    for copy in stores(pairs - 1):
        copy.wait()


def body(
    image_queries,
    image_keys,
    image_values,
    cotangent,
    text_keys,
    text_values,
    text_lengths,
    send_owner,
    recv_source,
    tile_counts,
    caption_ids,
):
    rows, width = image_queries.shape
    peers_grp = lax.axis_size("grp")
    pairs = width // (2 * LANES)
    mine = jnp.concatenate(
        [send_owner[0], recv_source[0], tile_counts[0], caption_ids[0], text_lengths]
    ).astype(jnp.int32)
    mine = jnp.pad(mine, (0, LANES - mine.shape[0]))[None, :]
    table = lax.all_gather(mine, ("grp", "seq"), axis=0, tiled=True)
    all_keys = lax.all_gather(text_keys, "grp", axis=0, tiled=True)
    all_values = lax.all_gather(text_values, "grp", axis=0, tiled=True)
    vmem = pl.BlockSpec(memory_space=pltpu.VMEM)
    smem = pl.BlockSpec(memory_space=pltpu.SMEM)
    anywhere = pl.BlockSpec(memory_space=pl.ANY)
    plan = pl.pallas_call(
        plan_kernel,
        out_shape=jax.ShapeDtypeStruct((8, 2 * P_SIZE), jnp.int32),
        in_specs=[vmem, smem],
        out_specs=vmem,
        name="plan",
    )(table, mine)
    bf16, f32 = jnp.bfloat16, jnp.float32
    quad = (4, TILE, LANES)
    text_rows = text_keys.shape[1]
    image = jax.ShapeDtypeStruct((rows, width), bf16)
    scratch = [
        pltpu.VMEM((2, 2, 4, rows, LANES), bf16),
        pltpu.VMEM((2, 2, peers_grp, text_rows, LANES), bf16),
        pltpu.VMEM((2, 2, 2, SLOTS) + quad, bf16),
        pltpu.VMEM((2, 2, 2, 2, SLOTS) + quad, bf16),
        pltpu.VMEM((2, 2, 2, 2, RELAY) + quad, bf16),
        pltpu.VMEM((2, 2, 2, SLOTS) + quad, bf16),
        pltpu.VMEM((2, 2, 2, 2, SLOTS) + quad, bf16),
        pltpu.VMEM((2, 2, 2, RELAY) + quad, bf16),
        pltpu.VMEM((2, 2, 2, 2, RELAY) + quad, bf16),
        pltpu.VMEM((POOL,) + quad, bf16),
        pltpu.VMEM((2, 9) + quad, bf16),
        pltpu.VMEM((2, 4, rows, LANES), bf16),
        pltpu.VMEM((2, peers_grp, 2, text_rows, LANES), f32),
        pltpu.VMEM((2, 2, peers_grp - 1, 2, text_rows, LANES), f32),
        pltpu.VMEM((2, 2, text_rows, LANES), f32),
        pltpu.SemaphoreType.DMA((64,)),
        pltpu.SemaphoreType.DMA((64,)),
        pltpu.SemaphoreType.DMA((4 * (peers_grp - 1),)),
        pltpu.SemaphoreType.DMA((4 * (peers_grp - 1),)),
        pltpu.SemaphoreType.DMA((12,)),
        pltpu.SemaphoreType.DMA((10,)),
    ]
    attended, grad_queries, grad_keys, grad_values, text = pl.pallas_call(
        functools.partial(main_kernel, peers_grp, pairs),
        out_shape=(image, image, image, image, jax.ShapeDtypeStruct((2, text_rows, width), f32)),
        in_specs=[smem, smem] + [anywhere] * 6,
        out_specs=(anywhere,) * 5,
        scratch_shapes=scratch,
        compiler_params=pltpu.CompilerParams(
            collective_id=0, has_side_effects=True, vmem_limit_bytes=63 * 2**20
        ),
        name="attend",
    )(plan, table, image_queries, image_keys, image_values, cotangent, all_keys, all_values)
    text = lax.psum(text, "seq").astype(bf16)
    return attended, grad_queries, grad_keys, grad_values, text[:1], text[1:]


def solution(mesh):
    tokens = P(("grp", "seq"), None)
    captions = P("grp", None, None)
    return jax.shard_map(
        body,
        mesh=mesh,
        in_specs=(tokens,) * 4 + (captions, captions, P("grp")) + (tokens,) * 4,
        out_specs=(tokens,) * 4 + (captions, captions),
        check_vma=False,
    )
```

```python
import functools

import jax
import jax.numpy as jnp
from jax import lax
from jax.experimental import pallas as pl
from jax.experimental.pallas import tpu as pltpu
from jax.sharding import PartitionSpec as P

HEAD_DIM = 64
LANES = 128
TILE = 128
MESH = pl.DeviceIdType.MESH

RING = 4
SLOTS = 4
RELAY = 2

OWN = 0
DIRECT = 9
FORWARD = 17
FINAL = 21
PASSING = 29
POOL = 33

P_SEND = 0
P_MID = 8
P_LATE = 16
P_IMAGE = 20
P_BACK = 32
P_BACK_MID = 40
P_BACK_LATE = 48
P_HOME = 52
P_LENGTH = 58
P_SIZE = 64

T_RECV, T_COUNT, T_CAPTION, T_LENGTH = 6, 12, 15, 18

SEND, PASS, MID, LATE = range(4)


def make_plan(tab, row_ref, lengths, me):
    peers = tab.shape[0]
    src = lax.broadcasted_iota(jnp.int32, (peers, LANES), 0)
    own = lax.broadcasted_iota(jnp.int32, (peers, LANES), 1)
    sends = jnp.zeros((peers, LANES), jnp.int32)
    place = jnp.zeros((peers, LANES), jnp.int32)
    for j in range(6):
        hit = (tab[:, j : j + 1] == own).astype(jnp.int32)
        sends += hit
        place += hit * j
    first = row_ref[0, T_COUNT]
    second = first + row_ref[0, T_COUNT + 1]
    result = jnp.zeros((peers, LANES), jnp.int32)
    padded = []
    for r in range(6):
        image = jnp.where(r >= first, 1, 0) + jnp.where(r >= second, 1, 0)
        begin = jnp.where(r >= second, second, jnp.where(r >= first, first, 0))
        where_r = image * 3 + r - begin
        padded.append(where_r)
        result += jnp.where(src == row_ref[0, T_RECV + r], where_r, 0)

    lower = (
        lax.broadcasted_iota(jnp.int32, (peers, peers), 1)
        < lax.broadcasted_iota(jnp.int32, (peers, peers), 0)
    ).astype(jnp.float32)
    upper = (
        lax.broadcasted_iota(jnp.int32, (LANES, LANES), 0)
        < lax.broadcasted_iota(jnp.int32, (LANES, LANES), 1)
    ).astype(jnp.float32)
    live = sends > 0
    coord = {"y": lambda t: lax.rem(t, RING), "z": lambda t: lax.div(t, RING) % RING}

    def slots(step, axis):
        count, rank = [], []
        for d in (1, 2, 3):
            picked = jnp.where(live & (step == d), 1.0, 0.0)
            if axis == 1:
                before = jnp.dot(picked, upper, preferred_element_type=jnp.float32)
            else:
                before = jnp.dot(lower, picked, preferred_element_type=jnp.float32)
            rank.append(before.astype(jnp.int32))
            count.append(jnp.sum(picked, axis=axis, keepdims=True).astype(jnp.int32))
        plus = jnp.minimum(jnp.minimum(RELAY, SLOTS - count[0]), count[1])
        code = jnp.where(
            step == 0,
            0,
            jnp.where(
                step == 1, 1, jnp.where(step == 3, 2, jnp.where(rank[1] < plus, 3, 4))
            ),
        )
        slot = jnp.where(
            code == 1,
            SLOTS - 1 - rank[0],
            jnp.where(
                code == 2,
                SLOTS - 1 - rank[2],
                jnp.where(code == 3, rank[1], rank[1] - plus),
            ),
        )
        return code, slot

    def arrived(code, slot, stay, flip):
        base = (DIRECT + SLOTS, DIRECT, FORWARD + RELAY, FORWARD) if flip else (
            DIRECT, DIRECT + SLOTS, FORWARD, FORWARD + RELAY)
        return jnp.where(
            code == 0,
            stay,
            slot
            + jnp.where(
                code == 1,
                base[0],
                jnp.where(code == 2, base[1], jnp.where(code == 3, base[2], base[3])),
            ),
        )

    def settled(code, slot, stay, flip):
        odd = (code == 1) | (code == 3)
        near, far = (FINAL + SLOTS, FINAL) if flip else (FINAL, FINAL + SLOTS)
        return jnp.where(code == 0, stay, slot + jnp.where(odd, near, far))

    zero_row = jnp.zeros((1, LANES), jnp.float32)
    rows = []
    for ring_a, ring_b in (("y", "z"), ("z", "y")):
        at_a, at_b = coord[ring_a], coord[ring_b]
        src_a, src_b, own_a, own_b = at_a(src), at_b(src), at_a(own), at_b(own)
        me_a, me_b = at_a(me), at_b(me)
        code_a, slot_a = slots(lax.rem(own_a - src_a + RING, RING), 1)
        code_b, slot_b = slots(lax.rem(own_b - src_b + RING, RING), 0)
        there = arrived(code_a, slot_a, place, False)
        there_end = settled(code_b, slot_b, there, False)
        back = arrived(code_b, slot_b, result, True)
        back_end = settled(code_a, slot_a, back, True)
        mine_src = live & (src == me)
        mine_own = live & (own == me)
        crossing = live & (own_a == me_a) & (src_b == me_b)
        part = {}

        def put(entry, condition, value):
            row = jnp.sum(
                jnp.where(condition, value, 0).astype(jnp.float32), axis=0, keepdims=True
            )
            part[entry] = part[entry] + row if entry in part else row

        def channel(code, sign, flip):
            sign = 1 - sign if flip else sign
            return (code == 1 + sign), (code == 3 + sign)

        for sign in (0, 1):
            ahead = 1 if sign == 0 else RING - 1
            near, far = channel(code_a, sign, False)
            for k in range(SLOTS):
                put(P_SEND + sign * SLOTS + k, mine_src & (near | far) & (slot_a == k), place)
            near, far = channel(code_b, sign, False)
            passing = live & (own_a == me_a) & far & (lax.rem(own_b - me_b + RING, RING) == ahead)
            for k in range(RELAY):
                put(P_MID + sign * SLOTS + k, crossing & far & (slot_b == k), there)
                put(P_LATE + sign * RELAY + k, crossing & near & (slot_b == k), there)
                put(P_LATE + sign * RELAY + k, passing & (slot_b == k), PASSING + sign * RELAY + k)
            for k in range(RELAY, SLOTS):
                put(P_MID + sign * SLOTS + k, crossing & near & (slot_b == k), there)
            near, far = channel(code_b, sign, True)
            for k in range(SLOTS):
                put(P_BACK + sign * SLOTS + k, mine_own & (near | far) & (slot_b == k), result)
            near, far = channel(code_a, sign, True)
            passing = live & (src_b == me_b) & far & (lax.rem(src_a - me_a + RING, RING) == ahead)
            for k in range(RELAY):
                put(P_BACK_MID + sign * SLOTS + k, crossing & far & (slot_a == k), back)
                put(P_BACK_LATE + sign * RELAY + k, crossing & near & (slot_a == k), back)
                put(P_BACK_LATE + sign * RELAY + k, passing & (slot_a == k), PASSING + sign * RELAY + k)
            for k in range(RELAY, SLOTS):
                put(P_BACK_MID + sign * SLOTS + k, crossing & near & (slot_a == k), back)
        begins = (0, first, second)
        for i in range(3):
            for j in range(3):
                r = jnp.minimum(begins[i] + j, 5)
                put(P_IMAGE + i * 3 + j, mine_own & (src == row_ref[0, T_RECV + r]), there_end)
        for j in range(6):
            put(P_HOME + j, mine_src & (place == j), back_end)
        if lengths is not None:
            captions = lax.broadcasted_iota(jnp.int32, lengths.shape, 0)
            column = lax.broadcasted_iota(jnp.int32, lengths.shape, 1) == T_LENGTH
            for i in range(3):
                put(P_LENGTH + i, column & (captions == row_ref[0, T_CAPTION + i]), lengths)
        rows.extend(part.get(entry, zero_row) for entry in range(P_SIZE))
    matrix = jnp.concatenate(rows, axis=0)
    ones = jnp.ones((8, LANES), jnp.float32)
    out = lax.dot_general(ones, matrix, (((1,), (1,)), ((), ())), preferred_element_type=jnp.float32)
    out = out.astype(jnp.int32)
    entry = lax.broadcasted_iota(jnp.int32, out.shape, 1) % P_SIZE
    return jnp.where(entry < P_LENGTH, jnp.clip(out, 0, POOL - 1), out)


def main_kernel(
    peers_grp,
    peers_seq,
    pairs,
    mine,
    mine_rows,
    queries,
    keys,
    values,
    grads,
    cap_keys,
    cap_values,
    out_rows,
    out_queries,
    out_keys,
    out_values,
    out_cap_keys,
    out_cap_values,
    tab_seq,
    tab_grp,
    plan_rows,
    plan_own,
    plan,
    inb,
    caps,
    txt,
    send_a,
    recv_a,
    recv_p,
    send_m,
    recv_m,
    send_l,
    recv_l,
    pool,
    res,
    stage,
    tsend,
    trecv,
    ttot,
    tpart,
    tdone,
    tall,
    ssem,
    rsem,
    tabssem,
    tabrsem,
    capssem,
    caprsem,
    tssem,
    trsem,
    sumssem,
    sumrsem,
    endssem,
    endrsem,
    insem,
    outsem,
    plansem,
):
    g = lax.axis_index("grp")
    s = lax.axis_index("seq")
    z, y = lax.div(s, RING), lax.rem(s, RING)
    sources = (queries, keys, values, grads)
    outs = (out_rows, out_queries, out_keys, out_values)

    def neighbour(ring, sign):
        step = 1 if sign == 0 else RING - 1
        if ring == "y":
            return (g, z * RING + lax.rem(y + step, RING))
        return (g, lax.rem(z + step, RING) * RING + y)

    def group_peer(k):
        return lax.rem(g + k, peers_grp)

    def seq_peer(k):
        return lax.rem(s + k, peers_seq)

    barrier = pltpu.get_barrier_semaphore()
    for k in range(1, peers_seq):
        pl.semaphore_signal(barrier, inc=1, device_id=(g, seq_peer(k)), device_id_type=MESH)
    for k in range(1, peers_grp):
        pl.semaphore_signal(barrier, inc=1, device_id=(group_peer(k), s), device_id_type=MESH)

    def message(io, par, ty, sign, kind):
        ring = "y" if (ty + io + (1 if kind >= MID else 0)) % 2 == 0 else "z"
        if kind == SEND:
            src, dst = send_a.at[io, ty, sign], recv_a.at[io, par, ty, sign]
        elif kind == PASS:
            src, dst = recv_a.at[io, par, ty, sign, pl.ds(0, RELAY)], recv_p.at[io, par, ty, sign]
        elif kind == MID:
            src, dst = send_m.at[io, ty, sign], recv_m.at[io, par, ty, sign]
        else:
            src, dst = send_l.at[io, ty, sign], recv_l.at[io, par, ty, sign]
        index = (((io * 2 + par) * 2 + ty) * 2 + sign) * 4 + kind
        return pltpu.make_async_remote_copy(
            src_ref=src,
            dst_ref=dst,
            send_sem=ssem.at[index],
            recv_sem=rsem.at[index],
            device_id=neighbour(ring, sign),
            device_id_type=MESH,
        )

    def text_message(par, ty, k):
        index = (par * 2 + ty) * (peers_grp - 1) + k - 1
        target = group_peer(k)
        return pltpu.make_async_remote_copy(
            src_ref=tsend.at[ty, target],
            dst_ref=trecv.at[par, ty, k - 1],
            send_sem=tssem.at[index],
            recv_sem=trsem.at[index],
            device_id=(target, s),
            device_id_type=MESH,
        )

    def table_messages():
        copies = []
        for k in range(1, peers_seq + peers_grp - 1):
            seq = k < peers_seq
            copies.append(
                pltpu.make_async_remote_copy(
                    src_ref=mine_rows,
                    dst_ref=tab_seq.at[s] if seq else tab_grp.at[g],
                    send_sem=tabssem.at[k - 1],
                    recv_sem=tabrsem.at[k - 1],
                    device_id=(g, seq_peer(k)) if seq else (group_peer(k - peers_seq + 1), s),
                    device_id_type=MESH,
                )
            )
        return copies

    def caption_messages(pair):
        copies = []
        for a, cap in enumerate((cap_keys, cap_values)):
            src = cap.at[0, :, wide(pair)]
            dst = caps.at[pair, g, a]
            for k in range(1, peers_grp):
                index = (pair * 2 + a) * (peers_grp - 1) + k - 1
                copies.append(
                    pltpu.make_async_remote_copy(
                        src_ref=src,
                        dst_ref=dst,
                        send_sem=capssem.at[index],
                        recv_sem=caprsem.at[index],
                        device_id=(group_peer(k), s),
                        device_id_type=MESH,
                    )
                )
            copies.append(pltpu.make_async_copy(src, dst, insem.at[8 + pair * 2 + a]))
        return copies

    share = 16

    def sum_messages(par):
        copies = []
        for k in range(1, peers_seq):
            target = seq_peer(k)
            index = par * (peers_seq - 1) + k - 1
            copies.append(
                pltpu.make_async_remote_copy(
                    src_ref=ttot.at[par, pl.ds(pl.multiple_of(target * share, share), share)],
                    dst_ref=tpart.at[par, k - 1],
                    send_sem=sumssem.at[index],
                    recv_sem=sumrsem.at[index],
                    device_id=(g, target),
                    device_id_type=MESH,
                )
            )
        return copies

    def end_messages(pair):
        copies = []
        at = pl.ds(pl.multiple_of(s * share, share), share)
        for k in range(1, peers_seq):
            index = pair * (peers_seq - 1) + k - 1
            copies.append(
                pltpu.make_async_remote_copy(
                    src_ref=tdone.at[pair],
                    dst_ref=tall.at[pair, at],
                    send_sem=endssem.at[index],
                    recv_sem=endrsem.at[index],
                    device_id=(g, seq_peer(k)),
                    device_id_type=MESH,
                )
            )
        return copies

    def wide(pair):
        return pl.ds(pl.multiple_of(pair * (2 * LANES), 2 * LANES), 2 * LANES)

    def columns(pair, ty):
        return pl.ds(pl.multiple_of((pair * 2 + ty) * LANES, LANES), LANES)

    def loads(pair):
        par = lax.rem(pair, 2)
        copies = []
        for ty in range(2):
            for a in range(4):
                copies.append(
                    pltpu.make_async_copy(
                        sources[a].at[:, columns(pair, ty)], inb.at[par, ty, a], insem.at[ty * 4 + a]
                    )
                )
        return copies

    def stores(pair):
        copies = []
        for ty in range(2):
            for a in range(4):
                copies.append(
                    pltpu.make_async_copy(
                        stage.at[ty, a], outs[a].at[:, columns(pair, ty)], outsem.at[ty * 4 + a]
                    )
                )
        rows = tall.shape[1] // 2
        for a, out in enumerate((out_cap_keys, out_cap_values)):
            copies.append(
                pltpu.make_async_copy(
                    tall.at[pair, pl.ds(a * rows, rows)], out.at[0, :, wide(pair)], outsem.at[8 + a]
                )
            )
        return copies

    def fill(base, count, read):
        def step(k, carry):
            pool[base + k] = read(k)
            return carry

        lax.fori_loop(0, count, step, 0)

    def fill_own(io, par, ty):
        if io == 0:
            def step(j, carry):
                at = pl.ds(pl.multiple_of(j * TILE, TILE), TILE)
                for a in range(4):
                    pool[OWN + j, a] = inb[par, ty, a, at, :]
                return carry

            lax.fori_loop(0, 6, step, 0)
        else:
            fill(OWN, 9, lambda k: res[ty, k])

    def fill_arrived(io, par, ty):
        for sign in range(2):
            fill(DIRECT + sign * SLOTS, SLOTS, lambda k: recv_a[io, par, ty, sign, k])
            fill(FORWARD + sign * RELAY, RELAY, lambda k: recv_p[io, par, ty, sign, k])

    def fill_passing(io, par, ty):
        for sign in range(2):
            fill(PASSING + sign * RELAY, RELAY, lambda k: recv_m[io, par, ty, sign, k])

    def fill_final(io, par, ty):
        for sign in range(2):
            fill(FINAL + sign * SLOTS, RELAY, lambda k: recv_l[io, par, ty, sign, k])
            fill(
                FINAL + sign * SLOTS + RELAY,
                SLOTS - RELAY,
                lambda k: recv_m[io, par, ty, sign, RELAY + k],
            )

    def choose(ref, io, ty, entry, count, table=plan):
        for sign in range(2):
            def step(k, carry):
                ref[io, ty, sign, k] = pool[table[0, ty * P_SIZE + entry + sign * count + k]]
                return carry

            lax.fori_loop(0, count, step, 0)

    def begin(io, par, ty, kind):
        for sign in range(2):
            message(io, par, ty, sign, kind).start()

    def finish(io, par, ty, kind):
        for sign in range(2):
            message(io, par, ty, sign, kind).wait()

    def first_send(io, par, ty, table=plan):
        fill_own(io, par, ty)
        choose(send_a, io, ty, P_BACK if io else P_SEND, SLOTS, table)
        begin(io, par, ty, SEND)

    def pass_on(io, par):
        for ty in range(2):
            finish(io, par, ty, SEND)
            begin(io, par, ty, PASS)

    def turn(io, par):
        for ty in range(2):
            finish(io, par, ty, PASS)
            fill_own(io, par, ty)
            fill_arrived(io, par, ty)
            choose(send_m, io, ty, P_BACK_MID if io else P_MID, SLOTS)
            begin(io, par, ty, MID)

    def last_send(io, par):
        for ty in range(2):
            finish(io, par, ty, MID)
            fill_own(io, par, ty)
            fill_arrived(io, par, ty)
            fill_passing(io, par, ty)
            choose(send_l, io, ty, P_BACK_LATE if io else P_LATE, RELAY)
            begin(io, par, ty, LATE)

    def compute(ty):
        tsend[ty] = jnp.zeros(tsend.shape[1:], tsend.dtype)

        def image(i, carry):
            tiles = mine[0, T_COUNT + i]
            caption = mine[0, T_CAPTION + i]
            length = plan[0, P_LENGTH + i]
            at = [plan[0, ty * P_SIZE + P_IMAGE + i * 3 + j] for j in range(3)]
            q = jnp.concatenate([pool[p, 0] for p in at], axis=0)
            k = jnp.concatenate([pool[p, 1] for p in at] + [txt[ty, 0, caption]], axis=0)
            v = jnp.concatenate([pool[p, 2] for p in at] + [txt[ty, 1, caption]], axis=0)
            do = jnp.concatenate([pool[p, 3] for p in at], axis=0)
            rows_q, rows_k = q.shape[0], k.shape[0]
            q_row = lax.broadcasted_iota(jnp.int32, (rows_q, LANES), 0)
            do = jnp.where(q_row < tiles * TILE, do, jnp.zeros_like(do))
            q = q * jnp.asarray(HEAD_DIM**-0.5, q.dtype)
            k_row = lax.broadcasted_iota(jnp.int32, (rows_k, LANES), 0)
            seen = (k_row < tiles * TILE) | ((k_row >= rows_q) & (k_row < rows_q + length))
            bias = jnp.where(seen, 0.0, -1e30)
            bias = jnp.concatenate([bias] * (rows_q // LANES), axis=1)
            lane_q = lax.broadcasted_iota(jnp.int32, (rows_q, LANES), 1) < HEAD_DIM
            lane_k = lax.broadcasted_iota(jnp.int32, (rows_k, LANES), 1) < HEAD_DIM
            k_t = k.T
            v_t = v.T
            o_parts, dq_parts, dk_parts, dv_parts = [], [], [], []
            contract_lanes = (((1,), (1,)), ((), ()))
            f32 = jnp.float32
            for h in range(2):
                keep = lane_q if h == 0 else jnp.logical_not(lane_q)
                q_h = jnp.where(keep, q, jnp.zeros_like(q))
                do_h = jnp.where(keep, do, jnp.zeros_like(do))
                scores = lax.dot_general(k, q_h, contract_lanes, preferred_element_type=f32) + bias
                weights = jnp.exp(scores - jnp.max(scores, axis=0, keepdims=True))
                probs = weights * (1.0 / jnp.sum(weights, axis=0, keepdims=True))
                dprobs = lax.dot_general(v, do_h, contract_lanes, preferred_element_type=f32)
                total = jnp.sum(probs * dprobs, axis=0, keepdims=True)
                dscores = (probs * (dprobs - total)).astype(jnp.bfloat16)
                low = probs.astype(jnp.bfloat16)
                span = slice(h * HEAD_DIM, (h + 1) * HEAD_DIM)
                o_parts.append(jnp.dot(v_t[span], low, preferred_element_type=f32))
                dq_parts.append(jnp.dot(k_t[span], dscores, preferred_element_type=f32))
                dk_parts.append(jnp.dot(dscores, q, preferred_element_type=f32))
                dv_parts.append(jnp.dot(low, do, preferred_element_type=f32))
            o = jnp.concatenate(o_parts, axis=0).T.astype(jnp.bfloat16)
            dq = (jnp.concatenate(dq_parts, axis=0).T * HEAD_DIM**-0.5).astype(jnp.bfloat16)
            dk = jnp.where(lane_k, dk_parts[0], dk_parts[1])
            dv = jnp.where(lane_k, dv_parts[0], dv_parts[1])
            for j in range(3):
                rows = slice(j * TILE, (j + 1) * TILE)
                res[ty, i * 3 + j, 0] = o[rows]
                res[ty, i * 3 + j, 1] = dq[rows]
                res[ty, i * 3 + j, 2] = dk[rows].astype(jnp.bfloat16)
                res[ty, i * 3 + j, 3] = dv[rows].astype(jnp.bfloat16)
            dk_text, dv_text = dk[rows_q:], dv[rows_q:]

            def spread(c, inner):
                hit = jnp.where(caption == c, 1.0, 0.0)
                tsend[ty, c, 0] += dk_text * hit
                tsend[ty, c, 1] += dv_text * hit
                return inner

            lax.fori_loop(0, peers_grp, spread, 0)
            return carry

        lax.fori_loop(0, 3, image, 0)

    def work(pair):
        par = lax.rem(pair, 2)
        for copy in caption_messages(pair):
            copy.wait()

        def current(c, carry):
            for a in range(2):
                for ty in range(2):
                    txt[ty, a, c] = caps[pair, c, a, :, ty * LANES : (ty + 1) * LANES]
            return carry

        lax.fori_loop(0, peers_grp, current, 0)
        for ty in range(2):
            finish(0, par, ty, LATE)
            fill_own(0, par, ty)
            fill_arrived(0, par, ty)
            fill_final(0, par, ty)
            compute(ty)
            first_send(1, par, ty)
            for k in range(1, peers_grp):
                text_message(par, ty, k).start()

    def home(pair):
        par = lax.rem(pair, 2)

        @pl.when(pair > 0)
        def _():
            for copy in stores(pair - 1):
                copy.wait()

        for ty in range(2):
            finish(1, par, ty, LATE)
            fill_own(1, par, ty)
            fill_arrived(1, par, ty)
            fill_final(1, par, ty)

            def place(j, carry):
                at = pl.ds(pl.multiple_of(j * TILE, TILE), TILE)
                for a in range(4):
                    stage[ty, a, at, :] = pool[plan[0, ty * P_SIZE + P_HOME + j], a]
                return carry

            lax.fori_loop(0, 6, place, 0)
        for copy in end_messages(pair):
            copy.wait()
        for copy in stores(pair):
            copy.start()

    def add_captions(pair):
        par = lax.rem(pair, 2)
        for ty in range(2):
            for k in range(1, peers_grp):
                text_message(par, ty, k).wait()
            at = slice(ty * LANES, (ty + 1) * LANES)
            for a in range(2):
                total = tsend[ty, g, a]
                for k in range(1, peers_grp):
                    total = total + trecv[par, ty, k - 1, a]
                ttot[par, a * TILE : (a + 1) * TILE, at] = total
        for copy in sum_messages(par):
            copy.start()

    def end_captions(pair):
        par = lax.rem(pair, 2)
        for copy in sum_messages(par):
            copy.wait()
        at = pl.ds(pl.multiple_of(s * share, share), share)
        total = ttot[par, at, :]
        for k in range(1, peers_seq):
            total = total + tpart[par, k - 1]
        done = total.astype(tdone.dtype)
        tdone[pair] = done
        tall[pair, at, :] = done
        for copy in end_messages(pair):
            copy.start()

    for copy in loads(0):
        copy.start()
    own_rows = mine_rows[...]
    tab_seq[s] = own_rows
    tab_grp[g] = own_rows

    def publish(values, place):
        plan_rows[...] = values
        copy = pltpu.make_async_copy(plan_rows, place, plansem)
        copy.start()
        copy.wait()

    source = lax.broadcasted_iota(jnp.int32, (peers_seq, LANES), 0)
    alone = jnp.where(source == s, jnp.concatenate([own_rows] * (peers_seq // 8), axis=0), -1)
    publish(make_plan(alone, mine, None, s), plan_own)
    pl.semaphore_wait(barrier, peers_seq + peers_grp - 2)
    for copy in table_messages():
        copy.start()
    for copy in loads(0):
        copy.wait()
    for ty in range(2):
        first_send(0, 0, ty, plan_own)
    for pair in range(pairs):
        for copy in caption_messages(pair):
            copy.start()
    for copy in table_messages():
        copy.wait()
    publish(make_plan(tab_seq[:, 0, :], mine, tab_grp[:, 0, :], s), plan)

    def superstep(step, carry):
        entering = step < pairs
        working = (step >= 1) & (step <= pairs)
        par_in = lax.rem(step, 2)
        par_out = lax.rem(step + 1, 2)

        @pl.when(step >= 2)
        def _():
            home(step - 2)

        @pl.when(entering & (step > 0))
        def _():
            for copy in loads(step):
                copy.wait()
            for ty in range(2):
                first_send(0, par_in, ty)

        @pl.when(working)
        def _():
            work(step - 1)

        @pl.when(step + 1 < pairs)
        def _():
            for copy in loads(step + 1):
                copy.start()

        @pl.when(working)
        def _():
            pass_on(1, par_out)
            add_captions(step - 1)

        @pl.when(entering)
        def _():
            pass_on(0, par_in)

        @pl.when(working)
        def _():
            turn(1, par_out)

        @pl.when(entering)
        def _():
            turn(0, par_in)

        @pl.when(working)
        def _():
            last_send(1, par_out)
            end_captions(step - 1)

        @pl.when(entering)
        def _():
            last_send(0, par_in)

        return carry

    lax.fori_loop(0, pairs + 2, superstep, 0)
    for copy in stores(pairs - 1):
        copy.wait()


def body(
    image_queries,
    image_keys,
    image_values,
    cotangent,
    text_keys,
    text_values,
    text_lengths,
    send_owner,
    recv_source,
    tile_counts,
    caption_ids,
):
    rows, width = image_queries.shape
    peers_grp, peers_seq = lax.axis_size("grp"), lax.axis_size("seq")
    pairs = width // (2 * LANES)
    mine = jnp.concatenate(
        [send_owner[0], recv_source[0], tile_counts[0], caption_ids[0], text_lengths]
    ).astype(jnp.int32)
    mine = jnp.broadcast_to(jnp.pad(mine, (0, LANES - mine.shape[0]))[None, :], (8, LANES))
    vmem = pl.BlockSpec(memory_space=pltpu.VMEM)
    smem = pl.BlockSpec(memory_space=pltpu.SMEM)
    anywhere = pl.BlockSpec(memory_space=pl.ANY)
    bf16, f32 = jnp.bfloat16, jnp.float32
    quad = (4, TILE, LANES)
    text_rows = text_keys.shape[1]
    image = jax.ShapeDtypeStruct((rows, width), bf16)
    caption = jax.ShapeDtypeStruct(text_keys.shape, bf16)
    dma = pltpu.SemaphoreType.DMA
    scratch = [
        pltpu.VMEM((peers_seq, 8, LANES), jnp.int32),
        pltpu.VMEM((peers_grp, 8, LANES), jnp.int32),
        pltpu.VMEM((8, 2 * P_SIZE), jnp.int32),
        pltpu.SMEM((8, 2 * P_SIZE), jnp.int32),
        pltpu.SMEM((8, 2 * P_SIZE), jnp.int32),
        pltpu.VMEM((2, 2, 4, rows, LANES), bf16),
        pltpu.VMEM((pairs, peers_grp, 2, text_rows, 2 * LANES), bf16),
        pltpu.VMEM((2, 2, peers_grp, text_rows, LANES), bf16),
        pltpu.VMEM((2, 2, 2, SLOTS) + quad, bf16),
        pltpu.VMEM((2, 2, 2, 2, SLOTS) + quad, bf16),
        pltpu.VMEM((2, 2, 2, 2, RELAY) + quad, bf16),
        pltpu.VMEM((2, 2, 2, SLOTS) + quad, bf16),
        pltpu.VMEM((2, 2, 2, 2, SLOTS) + quad, bf16),
        pltpu.VMEM((2, 2, 2, RELAY) + quad, bf16),
        pltpu.VMEM((2, 2, 2, 2, RELAY) + quad, bf16),
        pltpu.VMEM((POOL,) + quad, bf16),
        pltpu.VMEM((2, 9) + quad, bf16),
        pltpu.VMEM((2, 4, rows, LANES), bf16),
        pltpu.VMEM((2, peers_grp, 2, text_rows, LANES), f32),
        pltpu.VMEM((2, 2, peers_grp - 1, 2, text_rows, LANES), f32),
        pltpu.VMEM((2, 2 * text_rows, 2 * LANES), f32),
        pltpu.VMEM((2, peers_seq - 1, 2 * text_rows // peers_seq, 2 * LANES), f32),
        pltpu.VMEM((pairs, 2 * text_rows // peers_seq, 2 * LANES), bf16),
        pltpu.VMEM((pairs, 2 * text_rows, 2 * LANES), bf16),
        dma((64,)),
        dma((64,)),
        dma((peers_seq + peers_grp - 2,)),
        dma((peers_seq + peers_grp - 2,)),
        dma((pairs * 2 * (peers_grp - 1),)),
        dma((pairs * 2 * (peers_grp - 1),)),
        dma((4 * (peers_grp - 1),)),
        dma((4 * (peers_grp - 1),)),
        dma((2 * (peers_seq - 1),)),
        dma((2 * (peers_seq - 1),)),
        dma((pairs * (peers_seq - 1),)),
        dma((pairs * (peers_seq - 1),)),
        dma((8 + 2 * pairs,)),
        dma((10,)),
        dma,
    ]
    return pl.pallas_call(
        functools.partial(main_kernel, peers_grp, peers_seq, pairs),
        out_shape=(image, image, image, image, caption, caption),
        in_specs=[smem, vmem] + [anywhere] * 6,
        out_specs=(anywhere,) * 6,
        scratch_shapes=scratch,
        compiler_params=pltpu.CompilerParams(
            collective_id=0, has_side_effects=True, vmem_limit_bytes=63 * 2**20
        ),
        name="attend",
    )(mine, mine, image_queries, image_keys, image_values, cotangent, text_keys, text_values)


def solution(mesh):
    tokens = P(("grp", "seq"), None)
    captions = P("grp", None, None)
    return jax.shard_map(
        body,
        mesh=mesh,
        in_specs=(tokens,) * 4 + (captions, captions, P("grp")) + (tokens,) * 4,
        out_specs=(tokens,) * 4 + (captions, captions),
        check_vma=False,
    )
```

```python
import functools

import jax
import jax.numpy as jnp
from jax import lax
from jax.experimental import pallas as pl
from jax.experimental.pallas import tpu as pltpu
from jax.sharding import PartitionSpec as P

HEAD_DIM = 64
LANES = 128
TILE = 128
MESH = pl.DeviceIdType.MESH

RING = 4
SLOTS = 4
RELAY = 2

OWN = 0
DIRECT = 6
FORWARD = 14
FINAL = 18
PASSING = 26
POOL = 30

P_SEND = 0
P_MID = 8
P_LATE = 16
P_IMAGE = 20
P_BACK = 32
P_BACK_MID = 40
P_BACK_LATE = 48
P_HOME = 52
P_LENGTH = 58
P_SIZE = 64

T_RECV, T_COUNT, T_CAPTION, T_LENGTH = 6, 12, 15, 18

SEND, SEND_NEAR, PASS, MID, MID_NEAR, LATE = range(6)
KINDS = 6


def make_plan(tab, row_ref, lengths, me):
    peers = tab.shape[0]
    src = lax.broadcasted_iota(jnp.int32, (peers, LANES), 0)
    own = lax.broadcasted_iota(jnp.int32, (peers, LANES), 1)
    sends = jnp.zeros((peers, LANES), jnp.int32)
    place = jnp.zeros((peers, LANES), jnp.int32)
    for j in range(6):
        hit = (tab[:, j : j + 1] == own).astype(jnp.int32)
        sends += hit
        place += hit * j
    first = row_ref[0, T_COUNT]
    second = first + row_ref[0, T_COUNT + 1]
    result = jnp.zeros((peers, LANES), jnp.int32)
    for r in range(6):
        result += jnp.where(src == row_ref[0, T_RECV + r], r, 0)

    lower = (
        lax.broadcasted_iota(jnp.int32, (peers, peers), 1)
        < lax.broadcasted_iota(jnp.int32, (peers, peers), 0)
    ).astype(jnp.float32)
    upper = (
        lax.broadcasted_iota(jnp.int32, (LANES, LANES), 0)
        < lax.broadcasted_iota(jnp.int32, (LANES, LANES), 1)
    ).astype(jnp.float32)
    live = sends > 0
    coord = {"y": lambda t: lax.rem(t, RING), "z": lambda t: lax.div(t, RING) % RING}

    def slots(step, axis):
        count, rank = [], []
        for d in (1, 2, 3):
            picked = jnp.where(live & (step == d), 1.0, 0.0)
            if axis == 1:
                before = jnp.dot(picked, upper, preferred_element_type=jnp.float32)
            else:
                before = jnp.dot(lower, picked, preferred_element_type=jnp.float32)
            rank.append(before.astype(jnp.int32))
            count.append(jnp.sum(picked, axis=axis, keepdims=True).astype(jnp.int32))
        plus = jnp.minimum(jnp.minimum(RELAY, SLOTS - count[0]), count[1])
        code = jnp.where(
            step == 0,
            0,
            jnp.where(
                step == 1, 1, jnp.where(step == 3, 2, jnp.where(rank[1] < plus, 3, 4))
            ),
        )
        slot = jnp.where(
            code == 1,
            SLOTS - 1 - rank[0],
            jnp.where(
                code == 2,
                SLOTS - 1 - rank[2],
                jnp.where(code == 3, rank[1], rank[1] - plus),
            ),
        )
        return code, slot

    def arrived(code, slot, stay, flip):
        base = (DIRECT + SLOTS, DIRECT, FORWARD + RELAY, FORWARD) if flip else (
            DIRECT, DIRECT + SLOTS, FORWARD, FORWARD + RELAY)
        return jnp.where(
            code == 0,
            stay,
            slot
            + jnp.where(
                code == 1,
                base[0],
                jnp.where(code == 2, base[1], jnp.where(code == 3, base[2], base[3])),
            ),
        )

    def settled(code, slot, stay, flip):
        odd = (code == 1) | (code == 3)
        near, far = (FINAL + SLOTS, FINAL) if flip else (FINAL, FINAL + SLOTS)
        return jnp.where(code == 0, stay, slot + jnp.where(odd, near, far))

    zero_row = jnp.zeros((1, LANES), jnp.float32)
    rows = []
    for ring_a, ring_b in (("y", "z"), ("z", "y")):
        at_a, at_b = coord[ring_a], coord[ring_b]
        src_a, src_b, own_a, own_b = at_a(src), at_b(src), at_a(own), at_b(own)
        me_a, me_b = at_a(me), at_b(me)
        code_a, slot_a = slots(lax.rem(own_a - src_a + RING, RING), 1)
        code_b, slot_b = slots(lax.rem(own_b - src_b + RING, RING), 0)
        there = arrived(code_a, slot_a, place, False)
        there_end = settled(code_b, slot_b, there, False)
        back = arrived(code_b, slot_b, result, True)
        back_end = settled(code_a, slot_a, back, True)
        mine_src = live & (src == me)
        mine_own = live & (own == me)
        crossing = live & (own_a == me_a) & (src_b == me_b)
        part = {}

        def put(entry, condition, value):
            row = jnp.sum(
                jnp.where(condition, value, 0).astype(jnp.float32), axis=0, keepdims=True
            )
            part[entry] = part[entry] + row if entry in part else row

        def channel(code, sign, flip):
            sign = 1 - sign if flip else sign
            return (code == 1 + sign), (code == 3 + sign)

        for sign in (0, 1):
            ahead = 1 if sign == 0 else RING - 1
            near, far = channel(code_a, sign, False)
            for k in range(SLOTS):
                put(P_SEND + sign * SLOTS + k, mine_src & (near | far) & (slot_a == k), place)
            near, far = channel(code_b, sign, False)
            passing = live & (own_a == me_a) & far & (lax.rem(own_b - me_b + RING, RING) == ahead)
            for k in range(RELAY):
                put(P_MID + sign * SLOTS + k, crossing & far & (slot_b == k), there)
                put(P_LATE + sign * RELAY + k, crossing & near & (slot_b == k), there)
                put(P_LATE + sign * RELAY + k, passing & (slot_b == k), PASSING + sign * RELAY + k)
            for k in range(RELAY, SLOTS):
                put(P_MID + sign * SLOTS + k, crossing & near & (slot_b == k), there)
            near, far = channel(code_b, sign, True)
            for k in range(SLOTS):
                put(P_BACK + sign * SLOTS + k, mine_own & (near | far) & (slot_b == k), result)
            near, far = channel(code_a, sign, True)
            passing = live & (src_b == me_b) & far & (lax.rem(src_a - me_a + RING, RING) == ahead)
            for k in range(RELAY):
                put(P_BACK_MID + sign * SLOTS + k, crossing & far & (slot_a == k), back)
                put(P_BACK_LATE + sign * RELAY + k, crossing & near & (slot_a == k), back)
                put(P_BACK_LATE + sign * RELAY + k, passing & (slot_a == k), PASSING + sign * RELAY + k)
            for k in range(RELAY, SLOTS):
                put(P_BACK_MID + sign * SLOTS + k, crossing & near & (slot_a == k), back)
        begins = (0, first, second)
        for i in range(3):
            for j in range(3):
                r = jnp.minimum(begins[i] + j, 5)
                put(P_IMAGE + i * 3 + j, mine_own & (src == row_ref[0, T_RECV + r]), there_end)
        for j in range(6):
            put(P_HOME + j, mine_src & (place == j), back_end)
        if lengths is not None:
            captions = lax.broadcasted_iota(jnp.int32, lengths.shape, 0)
            column = lax.broadcasted_iota(jnp.int32, lengths.shape, 1) == T_LENGTH
            for i in range(3):
                put(P_LENGTH + i, column & (captions == row_ref[0, T_CAPTION + i]), lengths)
        rows.extend(part.get(entry, zero_row) for entry in range(P_SIZE))
    matrix = jnp.concatenate(rows, axis=0)
    ones = jnp.ones((8, LANES), jnp.float32)
    out = lax.dot_general(ones, matrix, (((1,), (1,)), ((), ())), preferred_element_type=jnp.float32)
    out = out.astype(jnp.int32)
    entry = lax.broadcasted_iota(jnp.int32, out.shape, 1) % P_SIZE
    return jnp.where(entry < P_LENGTH, jnp.clip(out, 0, POOL - 1), out)


def main_kernel(
    peers_grp,
    peers_seq,
    pairs,
    mine,
    mine_rows,
    queries,
    keys,
    values,
    grads,
    cap_keys,
    cap_values,
    out_rows,
    out_queries,
    out_keys,
    out_values,
    out_cap_keys,
    out_cap_values,
    tab_seq,
    tab_grp,
    plan_rows,
    plan_own,
    plan,
    inb,
    caps,
    txt,
    send_a,
    recv_a,
    recv_p,
    send_m,
    recv_m,
    send_l,
    recv_l,
    pool,
    res,
    stage,
    kk,
    vv,
    kt,
    vt,
    qm,
    dm,
    ps,
    ds,
    tgrad,
    tself,
    tsend,
    trecv,
    tsum,
    ttot,
    tpart,
    tdone,
    tall,
    ssem,
    rsem,
    tabssem,
    tabrsem,
    capssem,
    caprsem,
    tssem,
    trsem,
    sumssem,
    sumrsem,
    endssem,
    endrsem,
    insem,
    outsem,
    plansem,
):
    g = lax.axis_index("grp")
    s = lax.axis_index("seq")
    z, y = lax.div(s, RING), lax.rem(s, RING)
    sources = (queries, keys, values, grads)
    outs = (out_rows, out_queries, out_keys, out_values)

    def neighbour(ring, sign):
        step = 1 if sign == 0 else RING - 1
        if ring == "y":
            return (g, z * RING + lax.rem(y + step, RING))
        return (g, lax.rem(z + step, RING) * RING + y)

    def group_peer(k):
        return lax.rem(g + k, peers_grp)

    def seq_peer(k):
        return lax.rem(s + k, peers_seq)

    barrier = pltpu.get_barrier_semaphore()
    for k in range(1, peers_seq):
        pl.semaphore_signal(barrier, inc=1, device_id=(g, seq_peer(k)), device_id_type=MESH)
    for k in range(1, peers_grp):
        pl.semaphore_signal(barrier, inc=1, device_id=(group_peer(k), s), device_id_type=MESH)

    def first_ring(io, pair):
        return 2 + pair if io else lax.rem(pair, 2)

    def second_ring(io, pair):
        return io * 2 + lax.rem(pair, 2)

    def message(io, pair, ty, sign, kind):
        ring = "y" if (ty + io + (1 if kind >= MID else 0)) % 2 == 0 else "z"
        far, near = pl.ds(0, RELAY), pl.ds(RELAY, SLOTS - RELAY)
        one, two = first_ring(io, pair), second_ring(io, pair)
        if kind in (SEND, SEND_NEAR):
            at = far if kind == SEND else near
            src, dst = send_a.at[io, ty, sign, at], recv_a.at[one, ty, sign, at]
        elif kind == PASS:
            src, dst = recv_a.at[one, ty, sign, far], recv_p.at[one, ty, sign]
        elif kind in (MID, MID_NEAR):
            at = far if kind == MID else near
            src, dst = send_m.at[io, ty, sign, at], recv_m.at[two, ty, sign, at]
        else:
            src, dst = send_l.at[io, ty, sign], recv_l.at[two, ty, sign]
        index = ((one * 2 + ty) * 2 + sign) * KINDS + kind
        return pltpu.make_async_remote_copy(
            src_ref=src,
            dst_ref=dst,
            send_sem=ssem.at[index],
            recv_sem=rsem.at[index],
            device_id=neighbour(ring, sign),
            device_id_type=MESH,
        )

    def text_message(par, ty, k):
        index = (par * 2 + ty) * (peers_grp - 1) + k - 1
        target = group_peer(k)
        return pltpu.make_async_remote_copy(
            src_ref=tsend.at[ty, target],
            dst_ref=trecv.at[par, ty, k - 1],
            send_sem=tssem.at[index],
            recv_sem=trsem.at[index],
            device_id=(target, s),
            device_id_type=MESH,
        )

    def table_messages():
        copies = []
        for k in range(1, peers_seq + peers_grp - 1):
            seq = k < peers_seq
            copies.append(
                pltpu.make_async_remote_copy(
                    src_ref=mine_rows,
                    dst_ref=tab_seq.at[s] if seq else tab_grp.at[g],
                    send_sem=tabssem.at[k - 1],
                    recv_sem=tabrsem.at[k - 1],
                    device_id=(g, seq_peer(k)) if seq else (group_peer(k - peers_seq + 1), s),
                    device_id_type=MESH,
                )
            )
        return copies

    def caption_messages(pair):
        copies = []
        for a, cap in enumerate((cap_keys, cap_values)):
            src = cap.at[0, :, wide(pair)]
            dst = caps.at[pair, g, a]
            for k in range(1, peers_grp):
                index = (pair * 2 + a) * (peers_grp - 1) + k - 1
                copies.append(
                    pltpu.make_async_remote_copy(
                        src_ref=src,
                        dst_ref=dst,
                        send_sem=capssem.at[index],
                        recv_sem=caprsem.at[index],
                        device_id=(group_peer(k), s),
                        device_id_type=MESH,
                    )
                )
            copies.append(pltpu.make_async_copy(src, dst, insem.at[8 + pair * 2 + a]))
        return copies

    share = 16

    def sum_messages(par):
        copies = []
        for k in range(1, peers_seq):
            target = seq_peer(k)
            index = par * (peers_seq - 1) + k - 1
            copies.append(
                pltpu.make_async_remote_copy(
                    src_ref=ttot.at[par, pl.ds(pl.multiple_of(target * share, share), share)],
                    dst_ref=tpart.at[par, k - 1],
                    send_sem=sumssem.at[index],
                    recv_sem=sumrsem.at[index],
                    device_id=(g, target),
                    device_id_type=MESH,
                )
            )
        return copies

    def end_messages(pair):
        copies = []
        at = pl.ds(pl.multiple_of(s * share, share), share)
        for k in range(1, peers_seq):
            index = pair * (peers_seq - 1) + k - 1
            copies.append(
                pltpu.make_async_remote_copy(
                    src_ref=tdone.at[pair],
                    dst_ref=tall.at[pair, at],
                    send_sem=endssem.at[index],
                    recv_sem=endrsem.at[index],
                    device_id=(g, seq_peer(k)),
                    device_id_type=MESH,
                )
            )
        return copies

    def wide(pair):
        return pl.ds(pl.multiple_of(pair * (2 * LANES), 2 * LANES), 2 * LANES)

    def columns(pair, ty):
        return pl.ds(pl.multiple_of((pair * 2 + ty) * LANES, LANES), LANES)

    def loads(pair):
        par = lax.rem(pair, 2)
        copies = []
        for ty in range(2):
            for a in range(4):
                copies.append(
                    pltpu.make_async_copy(
                        sources[a].at[:, columns(pair, ty)], inb.at[par, ty, a], insem.at[ty * 4 + a]
                    )
                )
        return copies

    def stores(pair):
        copies = []
        for ty in range(2):
            for a in range(4):
                copies.append(
                    pltpu.make_async_copy(
                        stage.at[ty, a], outs[a].at[:, columns(pair, ty)], outsem.at[ty * 4 + a]
                    )
                )
        return copies

    def caption_stores():
        rows = tall.shape[1] // 2
        copies = []
        for pair in range(pairs):
            for a, out in enumerate((out_cap_keys, out_cap_values)):
                copies.append(
                    pltpu.make_async_copy(
                        tall.at[pair, pl.ds(a * rows, rows)],
                        out.at[0, :, wide(pair)],
                        outsem.at[8 + pair * 2 + a],
                    )
                )
        return copies

    def fill(base, count, read):
        def step(k, carry):
            pool[base + k] = read(k)
            return carry

        lax.fori_loop(0, count, step, 0)

    def fill_own(io, pair, ty):
        par = lax.rem(pair, 2)
        if io:
            fill(OWN, 6, lambda k: res[par, ty, k])
            return

        def step(j, carry):
            at = pl.ds(pl.multiple_of(j * TILE, TILE), TILE)
            for a in range(4):
                pool[OWN + j, a] = inb[par, ty, a, at, :]
            return carry

        lax.fori_loop(0, 6, step, 0)

    def fill_arrived(io, pair, ty):
        one = first_ring(io, pair)
        for sign in range(2):
            fill(DIRECT + sign * SLOTS, SLOTS, lambda k: recv_a[one, ty, sign, k])
            fill(FORWARD + sign * RELAY, RELAY, lambda k: recv_p[one, ty, sign, k])

    def fill_passing(io, pair, ty):
        two = second_ring(io, pair)
        for sign in range(2):
            fill(PASSING + sign * RELAY, RELAY, lambda k: recv_m[two, ty, sign, k])

    def fill_final(io, pair, ty):
        two = second_ring(io, pair)
        for sign in range(2):
            fill(FINAL + sign * SLOTS, RELAY, lambda k: recv_l[two, ty, sign, k])
            fill(
                FINAL + sign * SLOTS + RELAY,
                SLOTS - RELAY,
                lambda k: recv_m[two, ty, sign, RELAY + k],
            )

    def choose(ref, io, ty, entry, count, first, last, table=plan):
        for sign in range(2):

            def step(k, carry):
                ref[io, ty, sign, k] = pool[table[0, ty * P_SIZE + entry + sign * count + k]]
                return carry

            lax.fori_loop(first, last, step, 0)

    def begin(io, pair, ty, kind):
        for sign in range(2):
            message(io, pair, ty, sign, kind).start()

    def finish(io, pair, ty, kind):
        for sign in range(2):
            message(io, pair, ty, sign, kind).wait()

    def first_send(io, pair, ty, table=plan):
        fill_own(io, pair, ty)
        entry = P_BACK if io else P_SEND
        choose(send_a, io, ty, entry, SLOTS, 0, RELAY, table)
        begin(io, pair, ty, SEND)
        choose(send_a, io, ty, entry, SLOTS, RELAY, SLOTS, table)
        begin(io, pair, ty, SEND_NEAR)

    def pass_on(io, pair):
        for ty in range(2):
            finish(io, pair, ty, SEND)
            begin(io, pair, ty, PASS)

    def turn(io, pair):
        for ty in range(2):
            finish(io, pair, ty, SEND_NEAR)
            finish(io, pair, ty, PASS)
            fill_own(io, pair, ty)
            fill_arrived(io, pair, ty)
            entry = P_BACK_MID if io else P_MID
            choose(send_m, io, ty, entry, SLOTS, 0, RELAY)
            begin(io, pair, ty, MID)
            choose(send_m, io, ty, entry, SLOTS, RELAY, SLOTS)
            begin(io, pair, ty, MID_NEAR)

    def last_send(io, pair):
        for ty in range(2):
            finish(io, pair, ty, MID)
            fill_own(io, pair, ty)
            fill_arrived(io, pair, ty)
            fill_passing(io, pair, ty)
            choose(send_l, io, ty, P_BACK_LATE if io else P_LATE, RELAY, 0, RELAY)
            begin(io, pair, ty, LATE)

    def final(io, pair, ty):
        finish(io, pair, ty, MID_NEAR)
        finish(io, pair, ty, LATE)
        fill_own(io, pair, ty)
        fill_arrived(io, pair, ty)
        fill_final(io, pair, ty)

    def compute(pair, ty):
        par = lax.rem(pair, 2)
        bf16, f32 = jnp.bfloat16, jnp.float32
        scale = HEAD_DIM**-0.5
        lane = lax.broadcasted_iota(jnp.int32, (TILE, LANES), 1) < HEAD_DIM
        text_row = lax.broadcasted_iota(jnp.int32, (TILE, LANES), 0)
        contract_lanes = (((1,), (1,)), ((), ()))
        first = mine[0, T_COUNT]
        second = first + mine[0, T_COUNT + 1]
        text = 3 * TILE

        def begin_of(i):
            return jnp.where(i == 0, 0, jnp.where(i == 1, first, second))

        def half(tile, h):
            return jnp.where(lane if h == 0 else jnp.logical_not(lane), tile, jnp.zeros_like(tile))

        def prepare(i, carry):
            tiles = mine[0, T_COUNT + i]
            caption = mine[0, T_CAPTION + i]
            for j in range(4):
                at = slice(j * TILE, (j + 1) * TILE)
                if j < 3:
                    place = plan[0, ty * P_SIZE + P_IMAGE + i * 3 + j]
                    k, v = pool[place, 1], pool[place, 2]
                    live = jnp.where(j < tiles, 1.0, 0.0)
                    qm[i, at, :] = (pool[place, 0].astype(f32) * (live * scale)).astype(bf16)
                    dm[i, at, :] = (pool[place, 3].astype(f32) * live).astype(bf16)
                else:
                    k, v = txt[0, caption], txt[1, caption]
                kk[i, at, :] = k
                vv[i, at, :] = v
                kt[i, :, at] = k.T
                vt[i, :, at] = v.T
            return carry

        lax.fori_loop(0, 3, prepare, 0)

        def query(r, carry):
            i = jnp.where(r >= first, 1, 0) + jnp.where(r >= second, 1, 0)
            j = jnp.minimum(r - begin_of(i), 2)
            tiles = mine[0, T_COUNT + i]
            length = plan[0, P_LENGTH + i]
            place = plan[0, ty * P_SIZE + P_IMAGE + i * 3 + j]
            q = pool[place, 0] * jnp.asarray(scale, bf16)
            do = pool[place, 3]
            k, v = kk[i], vv[i]
            hide = [0.0] + [jnp.where(n < tiles, 0.0, -1e30) for n in (1, 2)]
            hide.append(jnp.where(text_row < length, 0.0, -1e30))
            o_parts, dq_parts = [], []
            for h in range(2):
                scores = lax.dot_general(k, half(q, h), contract_lanes, preferred_element_type=f32)
                scores = jnp.concatenate(
                    [scores[n * TILE : (n + 1) * TILE] + hide[n] for n in range(4)], axis=0
                )
                weights = jnp.exp(scores - jnp.max(scores, axis=0, keepdims=True))
                probs = weights * (1.0 / jnp.sum(weights, axis=0, keepdims=True))
                dprobs = lax.dot_general(v, half(do, h), contract_lanes, preferred_element_type=f32)
                total = jnp.sum(probs * dprobs, axis=0, keepdims=True)
                dscores = (probs * (dprobs - total)).astype(bf16)
                low = probs.astype(bf16)
                for n in range(4):
                    ps[r, h, n] = low[n * TILE : (n + 1) * TILE]
                    ds[r, h, n] = dscores[n * TILE : (n + 1) * TILE]
                span = slice(h * HEAD_DIM, (h + 1) * HEAD_DIM)
                o_parts.append(jnp.dot(vt[i, span, :], low, preferred_element_type=f32))
                dq_parts.append(jnp.dot(kt[i, span, :], dscores, preferred_element_type=f32))
            o = jnp.concatenate(o_parts, axis=0).T
            dq = jnp.concatenate(dq_parts, axis=0).T * scale
            res[par, ty, r, 0] = o.astype(bf16)
            res[par, ty, r, 1] = dq.astype(bf16)
            return carry

        lax.fori_loop(0, 6, query, 0)

        def key_grads(i, block):
            begin_i = begin_of(i)
            rows = [jnp.minimum(begin_i + n, 5) for n in range(3)]
            q, do = qm[i], dm[i]
            dk, dv = [], []
            for h in range(2):
                low = jnp.concatenate([ps[r, h, block] for r in rows], axis=1)
                dscores = jnp.concatenate([ds[r, h, block] for r in rows], axis=1)
                dk.append(jnp.dot(dscores, q, preferred_element_type=f32))
                dv.append(jnp.dot(low, do, preferred_element_type=f32))
            return jnp.where(lane, dk[0], dk[1]), jnp.where(lane, dv[0], dv[1])

        def key(r, carry):
            i = jnp.where(r >= first, 1, 0) + jnp.where(r >= second, 1, 0)
            dk, dv = key_grads(i, jnp.minimum(r - begin_of(i), 2))
            res[par, ty, r, 2] = dk.astype(bf16)
            res[par, ty, r, 3] = dv.astype(bf16)
            return carry

        lax.fori_loop(0, 6, key, 0)

        def caption_key(i, carry):
            dk, dv = key_grads(i, 3)
            tgrad[i, 0] = dk
            tgrad[i, 1] = dv
            return carry

        lax.fori_loop(0, 3, caption_key, 0)

        def spread(c, a):
            hits = [jnp.where(mine[0, T_CAPTION + i] == c, 1.0, 0.0) for i in range(3)]
            return tgrad[0, a] * hits[0] + tgrad[1, a] * hits[1] + tgrad[2, a] * hits[2]

        def settle(c, carry):
            for a in range(2):
                tsend[ty, c, a] = spread(c, a).astype(bf16)
            return carry

        lax.fori_loop(0, peers_grp, settle, 0)
        for a in range(2):
            tself[ty, a] = spread(g, a)

    def captions_in(pair, ty):
        def current(c, carry):
            for a in range(2):
                txt[a, c] = caps[pair, c, a, :, ty * LANES : (ty + 1) * LANES]
            return carry

        lax.fori_loop(0, peers_grp, current, 0)

    def work(pair, ty):
        final(0, pair, ty)
        captions_in(pair, ty)
        compute(pair, ty)
        first_send(1, pair, ty)
        for k in range(1, peers_grp):
            text_message(lax.rem(pair, 2), ty, k).start()

    def home(pair):
        @pl.when(pair > 0)
        def _():
            for copy in stores(pair - 1):
                copy.wait()

        for ty in range(2):
            final(1, pair, ty)

            def place(j, carry):
                at = pl.ds(pl.multiple_of(j * TILE, TILE), TILE)
                for a in range(4):
                    stage[ty, a, at, :] = pool[plan[0, ty * P_SIZE + P_HOME + j], a]
                return carry

            lax.fori_loop(0, 6, place, 0)
        for copy in stores(pair):
            copy.start()

    def add_captions(pair):
        par = lax.rem(pair, 2)
        for ty in range(2):
            for k in range(1, peers_grp):
                text_message(par, ty, k).wait()
            at = slice(ty * LANES, (ty + 1) * LANES)
            for a in range(2):
                total = tself[ty, a]
                for k in range(1, peers_grp):
                    total = total + trecv[par, ty, k - 1, a].astype(jnp.float32)
                tsum[a * TILE : (a + 1) * TILE, at] = total
                ttot[par, a * TILE : (a + 1) * TILE, at] = total.astype(ttot.dtype)
        for copy in sum_messages(par):
            copy.start()

    def end_captions(pair):
        par = lax.rem(pair, 2)
        for copy in sum_messages(par):
            copy.wait()
        at = pl.ds(pl.multiple_of(s * share, share), share)
        total = tsum[at, :]
        for k in range(1, peers_seq):
            total = total + tpart[par, k - 1].astype(jnp.float32)
        done = total.astype(tdone.dtype)
        tdone[pair] = done
        tall[pair, at, :] = done
        for copy in end_messages(pair):
            copy.start()

    for copy in loads(0):
        copy.start()
    own_rows = mine_rows[...]
    tab_seq[s] = own_rows
    tab_grp[g] = own_rows

    def publish(values, place):
        plan_rows[...] = values
        copy = pltpu.make_async_copy(plan_rows, place, plansem)
        copy.start()
        copy.wait()

    source = lax.broadcasted_iota(jnp.int32, (peers_seq, LANES), 0)
    alone = jnp.where(source == s, jnp.concatenate([own_rows] * (peers_seq // 8), axis=0), -1)
    publish(make_plan(alone, mine, None, s), plan_own)
    pl.semaphore_wait(barrier, peers_seq + peers_grp - 2)
    for copy in table_messages():
        copy.start()
    for copy in loads(0):
        copy.wait()
    for ty in range(2):
        first_send(0, jnp.int32(0), ty, plan_own)
    for pair in range(pairs):
        for copy in caption_messages(pair):
            copy.start()
    for copy in table_messages():
        copy.wait()
    publish(make_plan(tab_seq[:, 0, :], mine, tab_grp[:, 0, :], s), plan)

    for copy in loads(1):
        copy.start()

    def superstep(step, carry):
        entering = step < pairs
        working = (step >= 1) & (step <= pairs)
        leaving = step >= 2

        def following():
            for copy in loads(step + 1):
                copy.wait()
            for ty in range(2):
                first_send(0, step + 1, ty)

        @pl.when(leaving)
        def _():
            turn(1, step - 2)

        @pl.when(working)
        def _():
            for copy in caption_messages(step - 1):
                copy.wait()
            work(step - 1, 0)

        @pl.when(entering)
        def _():
            pass_on(0, step)

        @pl.when(leaving)
        def _():
            last_send(1, step - 2)

        @pl.when(working)
        def _():
            work(step - 1, 1)

        @pl.when(leaving)
        def _():
            end_captions(step - 2)

        @pl.when((step >= 1) & (step + 1 < pairs))
        def _():
            for copy in loads(step + 1):
                copy.start()

        @pl.when(working)
        def _():
            pass_on(1, step - 1)

        @pl.when(entering)
        def _():
            turn(0, step)

        @pl.when(step == 0)
        def _():
            following()

        @pl.when(leaving)
        def _():
            home(step - 2)

        @pl.when(entering)
        def _():
            last_send(0, step)

        @pl.when(working)
        def _():
            add_captions(step - 1)

        @pl.when((step >= 1) & (step + 1 < pairs))
        def _():
            following()

        return carry

    lax.fori_loop(0, pairs + 2, superstep, 0)
    for pair in range(pairs):
        for copy in end_messages(pair):
            copy.wait()
    for copy in caption_stores():
        copy.start()
    for copy in stores(pairs - 1):
        copy.wait()
    for copy in caption_stores():
        copy.wait()


def copy_kernel(*refs):
    count = len(refs) // 2
    for source, target in zip(refs[:count], refs[count:]):
        target[...] = source[...]


def body(
    image_queries,
    image_keys,
    image_values,
    cotangent,
    text_keys,
    text_values,
    text_lengths,
    send_owner,
    recv_source,
    tile_counts,
    caption_ids,
):
    rows, width = image_queries.shape
    peers_grp, peers_seq = lax.axis_size("grp"), lax.axis_size("seq")
    pairs = width // (2 * LANES)
    mine = jnp.concatenate(
        [send_owner[0], recv_source[0], tile_counts[0], caption_ids[0], text_lengths]
    ).astype(jnp.int32)
    mine = jnp.broadcast_to(jnp.pad(mine, (0, LANES - mine.shape[0]))[None, :], (8, LANES))
    vmem = pl.BlockSpec(memory_space=pltpu.VMEM)
    smem = pl.BlockSpec(memory_space=pltpu.SMEM)
    anywhere = pl.BlockSpec(memory_space=pl.ANY)
    bf16, f32 = jnp.bfloat16, jnp.float32
    quad = (4, TILE, LANES)
    text_rows = text_keys.shape[1]
    image = jax.ShapeDtypeStruct((rows, width), bf16)
    caption = jax.ShapeDtypeStruct(text_keys.shape, bf16)
    dma = pltpu.SemaphoreType.DMA
    scratch = [
        pltpu.VMEM((peers_seq, 8, LANES), jnp.int32),
        pltpu.VMEM((peers_grp, 8, LANES), jnp.int32),
        pltpu.VMEM((8, 2 * P_SIZE), jnp.int32),
        pltpu.SMEM((8, 2 * P_SIZE), jnp.int32),
        pltpu.SMEM((8, 2 * P_SIZE), jnp.int32),
        pltpu.VMEM((2, 2, 4, rows, LANES), bf16),
        pltpu.VMEM((pairs, peers_grp, 2, text_rows, 2 * LANES), bf16),
        pltpu.VMEM((2, peers_grp, text_rows, LANES), bf16),
        pltpu.VMEM((2, 2, 2, SLOTS) + quad, bf16),
        pltpu.VMEM((2 + pairs, 2, 2, SLOTS) + quad, bf16),
        pltpu.VMEM((2 + pairs, 2, 2, RELAY) + quad, bf16),
        pltpu.VMEM((2, 2, 2, SLOTS) + quad, bf16),
        pltpu.VMEM((4, 2, 2, SLOTS) + quad, bf16),
        pltpu.VMEM((2, 2, 2, RELAY) + quad, bf16),
        pltpu.VMEM((4, 2, 2, RELAY) + quad, bf16),
        pltpu.VMEM((POOL,) + quad, bf16),
        pltpu.VMEM((2, 2, 6) + quad, bf16),
        pltpu.VMEM((2, 4, rows, LANES), bf16),
        pltpu.VMEM((3, 4 * TILE, LANES), bf16),
        pltpu.VMEM((3, 4 * TILE, LANES), bf16),
        pltpu.VMEM((3, LANES, 4 * TILE), bf16),
        pltpu.VMEM((3, LANES, 4 * TILE), bf16),
        pltpu.VMEM((3, 3 * TILE, LANES), bf16),
        pltpu.VMEM((3, 3 * TILE, LANES), bf16),
        pltpu.VMEM((6, 2, 4, TILE, TILE), bf16),
        pltpu.VMEM((6, 2, 4, TILE, TILE), bf16),
        pltpu.VMEM((3, 2, TILE, LANES), f32),
        pltpu.VMEM((2, 2, text_rows, LANES), f32),
        pltpu.VMEM((2, peers_grp, 2, text_rows, LANES), bf16),
        pltpu.VMEM((2, 2, peers_grp - 1, 2, text_rows, LANES), bf16),
        pltpu.VMEM((2 * text_rows, 2 * LANES), f32),
        pltpu.VMEM((2, 2 * text_rows, 2 * LANES), bf16),
        pltpu.VMEM((2, peers_seq - 1, 2 * text_rows // peers_seq, 2 * LANES), bf16),
        pltpu.VMEM((pairs, 2 * text_rows // peers_seq, 2 * LANES), bf16),
        pltpu.VMEM((pairs, 2 * text_rows, 2 * LANES), bf16),
        dma((4 * (2 + pairs) * KINDS,)),
        dma((4 * (2 + pairs) * KINDS,)),
        dma((peers_seq + peers_grp - 2,)),
        dma((peers_seq + peers_grp - 2,)),
        dma((pairs * 2 * (peers_grp - 1),)),
        dma((pairs * 2 * (peers_grp - 1),)),
        dma((4 * (peers_grp - 1),)),
        dma((4 * (peers_grp - 1),)),
        dma((2 * (peers_seq - 1),)),
        dma((2 * (peers_seq - 1),)),
        dma((pairs * (peers_seq - 1),)),
        dma((pairs * (peers_seq - 1),)),
        dma((8 + 2 * pairs,)),
        dma((8 + 2 * pairs,)),
        dma,
    ]
    results = pl.pallas_call(
        functools.partial(main_kernel, peers_grp, peers_seq, pairs),
        out_shape=(image, image, image, image, caption, caption),
        in_specs=[smem, vmem] + [anywhere] * 6,
        out_specs=(anywhere,) * 6,
        scratch_shapes=scratch,
        compiler_params=pltpu.CompilerParams(
            collective_id=0, has_side_effects=True, vmem_limit_bytes=63 * 2**20
        ),
        name="attend",
    )(mine, mine, image_queries, image_keys, image_values, cotangent, text_keys, text_values)
    steps = 4
    blocks = [
        pl.BlockSpec((rows // steps, width), lambda i: (i, 0)),
        pl.BlockSpec((1, text_rows // steps, width), lambda i: (0, i, 0)),
    ]
    specs = [blocks[0]] * 4 + [blocks[1]] * 2
    return pl.pallas_call(
        copy_kernel,
        grid=(steps,),
        out_shape=(image, image, image, image, caption, caption),
        in_specs=specs,
        out_specs=tuple(specs),
        name="results",
    )(*results)


def solution(mesh):
    tokens = P(("grp", "seq"), None)
    captions = P("grp", None, None)
    return jax.shard_map(
        body,
        mesh=mesh,
        in_specs=(tokens,) * 4 + (captions, captions, P("grp")) + (tokens,) * 4,
        out_specs=(tokens,) * 4 + (captions, captions),
        check_vma=False,
    )
```

```python
import functools

import jax
import jax.numpy as jnp
from jax import lax
from jax.experimental import pallas as pl
from jax.experimental.pallas import tpu as pltpu
from jax.sharding import PartitionSpec as P

HEAD_DIM = 64
LANES = 128
TILE = 128
MESH = pl.DeviceIdType.MESH

RING = 4
SLOTS = 4
RELAY = 2

OWN = 0
DIRECT = 6
FORWARD = 14
FINAL = 18
PASSING = 26
POOL = 30

P_SEND = 0
P_MID = 8
P_LATE = 16
P_IMAGE = 20
P_BACK = 32
P_BACK_MID = 40
P_BACK_LATE = 48
P_HOME = 52
P_LENGTH = 58
P_SIZE = 64

T_RECV, T_COUNT, T_CAPTION, T_LENGTH = 6, 12, 15, 18

SEND, SEND_NEAR, PASS, MID, MID_NEAR, LATE = range(6)
KINDS = 6


def make_plan(tab, row_ref, lengths, me):
    peers = tab.shape[0]
    src = lax.broadcasted_iota(jnp.int32, (peers, LANES), 0)
    own = lax.broadcasted_iota(jnp.int32, (peers, LANES), 1)
    sends = jnp.zeros((peers, LANES), jnp.int32)
    place = jnp.zeros((peers, LANES), jnp.int32)
    for j in range(6):
        hit = (tab[:, j : j + 1] == own).astype(jnp.int32)
        sends += hit
        place += hit * j
    first = row_ref[0, T_COUNT]
    second = first + row_ref[0, T_COUNT + 1]
    result = jnp.zeros((peers, LANES), jnp.int32)
    for r in range(6):
        result += jnp.where(src == row_ref[0, T_RECV + r], r, 0)

    lower = (
        lax.broadcasted_iota(jnp.int32, (peers, peers), 1)
        < lax.broadcasted_iota(jnp.int32, (peers, peers), 0)
    ).astype(jnp.float32)
    upper = (
        lax.broadcasted_iota(jnp.int32, (LANES, LANES), 0)
        < lax.broadcasted_iota(jnp.int32, (LANES, LANES), 1)
    ).astype(jnp.float32)
    live = sends > 0
    coord = {"y": lambda t: lax.rem(t, RING), "z": lambda t: lax.div(t, RING) % RING}

    def slots(step, axis):
        count, rank = [], []
        for d in (1, 2, 3):
            picked = jnp.where(live & (step == d), 1.0, 0.0)
            if axis == 1:
                before = jnp.dot(picked, upper, preferred_element_type=jnp.float32)
            else:
                before = jnp.dot(lower, picked, preferred_element_type=jnp.float32)
            rank.append(before.astype(jnp.int32))
            count.append(jnp.sum(picked, axis=axis, keepdims=True).astype(jnp.int32))
        plus = jnp.minimum(jnp.minimum(RELAY, SLOTS - count[0]), count[1])
        code = jnp.where(
            step == 0,
            0,
            jnp.where(
                step == 1, 1, jnp.where(step == 3, 2, jnp.where(rank[1] < plus, 3, 4))
            ),
        )
        slot = jnp.where(
            code == 1,
            SLOTS - 1 - rank[0],
            jnp.where(
                code == 2,
                SLOTS - 1 - rank[2],
                jnp.where(code == 3, rank[1], rank[1] - plus),
            ),
        )
        return code, slot

    def arrived(code, slot, stay, flip):
        base = (DIRECT + SLOTS, DIRECT, FORWARD + RELAY, FORWARD) if flip else (
            DIRECT, DIRECT + SLOTS, FORWARD, FORWARD + RELAY)
        return jnp.where(
            code == 0,
            stay,
            slot
            + jnp.where(
                code == 1,
                base[0],
                jnp.where(code == 2, base[1], jnp.where(code == 3, base[2], base[3])),
            ),
        )

    def settled(code, slot, stay, flip):
        odd = (code == 1) | (code == 3)
        near, far = (FINAL + SLOTS, FINAL) if flip else (FINAL, FINAL + SLOTS)
        return jnp.where(code == 0, stay, slot + jnp.where(odd, near, far))

    zero_row = jnp.zeros((1, LANES), jnp.float32)
    rows = []
    for ring_a, ring_b in (("y", "z"), ("z", "y")):
        at_a, at_b = coord[ring_a], coord[ring_b]
        src_a, src_b, own_a, own_b = at_a(src), at_b(src), at_a(own), at_b(own)
        me_a, me_b = at_a(me), at_b(me)
        code_a, slot_a = slots(lax.rem(own_a - src_a + RING, RING), 1)
        code_b, slot_b = slots(lax.rem(own_b - src_b + RING, RING), 0)
        there = arrived(code_a, slot_a, place, False)
        there_end = settled(code_b, slot_b, there, False)
        back = arrived(code_b, slot_b, result, True)
        back_end = settled(code_a, slot_a, back, True)
        mine_src = live & (src == me)
        mine_own = live & (own == me)
        crossing = live & (own_a == me_a) & (src_b == me_b)
        part = {}

        def put(entry, condition, value):
            row = jnp.sum(
                jnp.where(condition, value, 0).astype(jnp.float32), axis=0, keepdims=True
            )
            part[entry] = part[entry] + row if entry in part else row

        def channel(code, sign, flip):
            sign = 1 - sign if flip else sign
            return (code == 1 + sign), (code == 3 + sign)

        for sign in (0, 1):
            ahead = 1 if sign == 0 else RING - 1
            near, far = channel(code_a, sign, False)
            for k in range(SLOTS):
                put(P_SEND + sign * SLOTS + k, mine_src & (near | far) & (slot_a == k), place)
            near, far = channel(code_b, sign, False)
            passing = live & (own_a == me_a) & far & (lax.rem(own_b - me_b + RING, RING) == ahead)
            for k in range(RELAY):
                put(P_MID + sign * SLOTS + k, crossing & far & (slot_b == k), there)
                put(P_LATE + sign * RELAY + k, crossing & near & (slot_b == k), there)
                put(P_LATE + sign * RELAY + k, passing & (slot_b == k), PASSING + sign * RELAY + k)
            for k in range(RELAY, SLOTS):
                put(P_MID + sign * SLOTS + k, crossing & near & (slot_b == k), there)
            near, far = channel(code_b, sign, True)
            for k in range(SLOTS):
                put(P_BACK + sign * SLOTS + k, mine_own & (near | far) & (slot_b == k), result)
            near, far = channel(code_a, sign, True)
            passing = live & (src_b == me_b) & far & (lax.rem(src_a - me_a + RING, RING) == ahead)
            for k in range(RELAY):
                put(P_BACK_MID + sign * SLOTS + k, crossing & far & (slot_a == k), back)
                put(P_BACK_LATE + sign * RELAY + k, crossing & near & (slot_a == k), back)
                put(P_BACK_LATE + sign * RELAY + k, passing & (slot_a == k), PASSING + sign * RELAY + k)
            for k in range(RELAY, SLOTS):
                put(P_BACK_MID + sign * SLOTS + k, crossing & near & (slot_a == k), back)
        begins = (0, first, second)
        for i in range(3):
            for j in range(3):
                r = jnp.minimum(begins[i] + j, 5)
                put(P_IMAGE + i * 3 + j, mine_own & (src == row_ref[0, T_RECV + r]), there_end)
        for j in range(6):
            put(P_HOME + j, mine_src & (place == j), back_end)
        if lengths is not None:
            captions = lax.broadcasted_iota(jnp.int32, lengths.shape, 0)
            column = lax.broadcasted_iota(jnp.int32, lengths.shape, 1) == T_LENGTH
            for i in range(3):
                put(P_LENGTH + i, column & (captions == row_ref[0, T_CAPTION + i]), lengths)
        rows.extend(part.get(entry, zero_row) for entry in range(P_SIZE))
    matrix = jnp.concatenate(rows, axis=0)
    ones = jnp.ones((8, LANES), jnp.float32)
    out = lax.dot_general(ones, matrix, (((1,), (1,)), ((), ())), preferred_element_type=jnp.float32)
    out = out.astype(jnp.int32)
    entry = lax.broadcasted_iota(jnp.int32, out.shape, 1) % P_SIZE
    return jnp.where(entry < P_LENGTH, jnp.clip(out, 0, POOL - 1), out)


def main_kernel(
    peers_grp,
    peers_seq,
    pairs,
    mine,
    mine_rows,
    queries,
    keys,
    values,
    grads,
    cap_keys,
    cap_values,
    out_rows,
    out_queries,
    out_keys,
    out_values,
    out_cap_keys,
    out_cap_values,
    tab_seq,
    tab_grp,
    plan_rows,
    plan_own,
    plan,
    inb,
    caps,
    txt,
    send_a,
    recv_a,
    recv_p,
    send_m,
    recv_m,
    send_l,
    recv_l,
    pool,
    res,
    stage,
    kk,
    vv,
    kt,
    vt,
    qm,
    dm,
    ps,
    ds,
    tgrad,
    tself,
    tsend,
    trecv,
    tsum,
    ttot,
    tpart,
    tdone,
    tall,
    ssem,
    rsem,
    tabssem,
    tabrsem,
    capssem,
    caprsem,
    tssem,
    trsem,
    sumssem,
    sumrsem,
    endssem,
    endrsem,
    insem,
    outsem,
    plansem,
):
    g = lax.axis_index("grp")
    s = lax.axis_index("seq")
    z, y = lax.div(s, RING), lax.rem(s, RING)
    sources = (queries, keys, values, grads)
    outs = (out_rows, out_queries, out_keys, out_values)

    def neighbour(ring, sign):
        step = 1 if sign == 0 else RING - 1
        if ring == "y":
            return (g, z * RING + lax.rem(y + step, RING))
        return (g, lax.rem(z + step, RING) * RING + y)

    def group_peer(k):
        return lax.rem(g + k, peers_grp)

    def seq_peer(k):
        return lax.rem(s + k, peers_seq)

    barrier = pltpu.get_barrier_semaphore()
    for k in range(1, peers_seq):
        pl.semaphore_signal(barrier, inc=1, device_id=(g, seq_peer(k)), device_id_type=MESH)
    for k in range(1, peers_grp):
        pl.semaphore_signal(barrier, inc=1, device_id=(group_peer(k), s), device_id_type=MESH)

    def first_ring(io, pair):
        return 2 + pair if io else lax.rem(pair, 2)

    def second_ring(io, pair):
        return io * 2 + lax.rem(pair, 2)

    def message(io, pair, ty, sign, kind):
        ring = "y" if (ty + io + (1 if kind >= MID else 0)) % 2 == 0 else "z"
        far, near = pl.ds(0, RELAY), pl.ds(RELAY, SLOTS - RELAY)
        one, two = first_ring(io, pair), second_ring(io, pair)
        if kind in (SEND, SEND_NEAR):
            at = far if kind == SEND else near
            src, dst = send_a.at[io, ty, sign, at], recv_a.at[one, ty, sign, at]
        elif kind == PASS:
            src, dst = recv_a.at[one, ty, sign, far], recv_p.at[one, ty, sign]
        elif kind in (MID, MID_NEAR):
            at = far if kind == MID else near
            src, dst = send_m.at[io, ty, sign, at], recv_m.at[two, ty, sign, at]
        else:
            src, dst = send_l.at[io, ty, sign], recv_l.at[two, ty, sign]
        index = ((one * 2 + ty) * 2 + sign) * KINDS + kind
        return pltpu.make_async_remote_copy(
            src_ref=src,
            dst_ref=dst,
            send_sem=ssem.at[index],
            recv_sem=rsem.at[index],
            device_id=neighbour(ring, sign),
            device_id_type=MESH,
        )

    def text_message(par, ty, k):
        index = (par * 2 + ty) * (peers_grp - 1) + k - 1
        target = group_peer(k)
        return pltpu.make_async_remote_copy(
            src_ref=tsend.at[ty, target],
            dst_ref=trecv.at[par, ty, k - 1],
            send_sem=tssem.at[index],
            recv_sem=trsem.at[index],
            device_id=(target, s),
            device_id_type=MESH,
        )

    def table_messages():
        copies = []
        for k in range(1, peers_seq + peers_grp - 1):
            seq = k < peers_seq
            copies.append(
                pltpu.make_async_remote_copy(
                    src_ref=mine_rows,
                    dst_ref=tab_seq.at[s] if seq else tab_grp.at[g],
                    send_sem=tabssem.at[k - 1],
                    recv_sem=tabrsem.at[k - 1],
                    device_id=(g, seq_peer(k)) if seq else (group_peer(k - peers_seq + 1), s),
                    device_id_type=MESH,
                )
            )
        return copies

    def caption_messages(pair):
        copies = []
        for a, cap in enumerate((cap_keys, cap_values)):
            src = cap.at[0, :, wide(pair)]
            dst = caps.at[pair, g, a]
            for k in range(1, peers_grp):
                index = (pair * 2 + a) * (peers_grp - 1) + k - 1
                copies.append(
                    pltpu.make_async_remote_copy(
                        src_ref=src,
                        dst_ref=dst,
                        send_sem=capssem.at[index],
                        recv_sem=caprsem.at[index],
                        device_id=(group_peer(k), s),
                        device_id_type=MESH,
                    )
                )
            copies.append(pltpu.make_async_copy(src, dst, insem.at[8 + pair * 2 + a]))
        return copies

    share = 16

    def sum_messages(par):
        copies = []
        for k in range(1, peers_seq):
            target = seq_peer(k)
            index = par * (peers_seq - 1) + k - 1
            copies.append(
                pltpu.make_async_remote_copy(
                    src_ref=ttot.at[par, pl.ds(pl.multiple_of(target * share, share), share)],
                    dst_ref=tpart.at[par, k - 1],
                    send_sem=sumssem.at[index],
                    recv_sem=sumrsem.at[index],
                    device_id=(g, target),
                    device_id_type=MESH,
                )
            )
        return copies

    def end_messages(pair):
        copies = []
        at = pl.ds(pl.multiple_of(s * share, share), share)
        for k in range(1, peers_seq):
            index = pair * (peers_seq - 1) + k - 1
            copies.append(
                pltpu.make_async_remote_copy(
                    src_ref=tdone.at[pair],
                    dst_ref=tall.at[pair, at],
                    send_sem=endssem.at[index],
                    recv_sem=endrsem.at[index],
                    device_id=(g, seq_peer(k)),
                    device_id_type=MESH,
                )
            )
        return copies

    def wide(pair):
        return pl.ds(pl.multiple_of(pair * (2 * LANES), 2 * LANES), 2 * LANES)

    def columns(pair, ty):
        return pl.ds(pl.multiple_of((pair * 2 + ty) * LANES, LANES), LANES)

    def loads(pair):
        par = lax.rem(pair, 2)
        copies = []
        for ty in range(2):
            for a in range(4):
                copies.append(
                    pltpu.make_async_copy(
                        sources[a].at[:, columns(pair, ty)], inb.at[par, ty, a], insem.at[ty * 4 + a]
                    )
                )
        return copies

    def stores(pair):
        copies = []
        for ty in range(2):
            for a in range(4):
                copies.append(
                    pltpu.make_async_copy(
                        stage.at[ty, a], outs[a].at[:, columns(pair, ty)], outsem.at[ty * 4 + a]
                    )
                )
        return copies

    def caption_stores():
        rows = tall.shape[1] // 2
        copies = []
        for pair in range(pairs):
            for a, out in enumerate((out_cap_keys, out_cap_values)):
                copies.append(
                    pltpu.make_async_copy(
                        tall.at[pair, pl.ds(a * rows, rows)],
                        out.at[0, :, wide(pair)],
                        outsem.at[8 + pair * 2 + a],
                    )
                )
        return copies

    def fill(base, count, read):
        def step(k, carry):
            pool[base + k] = read(k)
            return carry

        lax.fori_loop(0, count, step, 0)

    def fill_own(io, pair, ty):
        par = lax.rem(pair, 2)
        if io:
            fill(OWN, 6, lambda k: res[par, ty, k])
            return

        def step(j, carry):
            at = pl.ds(pl.multiple_of(j * TILE, TILE), TILE)
            for a in range(4):
                pool[OWN + j, a] = inb[par, ty, a, at, :]
            return carry

        lax.fori_loop(0, 6, step, 0)

    def fill_arrived(io, pair, ty):
        one = first_ring(io, pair)
        for sign in range(2):
            fill(DIRECT + sign * SLOTS, SLOTS, lambda k: recv_a[one, ty, sign, k])
            fill(FORWARD + sign * RELAY, RELAY, lambda k: recv_p[one, ty, sign, k])

    def fill_passing(io, pair, ty):
        two = second_ring(io, pair)
        for sign in range(2):
            fill(PASSING + sign * RELAY, RELAY, lambda k: recv_m[two, ty, sign, k])

    def fill_final(io, pair, ty):
        two = second_ring(io, pair)
        for sign in range(2):
            fill(FINAL + sign * SLOTS, RELAY, lambda k: recv_l[two, ty, sign, k])
            fill(
                FINAL + sign * SLOTS + RELAY,
                SLOTS - RELAY,
                lambda k: recv_m[two, ty, sign, RELAY + k],
            )

    def choose(ref, io, ty, entry, count, first, last, table=plan):
        for sign in range(2):

            def step(k, carry):
                ref[io, ty, sign, k] = pool[table[0, ty * P_SIZE + entry + sign * count + k]]
                return carry

            lax.fori_loop(first, last, step, 0)

    def begin(io, pair, ty, kind):
        for sign in range(2):
            message(io, pair, ty, sign, kind).start()

    def finish(io, pair, ty, kind):
        for sign in range(2):
            message(io, pair, ty, sign, kind).wait()

    def first_send(io, pair, ty, table=plan):
        fill_own(io, pair, ty)
        entry = P_BACK if io else P_SEND
        choose(send_a, io, ty, entry, SLOTS, 0, RELAY, table)
        begin(io, pair, ty, SEND)
        choose(send_a, io, ty, entry, SLOTS, RELAY, SLOTS, table)
        begin(io, pair, ty, SEND_NEAR)

    def pass_on(io, pair):
        for ty in range(2):
            finish(io, pair, ty, SEND)
            begin(io, pair, ty, PASS)

    def turn(io, pair):
        for ty in range(2):
            finish(io, pair, ty, SEND_NEAR)
            finish(io, pair, ty, PASS)
            if io == 0 and ty == 1:
                @pl.when(pair > 0)
                def _():
                    sent(pair - 1)

            fill_own(io, pair, ty)
            fill_arrived(io, pair, ty)
            entry = P_BACK_MID if io else P_MID
            choose(send_m, io, ty, entry, SLOTS, 0, RELAY)
            begin(io, pair, ty, MID)
            choose(send_m, io, ty, entry, SLOTS, RELAY, SLOTS)
            begin(io, pair, ty, MID_NEAR)

    def last_send(io, pair):
        for ty in range(2):
            finish(io, pair, ty, MID)
            fill_own(io, pair, ty)
            fill_arrived(io, pair, ty)
            fill_passing(io, pair, ty)
            choose(send_l, io, ty, P_BACK_LATE if io else P_LATE, RELAY, 0, RELAY)
            begin(io, pair, ty, LATE)

    def sent(pair):
        for sign in range(2):
            message(0, pair, 1, sign, MID_NEAR).wait_send()

    def final(io, pair, ty):
        if io == 0 and ty == 1:
            for sign in range(2):
                message(io, pair, ty, sign, MID_NEAR).wait_recv()
        else:
            finish(io, pair, ty, MID_NEAR)
        finish(io, pair, ty, LATE)
        fill_own(io, pair, ty)
        fill_arrived(io, pair, ty)
        fill_final(io, pair, ty)

    def compute(pair, ty):
        par = lax.rem(pair, 2)
        bf16, f32 = jnp.bfloat16, jnp.float32
        scale = HEAD_DIM**-0.5
        lane = lax.broadcasted_iota(jnp.int32, (TILE, LANES), 1) < HEAD_DIM
        text_row = lax.broadcasted_iota(jnp.int32, (TILE, LANES), 0)
        contract_lanes = (((1,), (1,)), ((), ()))
        first = mine[0, T_COUNT]
        second = first + mine[0, T_COUNT + 1]
        text = 3 * TILE

        def begin_of(i):
            return jnp.where(i == 0, 0, jnp.where(i == 1, first, second))

        def half(tile, h):
            return jnp.where(lane if h == 0 else jnp.logical_not(lane), tile, jnp.zeros_like(tile))

        def prepare(i, carry):
            tiles = mine[0, T_COUNT + i]
            caption = mine[0, T_CAPTION + i]
            for j in range(4):
                at = slice(j * TILE, (j + 1) * TILE)
                if j < 3:
                    place = plan[0, ty * P_SIZE + P_IMAGE + i * 3 + j]
                    k, v = pool[place, 1], pool[place, 2]
                    live = jnp.where(j < tiles, 1.0, 0.0)
                    qm[i, at, :] = (pool[place, 0].astype(f32) * (live * scale)).astype(bf16)
                    dm[i, at, :] = (pool[place, 3].astype(f32) * live).astype(bf16)
                else:
                    k, v = txt[0, caption], txt[1, caption]
                kk[i, at, :] = k
                vv[i, at, :] = v
                kt[i, :, at] = k.T
                vt[i, :, at] = v.T
            return carry

        lax.fori_loop(0, 3, prepare, 0)

        def query(r, carry):
            i = jnp.where(r >= first, 1, 0) + jnp.where(r >= second, 1, 0)
            j = jnp.minimum(r - begin_of(i), 2)
            tiles = mine[0, T_COUNT + i]
            length = plan[0, P_LENGTH + i]
            place = plan[0, ty * P_SIZE + P_IMAGE + i * 3 + j]
            q = pool[place, 0] * jnp.asarray(scale, bf16)
            do = pool[place, 3]
            k, v = kk[i], vv[i]
            hide = [0.0] + [jnp.where(n < tiles, 0.0, -1e30) for n in (1, 2)]
            hide.append(jnp.where(text_row < length, 0.0, -1e30))
            o_parts, dq_parts = [], []
            for h in range(2):
                scores = lax.dot_general(k, half(q, h), contract_lanes, preferred_element_type=f32)
                scores = jnp.concatenate(
                    [scores[n * TILE : (n + 1) * TILE] + hide[n] for n in range(4)], axis=0
                )
                weights = jnp.exp(scores - jnp.max(scores, axis=0, keepdims=True))
                probs = weights * (1.0 / jnp.sum(weights, axis=0, keepdims=True))
                dprobs = lax.dot_general(v, half(do, h), contract_lanes, preferred_element_type=f32)
                total = jnp.sum(probs * dprobs, axis=0, keepdims=True)
                dscores = (probs * (dprobs - total)).astype(bf16)
                low = probs.astype(bf16)
                for n in range(4):
                    ps[r, h, n] = low[n * TILE : (n + 1) * TILE]
                    ds[r, h, n] = dscores[n * TILE : (n + 1) * TILE]
                span = slice(h * HEAD_DIM, (h + 1) * HEAD_DIM)
                o_parts.append(jnp.dot(vt[i, span, :], low, preferred_element_type=f32))
                dq_parts.append(jnp.dot(kt[i, span, :], dscores, preferred_element_type=f32))
            o = jnp.concatenate(o_parts, axis=0).T
            dq = jnp.concatenate(dq_parts, axis=0).T * scale
            res[par, ty, r, 0] = o.astype(bf16)
            res[par, ty, r, 1] = dq.astype(bf16)
            return carry

        def query_two(r, carry):
            query(2 * r, carry)
            return query(2 * r + 1, carry)

        lax.fori_loop(0, 3, query_two, 0)

        def key_grads(i, block):
            begin_i = begin_of(i)
            rows = [jnp.minimum(begin_i + n, 5) for n in range(3)]
            q, do = qm[i], dm[i]
            dk, dv = [], []
            for h in range(2):
                low = jnp.concatenate([ps[r, h, block] for r in rows], axis=1)
                dscores = jnp.concatenate([ds[r, h, block] for r in rows], axis=1)
                dk.append(jnp.dot(dscores, q, preferred_element_type=f32))
                dv.append(jnp.dot(low, do, preferred_element_type=f32))
            return jnp.where(lane, dk[0], dk[1]), jnp.where(lane, dv[0], dv[1])

        def key(r, carry):
            i = jnp.where(r >= first, 1, 0) + jnp.where(r >= second, 1, 0)
            dk, dv = key_grads(i, jnp.minimum(r - begin_of(i), 2))
            res[par, ty, r, 2] = dk.astype(bf16)
            res[par, ty, r, 3] = dv.astype(bf16)
            return carry

        lax.fori_loop(0, 6, key, 0)

        def caption_key(i, carry):
            dk, dv = key_grads(i, 3)
            tgrad[i, 0] = dk
            tgrad[i, 1] = dv
            return carry

        lax.fori_loop(0, 3, caption_key, 0)

        def spread(c, a):
            hits = [jnp.where(mine[0, T_CAPTION + i] == c, 1.0, 0.0) for i in range(3)]
            return tgrad[0, a] * hits[0] + tgrad[1, a] * hits[1] + tgrad[2, a] * hits[2]

        def settle(c, carry):
            for a in range(2):
                tsend[ty, c, a] = spread(c, a).astype(bf16)
            return carry

        lax.fori_loop(0, peers_grp, settle, 0)
        for a in range(2):
            tself[ty, a] = spread(g, a)

    def captions_in(pair, ty):
        def current(c, carry):
            for a in range(2):
                txt[a, c] = caps[pair, c, a, :, ty * LANES : (ty + 1) * LANES]
            return carry

        lax.fori_loop(0, peers_grp, current, 0)

    def work(pair, ty):
        final(0, pair, ty)
        captions_in(pair, ty)
        compute(pair, ty)
        first_send(1, pair, ty)
        for k in range(1, peers_grp):
            text_message(lax.rem(pair, 2), ty, k).start()

    def home(pair):
        @pl.when(pair > 0)
        def _():
            for copy in stores(pair - 1):
                copy.wait()

        for ty in range(2):
            final(1, pair, ty)

            def place(j, carry):
                at = pl.ds(pl.multiple_of(j * TILE, TILE), TILE)
                for a in range(4):
                    stage[ty, a, at, :] = pool[plan[0, ty * P_SIZE + P_HOME + j], a]
                return carry

            lax.fori_loop(0, 6, place, 0)
        for copy in stores(pair):
            copy.start()

    def add_captions(pair):
        par = lax.rem(pair, 2)
        for ty in range(2):
            for k in range(1, peers_grp):
                text_message(par, ty, k).wait()
            at = slice(ty * LANES, (ty + 1) * LANES)
            for a in range(2):
                total = tself[ty, a]
                for k in range(1, peers_grp):
                    total = total + trecv[par, ty, k - 1, a].astype(jnp.float32)
                tsum[a * TILE : (a + 1) * TILE, at] = total
                ttot[par, a * TILE : (a + 1) * TILE, at] = total.astype(ttot.dtype)
        for copy in sum_messages(par):
            copy.start()

    def end_captions(pair):
        par = lax.rem(pair, 2)
        for copy in sum_messages(par):
            copy.wait()
        at = pl.ds(pl.multiple_of(s * share, share), share)
        total = tsum[at, :]
        for k in range(1, peers_seq):
            total = total + tpart[par, k - 1].astype(jnp.float32)
        done = total.astype(tdone.dtype)
        tdone[pair] = done
        tall[pair, at, :] = done
        for copy in end_messages(pair):
            copy.start()

    for copy in loads(0):
        copy.start()
    own_rows = mine_rows[...]
    tab_seq[s] = own_rows
    tab_grp[g] = own_rows

    def publish(values, place):
        plan_rows[...] = values
        copy = pltpu.make_async_copy(plan_rows, place, plansem)
        copy.start()
        copy.wait()

    source = lax.broadcasted_iota(jnp.int32, (peers_seq, LANES), 0)
    alone = jnp.where(source == s, jnp.concatenate([own_rows] * (peers_seq // 8), axis=0), -1)
    publish(make_plan(alone, mine, None, s), plan_own)
    pl.semaphore_wait(barrier, peers_seq + peers_grp - 2)
    for copy in table_messages():
        copy.start()
    for copy in loads(0):
        copy.wait()
    for ty in range(2):
        first_send(0, jnp.int32(0), ty, plan_own)
    for pair in range(pairs):
        for copy in caption_messages(pair):
            copy.start()
    for copy in table_messages():
        copy.wait()
    publish(make_plan(tab_seq[:, 0, :], mine, tab_grp[:, 0, :], s), plan)

    for copy in loads(1):
        copy.start()

    def superstep(step, carry):
        entering = step < pairs
        working = (step >= 1) & (step <= pairs)
        leaving = step >= 2

        def following():
            for copy in loads(step + 1):
                copy.wait()
            for ty in range(2):
                first_send(0, step + 1, ty)

        @pl.when(entering)
        def _():
            pass_on(0, step)

        @pl.when(working)
        def _():
            for copy in caption_messages(step - 1):
                copy.wait()
            work(step - 1, 0)

        @pl.when(entering)
        def _():
            turn(0, step)

        @pl.when(leaving)
        def _():
            last_send(1, step - 2)

        @pl.when(working)
        def _():
            work(step - 1, 1)

        @pl.when(working)
        def _():
            pass_on(1, step - 1)

        @pl.when(entering)
        def _():
            last_send(0, step)

        @pl.when(leaving)
        def _():
            end_captions(step - 2)

        @pl.when((step >= 1) & (step + 1 < pairs))
        def _():
            for copy in loads(step + 1):
                copy.start()

        @pl.when(leaving)
        def _():
            home(step - 2)

        @pl.when(working)
        def _():
            add_captions(step - 1)

        @pl.when(step == 0)
        def _():
            following()

        @pl.when(working)
        def _():
            turn(1, step - 1)

        @pl.when((step >= 1) & (step + 1 < pairs))
        def _():
            following()

        return carry

    lax.fori_loop(0, pairs + 2, superstep, 0)
    sent(pairs - 1)
    for pair in range(pairs):
        for copy in end_messages(pair):
            copy.wait()
    for copy in caption_stores():
        copy.start()
    for copy in stores(pairs - 1):
        copy.wait()
    for copy in caption_stores():
        copy.wait()


def copy_kernel(*refs):
    count = len(refs) // 2
    for source, target in zip(refs[:count], refs[count:]):
        target[...] = source[...]


def body(
    image_queries,
    image_keys,
    image_values,
    cotangent,
    text_keys,
    text_values,
    text_lengths,
    send_owner,
    recv_source,
    tile_counts,
    caption_ids,
):
    rows, width = image_queries.shape
    peers_grp, peers_seq = lax.axis_size("grp"), lax.axis_size("seq")
    pairs = width // (2 * LANES)
    mine = jnp.concatenate(
        [send_owner[0], recv_source[0], tile_counts[0], caption_ids[0], text_lengths]
    ).astype(jnp.int32)
    mine = jnp.broadcast_to(jnp.pad(mine, (0, LANES - mine.shape[0]))[None, :], (8, LANES))
    vmem = pl.BlockSpec(memory_space=pltpu.VMEM)
    smem = pl.BlockSpec(memory_space=pltpu.SMEM)
    anywhere = pl.BlockSpec(memory_space=pl.ANY)
    bf16, f32 = jnp.bfloat16, jnp.float32
    quad = (4, TILE, LANES)
    text_rows = text_keys.shape[1]
    image = jax.ShapeDtypeStruct((rows, width), bf16)
    caption = jax.ShapeDtypeStruct(text_keys.shape, bf16)
    dma = pltpu.SemaphoreType.DMA
    scratch = [
        pltpu.VMEM((peers_seq, 8, LANES), jnp.int32),
        pltpu.VMEM((peers_grp, 8, LANES), jnp.int32),
        pltpu.VMEM((8, 2 * P_SIZE), jnp.int32),
        pltpu.SMEM((8, 2 * P_SIZE), jnp.int32),
        pltpu.SMEM((8, 2 * P_SIZE), jnp.int32),
        pltpu.VMEM((2, 2, 4, rows, LANES), bf16),
        pltpu.VMEM((pairs, peers_grp, 2, text_rows, 2 * LANES), bf16),
        pltpu.VMEM((2, peers_grp, text_rows, LANES), bf16),
        pltpu.VMEM((2, 2, 2, SLOTS) + quad, bf16),
        pltpu.VMEM((2 + pairs, 2, 2, SLOTS) + quad, bf16),
        pltpu.VMEM((2 + pairs, 2, 2, RELAY) + quad, bf16),
        pltpu.VMEM((2, 2, 2, SLOTS) + quad, bf16),
        pltpu.VMEM((4, 2, 2, SLOTS) + quad, bf16),
        pltpu.VMEM((2, 2, 2, RELAY) + quad, bf16),
        pltpu.VMEM((4, 2, 2, RELAY) + quad, bf16),
        pltpu.VMEM((POOL,) + quad, bf16),
        pltpu.VMEM((2, 2, 6) + quad, bf16),
        pltpu.VMEM((2, 4, rows, LANES), bf16),
        pltpu.VMEM((3, 4 * TILE, LANES), bf16),
        pltpu.VMEM((3, 4 * TILE, LANES), bf16),
        pltpu.VMEM((3, LANES, 4 * TILE), bf16),
        pltpu.VMEM((3, LANES, 4 * TILE), bf16),
        pltpu.VMEM((3, 3 * TILE, LANES), bf16),
        pltpu.VMEM((3, 3 * TILE, LANES), bf16),
        pltpu.VMEM((6, 2, 4, TILE, TILE), bf16),
        pltpu.VMEM((6, 2, 4, TILE, TILE), bf16),
        pltpu.VMEM((3, 2, TILE, LANES), f32),
        pltpu.VMEM((2, 2, text_rows, LANES), f32),
        pltpu.VMEM((2, peers_grp, 2, text_rows, LANES), bf16),
        pltpu.VMEM((2, 2, peers_grp - 1, 2, text_rows, LANES), bf16),
        pltpu.VMEM((2 * text_rows, 2 * LANES), f32),
        pltpu.VMEM((2, 2 * text_rows, 2 * LANES), bf16),
        pltpu.VMEM((2, peers_seq - 1, 2 * text_rows // peers_seq, 2 * LANES), bf16),
        pltpu.VMEM((pairs, 2 * text_rows // peers_seq, 2 * LANES), bf16),
        pltpu.VMEM((pairs, 2 * text_rows, 2 * LANES), bf16),
        dma((4 * (2 + pairs) * KINDS,)),
        dma((4 * (2 + pairs) * KINDS,)),
        dma((peers_seq + peers_grp - 2,)),
        dma((peers_seq + peers_grp - 2,)),
        dma((pairs * 2 * (peers_grp - 1),)),
        dma((pairs * 2 * (peers_grp - 1),)),
        dma((4 * (peers_grp - 1),)),
        dma((4 * (peers_grp - 1),)),
        dma((2 * (peers_seq - 1),)),
        dma((2 * (peers_seq - 1),)),
        dma((pairs * (peers_seq - 1),)),
        dma((pairs * (peers_seq - 1),)),
        dma((8 + 2 * pairs,)),
        dma((8 + 2 * pairs,)),
        dma,
    ]
    results = pl.pallas_call(
        functools.partial(main_kernel, peers_grp, peers_seq, pairs),
        out_shape=(image, image, image, image, caption, caption),
        in_specs=[smem, vmem] + [anywhere] * 6,
        out_specs=(anywhere,) * 6,
        scratch_shapes=scratch,
        compiler_params=pltpu.CompilerParams(
            collective_id=0, has_side_effects=True, vmem_limit_bytes=63 * 2**20
        ),
        name="attend",
    )(mine, mine, image_queries, image_keys, image_values, cotangent, text_keys, text_values)
    steps = 4
    blocks = [
        pl.BlockSpec((rows // steps, width), lambda i: (i, 0)),
        pl.BlockSpec((1, text_rows // steps, width), lambda i: (0, i, 0)),
    ]
    specs = [blocks[0]] * 4 + [blocks[1]] * 2
    return pl.pallas_call(
        copy_kernel,
        grid=(steps,),
        out_shape=(image, image, image, image, caption, caption),
        in_specs=specs,
        out_specs=tuple(specs),
        name="results",
    )(*results)


def solution(mesh):
    tokens = P(("grp", "seq"), None)
    captions = P("grp", None, None)
    return jax.shard_map(
        body,
        mesh=mesh,
        in_specs=(tokens,) * 4 + (captions, captions, P("grp")) + (tokens,) * 4,
        out_specs=(tokens,) * 4 + (captions, captions),
        check_vma=False,
    )
```

```python
import functools

import jax
import jax.numpy as jnp
from jax import lax
from jax.experimental import pallas as pl
from jax.experimental.pallas import tpu as pltpu
from jax.sharding import PartitionSpec as P

HEAD_DIM = 64
LANES = 128
TILE = 128
MESH = pl.DeviceIdType.MESH

RING = 4
SLOTS = 4
RELAY = 2

OWN = 0
DIRECT = 6
FORWARD = 14
FINAL = 18
PASSING = 26
POOL = 30

P_SEND = 0
P_MID = 8
P_LATE = 16
P_IMAGE = 20
P_BACK = 32
P_BACK_MID = 40
P_BACK_LATE = 48
P_HOME = 52
P_LENGTH = 58
P_SIZE = 64

T_RECV, T_COUNT, T_CAPTION, T_LENGTH = 6, 12, 15, 18

SEND, SEND_NEAR, PASS, MID, MID_NEAR, LATE = range(6)
KINDS = 6


def make_plan(tab, row_ref, lengths, me):
    peers = tab.shape[0]
    src = lax.broadcasted_iota(jnp.int32, (peers, LANES), 0)
    own = lax.broadcasted_iota(jnp.int32, (peers, LANES), 1)
    sends = jnp.zeros((peers, LANES), jnp.int32)
    place = jnp.zeros((peers, LANES), jnp.int32)
    for j in range(6):
        hit = (tab[:, j : j + 1] == own).astype(jnp.int32)
        sends += hit
        place += hit * j
    first = row_ref[0, T_COUNT]
    second = first + row_ref[0, T_COUNT + 1]
    result = jnp.zeros((peers, LANES), jnp.int32)
    for r in range(6):
        result += jnp.where(src == row_ref[0, T_RECV + r], r, 0)

    lower = (
        lax.broadcasted_iota(jnp.int32, (peers, peers), 1)
        < lax.broadcasted_iota(jnp.int32, (peers, peers), 0)
    ).astype(jnp.float32)
    upper = (
        lax.broadcasted_iota(jnp.int32, (LANES, LANES), 0)
        < lax.broadcasted_iota(jnp.int32, (LANES, LANES), 1)
    ).astype(jnp.float32)
    live = sends > 0
    coord = {"y": lambda t: lax.rem(t, RING), "z": lambda t: lax.div(t, RING) % RING}

    def slots(step, axis):
        count, rank = [], []
        for d in (1, 2, 3):
            picked = jnp.where(live & (step == d), 1.0, 0.0)
            if axis == 1:
                before = jnp.dot(picked, upper, preferred_element_type=jnp.float32)
            else:
                before = jnp.dot(lower, picked, preferred_element_type=jnp.float32)
            rank.append(before.astype(jnp.int32))
            count.append(jnp.sum(picked, axis=axis, keepdims=True).astype(jnp.int32))
        plus = jnp.minimum(jnp.minimum(RELAY, SLOTS - count[0]), count[1])
        code = jnp.where(
            step == 0,
            0,
            jnp.where(
                step == 1, 1, jnp.where(step == 3, 2, jnp.where(rank[1] < plus, 3, 4))
            ),
        )
        slot = jnp.where(
            code == 1,
            SLOTS - 1 - rank[0],
            jnp.where(
                code == 2,
                SLOTS - 1 - rank[2],
                jnp.where(code == 3, rank[1], rank[1] - plus),
            ),
        )
        return code, slot

    def arrived(code, slot, stay, flip):
        base = (DIRECT + SLOTS, DIRECT, FORWARD + RELAY, FORWARD) if flip else (
            DIRECT, DIRECT + SLOTS, FORWARD, FORWARD + RELAY)
        return jnp.where(
            code == 0,
            stay,
            slot
            + jnp.where(
                code == 1,
                base[0],
                jnp.where(code == 2, base[1], jnp.where(code == 3, base[2], base[3])),
            ),
        )

    def settled(code, slot, stay, flip):
        odd = (code == 1) | (code == 3)
        near, far = (FINAL + SLOTS, FINAL) if flip else (FINAL, FINAL + SLOTS)
        return jnp.where(code == 0, stay, slot + jnp.where(odd, near, far))

    zero_row = jnp.zeros((1, LANES), jnp.float32)
    rows = []
    for ring_a, ring_b in (("y", "z"), ("z", "y")):
        at_a, at_b = coord[ring_a], coord[ring_b]
        src_a, src_b, own_a, own_b = at_a(src), at_b(src), at_a(own), at_b(own)
        me_a, me_b = at_a(me), at_b(me)
        code_a, slot_a = slots(lax.rem(own_a - src_a + RING, RING), 1)
        code_b, slot_b = slots(lax.rem(own_b - src_b + RING, RING), 0)
        there = arrived(code_a, slot_a, place, False)
        there_end = settled(code_b, slot_b, there, False)
        back = arrived(code_b, slot_b, result, True)
        back_end = settled(code_a, slot_a, back, True)
        mine_src = live & (src == me)
        mine_own = live & (own == me)
        crossing = live & (own_a == me_a) & (src_b == me_b)
        part = {}

        def put(entry, condition, value):
            row = jnp.sum(
                jnp.where(condition, value, 0).astype(jnp.float32), axis=0, keepdims=True
            )
            part[entry] = part[entry] + row if entry in part else row

        def channel(code, sign, flip):
            sign = 1 - sign if flip else sign
            return (code == 1 + sign), (code == 3 + sign)

        for sign in (0, 1):
            ahead = 1 if sign == 0 else RING - 1
            near, far = channel(code_a, sign, False)
            for k in range(SLOTS):
                put(P_SEND + sign * SLOTS + k, mine_src & (near | far) & (slot_a == k), place)
            near, far = channel(code_b, sign, False)
            passing = live & (own_a == me_a) & far & (lax.rem(own_b - me_b + RING, RING) == ahead)
            for k in range(RELAY):
                put(P_MID + sign * SLOTS + k, crossing & far & (slot_b == k), there)
                put(P_LATE + sign * RELAY + k, crossing & near & (slot_b == k), there)
                put(P_LATE + sign * RELAY + k, passing & (slot_b == k), PASSING + sign * RELAY + k)
            for k in range(RELAY, SLOTS):
                put(P_MID + sign * SLOTS + k, crossing & near & (slot_b == k), there)
            near, far = channel(code_b, sign, True)
            for k in range(SLOTS):
                put(P_BACK + sign * SLOTS + k, mine_own & (near | far) & (slot_b == k), result)
            near, far = channel(code_a, sign, True)
            passing = live & (src_b == me_b) & far & (lax.rem(src_a - me_a + RING, RING) == ahead)
            for k in range(RELAY):
                put(P_BACK_MID + sign * SLOTS + k, crossing & far & (slot_a == k), back)
                put(P_BACK_LATE + sign * RELAY + k, crossing & near & (slot_a == k), back)
                put(P_BACK_LATE + sign * RELAY + k, passing & (slot_a == k), PASSING + sign * RELAY + k)
            for k in range(RELAY, SLOTS):
                put(P_BACK_MID + sign * SLOTS + k, crossing & near & (slot_a == k), back)
        begins = (0, first, second)
        for i in range(3):
            for j in range(3):
                r = jnp.minimum(begins[i] + j, 5)
                put(P_IMAGE + i * 3 + j, mine_own & (src == row_ref[0, T_RECV + r]), there_end)
        for j in range(6):
            put(P_HOME + j, mine_src & (place == j), back_end)
        if lengths is not None:
            captions = lax.broadcasted_iota(jnp.int32, lengths.shape, 0)
            column = lax.broadcasted_iota(jnp.int32, lengths.shape, 1) == T_LENGTH
            for i in range(3):
                put(P_LENGTH + i, column & (captions == row_ref[0, T_CAPTION + i]), lengths)
        rows.extend(part.get(entry, zero_row) for entry in range(P_SIZE))
    matrix = jnp.concatenate(rows, axis=0)
    ones = jnp.ones((8, LANES), jnp.float32)
    out = lax.dot_general(ones, matrix, (((1,), (1,)), ((), ())), preferred_element_type=jnp.float32)
    out = out.astype(jnp.int32)
    entry = lax.broadcasted_iota(jnp.int32, out.shape, 1) % P_SIZE
    return jnp.where(entry < P_LENGTH, jnp.clip(out, 0, POOL - 1), out)


def main_kernel(
    peers_grp,
    peers_seq,
    pairs,
    mine,
    mine_rows,
    queries,
    keys,
    values,
    grads,
    cap_keys,
    cap_values,
    out_rows,
    out_queries,
    out_keys,
    out_values,
    out_cap_keys,
    out_cap_values,
    tab_seq,
    tab_grp,
    plan_rows,
    plan_own,
    plan,
    inb,
    caps,
    txt,
    send_a,
    recv_a,
    recv_p,
    send_m,
    recv_m,
    send_l,
    recv_l,
    pool,
    res,
    stage,
    kk,
    vv,
    kt,
    vt,
    qm,
    dm,
    ps,
    ds,
    tgrad,
    tself,
    tsend,
    trecv,
    tsum,
    ttot,
    tpart,
    tdone,
    tall,
    ssem,
    rsem,
    tabssem,
    tabrsem,
    capssem,
    caprsem,
    tssem,
    trsem,
    sumssem,
    sumrsem,
    endssem,
    endrsem,
    insem,
    outsem,
    plansem,
):
    g = lax.axis_index("grp")
    s = lax.axis_index("seq")
    z, y = lax.div(s, RING), lax.rem(s, RING)
    sources = (queries, keys, values, grads)
    outs = (out_rows, out_queries, out_keys, out_values)

    def neighbour(ring, sign):
        step = 1 if sign == 0 else RING - 1
        if ring == "y":
            return (g, z * RING + lax.rem(y + step, RING))
        return (g, lax.rem(z + step, RING) * RING + y)

    def group_peer(k):
        return lax.rem(g + k, peers_grp)

    def seq_peer(k):
        return lax.rem(s + k, peers_seq)

    barrier = pltpu.get_barrier_semaphore()
    for k in range(1, peers_seq):
        pl.semaphore_signal(barrier, inc=1, device_id=(g, seq_peer(k)), device_id_type=MESH)
    for k in range(1, peers_grp):
        pl.semaphore_signal(barrier, inc=1, device_id=(group_peer(k), s), device_id_type=MESH)

    def first_ring(io, pair):
        return 2 + pair if io else lax.rem(pair, 2)

    def second_ring(io, pair):
        return io * 2 + lax.rem(pair, 2)

    def message(io, pair, ty, sign, kind):
        ring = "y" if (ty + io + (1 if kind >= MID else 0)) % 2 == 0 else "z"
        far, near = pl.ds(0, RELAY), pl.ds(RELAY, SLOTS - RELAY)
        one, two = first_ring(io, pair), second_ring(io, pair)
        if kind in (SEND, SEND_NEAR):
            at = far if kind == SEND else near
            src, dst = send_a.at[io, ty, sign, at], recv_a.at[one, ty, sign, at]
        elif kind == PASS:
            src, dst = recv_a.at[one, ty, sign, far], recv_p.at[one, ty, sign]
        elif kind in (MID, MID_NEAR):
            at = far if kind == MID else near
            src, dst = send_m.at[io, ty, sign, at], recv_m.at[two, ty, sign, at]
        else:
            src, dst = send_l.at[io, ty, sign], recv_l.at[two, ty, sign]
        index = ((one * 2 + ty) * 2 + sign) * KINDS + kind
        return pltpu.make_async_remote_copy(
            src_ref=src,
            dst_ref=dst,
            send_sem=ssem.at[index],
            recv_sem=rsem.at[index],
            device_id=neighbour(ring, sign),
            device_id_type=MESH,
        )

    def text_message(par, ty, k):
        index = (par * 2 + ty) * (peers_grp - 1) + k - 1
        target = group_peer(k)
        return pltpu.make_async_remote_copy(
            src_ref=tsend.at[ty, target],
            dst_ref=trecv.at[par, ty, k - 1],
            send_sem=tssem.at[index],
            recv_sem=trsem.at[index],
            device_id=(target, s),
            device_id_type=MESH,
        )

    def table_messages():
        copies = []
        for k in range(1, peers_seq + peers_grp - 1):
            seq = k < peers_seq
            copies.append(
                pltpu.make_async_remote_copy(
                    src_ref=mine_rows,
                    dst_ref=tab_seq.at[s] if seq else tab_grp.at[g],
                    send_sem=tabssem.at[k - 1],
                    recv_sem=tabrsem.at[k - 1],
                    device_id=(g, seq_peer(k)) if seq else (group_peer(k - peers_seq + 1), s),
                    device_id_type=MESH,
                )
            )
        return copies

    def caption_messages(pair):
        copies = []
        for a, cap in enumerate((cap_keys, cap_values)):
            src = cap.at[0, :, wide(pair)]
            dst = caps.at[pair, g, a]
            for k in range(1, peers_grp):
                index = (pair * 2 + a) * (peers_grp - 1) + k - 1
                copies.append(
                    pltpu.make_async_remote_copy(
                        src_ref=src,
                        dst_ref=dst,
                        send_sem=capssem.at[index],
                        recv_sem=caprsem.at[index],
                        device_id=(group_peer(k), s),
                        device_id_type=MESH,
                    )
                )
            copies.append(pltpu.make_async_copy(src, dst, insem.at[8 + pair * 2 + a]))
        return copies

    share = 16

    def sum_messages(par):
        copies = []
        for k in range(1, peers_seq):
            target = seq_peer(k)
            index = par * (peers_seq - 1) + k - 1
            copies.append(
                pltpu.make_async_remote_copy(
                    src_ref=ttot.at[par, pl.ds(pl.multiple_of(target * share, share), share)],
                    dst_ref=tpart.at[par, k - 1],
                    send_sem=sumssem.at[index],
                    recv_sem=sumrsem.at[index],
                    device_id=(g, target),
                    device_id_type=MESH,
                )
            )
        return copies

    def end_messages(pair):
        copies = []
        at = pl.ds(pl.multiple_of(s * share, share), share)
        for k in range(1, peers_seq):
            index = pair * (peers_seq - 1) + k - 1
            copies.append(
                pltpu.make_async_remote_copy(
                    src_ref=tdone.at[pair],
                    dst_ref=tall.at[pair, at],
                    send_sem=endssem.at[index],
                    recv_sem=endrsem.at[index],
                    device_id=(g, seq_peer(k)),
                    device_id_type=MESH,
                )
            )
        return copies

    def wide(pair):
        return pl.ds(pl.multiple_of(pair * (2 * LANES), 2 * LANES), 2 * LANES)

    def columns(pair, ty):
        return pl.ds(pl.multiple_of((pair * 2 + ty) * LANES, LANES), LANES)

    def loads(pair):
        par = lax.rem(pair, 2)
        copies = []
        for ty in range(2):
            for a in range(4):
                copies.append(
                    pltpu.make_async_copy(
                        sources[a].at[:, columns(pair, ty)], inb.at[par, ty, a], insem.at[ty * 4 + a]
                    )
                )
        return copies

    def stores(pair):
        copies = []
        for ty in range(2):
            for a in range(4):
                copies.append(
                    pltpu.make_async_copy(
                        stage.at[ty, a], outs[a].at[:, columns(pair, ty)], outsem.at[ty * 4 + a]
                    )
                )
        return copies

    def caption_stores():
        rows = tall.shape[1] // 2
        copies = []
        for pair in range(pairs):
            for a, out in enumerate((out_cap_keys, out_cap_values)):
                copies.append(
                    pltpu.make_async_copy(
                        tall.at[pair, pl.ds(a * rows, rows)],
                        out.at[0, :, wide(pair)],
                        outsem.at[8 + pair * 2 + a],
                    )
                )
        return copies

    def fill(base, count, read):
        def step(k, carry):
            pool[base + 2 * k] = read(2 * k)
            pool[base + 2 * k + 1] = read(2 * k + 1)
            return carry

        lax.fori_loop(0, count // 2, step, 0)

    def fill_own(io, pair, ty):
        par = lax.rem(pair, 2)
        if io:
            fill(OWN, 6, lambda k: res[par, ty, k])
            return

        def step(j, carry):
            at = pl.ds(pl.multiple_of(j * TILE, TILE), TILE)
            for a in range(4):
                pool[OWN + j, a] = inb[par, ty, a, at, :]
            return carry

        lax.fori_loop(0, 6, step, 0)

    def fill_arrived(io, pair, ty):
        one = first_ring(io, pair)
        for sign in range(2):
            fill(DIRECT + sign * SLOTS, SLOTS, lambda k: recv_a[one, ty, sign, k])
            fill(FORWARD + sign * RELAY, RELAY, lambda k: recv_p[one, ty, sign, k])

    def fill_passing(io, pair, ty):
        two = second_ring(io, pair)
        for sign in range(2):
            fill(PASSING + sign * RELAY, RELAY, lambda k: recv_m[two, ty, sign, k])

    def fill_final(io, pair, ty):
        two = second_ring(io, pair)
        for sign in range(2):
            fill(FINAL + sign * SLOTS, RELAY, lambda k: recv_l[two, ty, sign, k])
            fill(
                FINAL + sign * SLOTS + RELAY,
                SLOTS - RELAY,
                lambda k: recv_m[two, ty, sign, RELAY + k],
            )

    def choose(ref, io, ty, entry, count, first, last, table=plan):
        for sign in range(2):

            def step(k, carry):
                ref[io, ty, sign, k] = pool[table[0, ty * P_SIZE + entry + sign * count + k]]
                return carry

            lax.fori_loop(first, last, step, 0)

    def begin(io, pair, ty, kind):
        for sign in range(2):
            message(io, pair, ty, sign, kind).start()

    def finish(io, pair, ty, kind):
        for sign in range(2):
            message(io, pair, ty, sign, kind).wait()

    def first_send(io, pair, ty, table=plan):
        fill_own(io, pair, ty)
        entry = P_BACK if io else P_SEND
        choose(send_a, io, ty, entry, SLOTS, 0, RELAY, table)
        begin(io, pair, ty, SEND)
        choose(send_a, io, ty, entry, SLOTS, RELAY, SLOTS, table)
        begin(io, pair, ty, SEND_NEAR)

    def pass_on(io, pair):
        for ty in range(2):
            finish(io, pair, ty, SEND)
            begin(io, pair, ty, PASS)

    def turn(io, pair):
        for ty in range(2):
            finish(io, pair, ty, SEND_NEAR)
            finish(io, pair, ty, PASS)
            if io == 0 and ty == 1:
                @pl.when(pair > 0)
                def _():
                    sent(pair - 1)

            fill_own(io, pair, ty)
            fill_arrived(io, pair, ty)
            entry = P_BACK_MID if io else P_MID
            choose(send_m, io, ty, entry, SLOTS, 0, RELAY)
            begin(io, pair, ty, MID)
            choose(send_m, io, ty, entry, SLOTS, RELAY, SLOTS)
            begin(io, pair, ty, MID_NEAR)

    def last_send(io, pair):
        for ty in range(2):
            finish(io, pair, ty, MID)
            fill_own(io, pair, ty)
            fill_arrived(io, pair, ty)
            fill_passing(io, pair, ty)
            choose(send_l, io, ty, P_BACK_LATE if io else P_LATE, RELAY, 0, RELAY)
            begin(io, pair, ty, LATE)

    def sent(pair):
        for sign in range(2):
            message(0, pair, 1, sign, MID_NEAR).wait_send()

    def final(io, pair, ty):
        if io == 0 and ty == 1:
            for sign in range(2):
                message(io, pair, ty, sign, MID_NEAR).wait_recv()
        else:
            finish(io, pair, ty, MID_NEAR)
        finish(io, pair, ty, LATE)
        fill_own(io, pair, ty)
        fill_arrived(io, pair, ty)
        fill_final(io, pair, ty)

    def compute(pair, ty):
        par = lax.rem(pair, 2)
        bf16, f32 = jnp.bfloat16, jnp.float32
        scale = HEAD_DIM**-0.5
        lane = lax.broadcasted_iota(jnp.int32, (TILE, LANES), 1) < HEAD_DIM
        text_row = lax.broadcasted_iota(jnp.int32, (TILE, LANES), 0)
        contract_lanes = (((1,), (1,)), ((), ()))
        first = mine[0, T_COUNT]
        second = first + mine[0, T_COUNT + 1]
        text = 3 * TILE

        def begin_of(i):
            return jnp.where(i == 0, 0, jnp.where(i == 1, first, second))

        def half(tile, h):
            return jnp.where(lane if h == 0 else jnp.logical_not(lane), tile, jnp.zeros_like(tile))

        def prepare(i, carry):
            tiles = mine[0, T_COUNT + i]
            caption = mine[0, T_CAPTION + i]
            for j in range(4):
                at = slice(j * TILE, (j + 1) * TILE)
                if j < 3:
                    place = plan[0, ty * P_SIZE + P_IMAGE + i * 3 + j]
                    k, v = pool[place, 1], pool[place, 2]
                    live = jnp.where(j < tiles, 1.0, 0.0)
                    qm[i, at, :] = (pool[place, 0].astype(f32) * (live * scale)).astype(bf16)
                    dm[i, at, :] = (pool[place, 3].astype(f32) * live).astype(bf16)
                else:
                    k, v = txt[0, caption], txt[1, caption]
                kk[i, at, :] = k
                vv[i, at, :] = v
                kt[i, :, at] = k.T
                vt[i, :, at] = v.T
            return carry

        lax.fori_loop(0, 3, prepare, 0)

        def query(r, carry):
            i = jnp.where(r >= first, 1, 0) + jnp.where(r >= second, 1, 0)
            j = jnp.minimum(r - begin_of(i), 2)
            tiles = mine[0, T_COUNT + i]
            length = plan[0, P_LENGTH + i]
            place = plan[0, ty * P_SIZE + P_IMAGE + i * 3 + j]
            q = pool[place, 0] * jnp.asarray(scale, bf16)
            do = pool[place, 3]
            k, v = kk[i], vv[i]
            hide = [0.0] + [jnp.where(n < tiles, 0.0, -1e30) for n in (1, 2)]
            hide.append(jnp.where(text_row < length, 0.0, -1e30))
            o_parts, dq_parts = [], []
            for h in range(2):
                scores = lax.dot_general(k, half(q, h), contract_lanes, preferred_element_type=f32)
                scores = jnp.concatenate(
                    [scores[n * TILE : (n + 1) * TILE] + hide[n] for n in range(4)], axis=0
                )
                weights = jnp.exp(scores - jnp.max(scores, axis=0, keepdims=True))
                probs = weights * (1.0 / jnp.sum(weights, axis=0, keepdims=True))
                dprobs = lax.dot_general(v, half(do, h), contract_lanes, preferred_element_type=f32)
                total = jnp.sum(probs * dprobs, axis=0, keepdims=True)
                dscores = (probs * (dprobs - total)).astype(bf16)
                low = probs.astype(bf16)
                for n in range(4):
                    ps[r, h, n] = low[n * TILE : (n + 1) * TILE]
                    ds[r, h, n] = dscores[n * TILE : (n + 1) * TILE]
                span = slice(h * HEAD_DIM, (h + 1) * HEAD_DIM)
                o_parts.append(jnp.dot(vt[i, span, :], low, preferred_element_type=f32))
                dq_parts.append(jnp.dot(kt[i, span, :], dscores, preferred_element_type=f32))
            o = jnp.concatenate(o_parts, axis=0).T
            dq = jnp.concatenate(dq_parts, axis=0).T * scale
            res[par, ty, r, 0] = o.astype(bf16)
            res[par, ty, r, 1] = dq.astype(bf16)
            return carry

        def query_three(r, carry):
            query(3 * r, carry)
            query(3 * r + 1, carry)
            return query(3 * r + 2, carry)

        lax.fori_loop(0, 2, query_three, 0)

        def key_grads(i, block):
            begin_i = begin_of(i)
            rows = [jnp.minimum(begin_i + n, 5) for n in range(3)]
            q, do = qm[i], dm[i]
            dk, dv = [], []
            for h in range(2):
                low = jnp.concatenate([ps[r, h, block] for r in rows], axis=1)
                dscores = jnp.concatenate([ds[r, h, block] for r in rows], axis=1)
                dk.append(jnp.dot(dscores, q, preferred_element_type=f32))
                dv.append(jnp.dot(low, do, preferred_element_type=f32))
            return jnp.where(lane, dk[0], dk[1]), jnp.where(lane, dv[0], dv[1])

        def key(r, carry):
            i = jnp.where(r >= first, 1, 0) + jnp.where(r >= second, 1, 0)
            dk, dv = key_grads(i, jnp.minimum(r - begin_of(i), 2))
            res[par, ty, r, 2] = dk.astype(bf16)
            res[par, ty, r, 3] = dv.astype(bf16)
            return carry

        def key_two(r, carry):
            key(2 * r, carry)
            return key(2 * r + 1, carry)

        lax.fori_loop(0, 3, key_two, 0)

        def caption_key(i, carry):
            dk, dv = key_grads(i, 3)
            tgrad[i, 0] = dk
            tgrad[i, 1] = dv
            return carry

        lax.fori_loop(0, 3, caption_key, 0)

        def spread(c, a):
            hits = [jnp.where(mine[0, T_CAPTION + i] == c, 1.0, 0.0) for i in range(3)]
            return tgrad[0, a] * hits[0] + tgrad[1, a] * hits[1] + tgrad[2, a] * hits[2]

        def settle(c, carry):
            for a in range(2):
                tsend[ty, c, a] = spread(c, a).astype(bf16)
            return carry

        lax.fori_loop(0, peers_grp, settle, 0)
        for a in range(2):
            tself[ty, a] = spread(g, a)

    def captions_in(pair, ty):
        def current(c, carry):
            for a in range(2):
                txt[a, c] = caps[pair, c, a, :, ty * LANES : (ty + 1) * LANES]
            return carry

        lax.fori_loop(0, peers_grp, current, 0)

    def work(pair, ty):
        final(0, pair, ty)
        captions_in(pair, ty)
        compute(pair, ty)
        first_send(1, pair, ty)
        for k in range(1, peers_grp):
            text_message(lax.rem(pair, 2), ty, k).start()

    def home(pair):
        @pl.when(pair > 0)
        def _():
            for copy in stores(pair - 1):
                copy.wait()

        for ty in range(2):
            final(1, pair, ty)

            def place(j, carry):
                at = pl.ds(pl.multiple_of(j * TILE, TILE), TILE)
                for a in range(4):
                    stage[ty, a, at, :] = pool[plan[0, ty * P_SIZE + P_HOME + j], a]
                return carry

            lax.fori_loop(0, 6, place, 0)
        for copy in stores(pair):
            copy.start()

    def add_captions(pair):
        par = lax.rem(pair, 2)
        for ty in range(2):
            for k in range(1, peers_grp):
                text_message(par, ty, k).wait()
            at = slice(ty * LANES, (ty + 1) * LANES)
            for a in range(2):
                total = tself[ty, a]
                for k in range(1, peers_grp):
                    total = total + trecv[par, ty, k - 1, a].astype(jnp.float32)
                tsum[a * TILE : (a + 1) * TILE, at] = total
                ttot[par, a * TILE : (a + 1) * TILE, at] = total.astype(ttot.dtype)
        for copy in sum_messages(par):
            copy.start()

    def end_captions(pair):
        par = lax.rem(pair, 2)
        for copy in sum_messages(par):
            copy.wait()
        at = pl.ds(pl.multiple_of(s * share, share), share)
        total = tsum[at, :]
        for k in range(1, peers_seq):
            total = total + tpart[par, k - 1].astype(jnp.float32)
        done = total.astype(tdone.dtype)
        tdone[pair] = done
        tall[pair, at, :] = done
        for copy in end_messages(pair):
            copy.start()

    for copy in loads(0):
        copy.start()
    own_rows = mine_rows[...]
    tab_seq[s] = own_rows
    tab_grp[g] = own_rows

    def publish(values, place):
        plan_rows[...] = values
        copy = pltpu.make_async_copy(plan_rows, place, plansem)
        copy.start()
        copy.wait()

    source = lax.broadcasted_iota(jnp.int32, (peers_seq, LANES), 0)
    alone = jnp.where(source == s, jnp.concatenate([own_rows] * (peers_seq // 8), axis=0), -1)
    publish(make_plan(alone, mine, None, s), plan_own)
    pl.semaphore_wait(barrier, peers_seq + peers_grp - 2)
    for copy in table_messages():
        copy.start()
    for copy in loads(0):
        copy.wait()
    for ty in range(2):
        first_send(0, jnp.int32(0), ty, plan_own)
    for pair in range(pairs):
        for copy in caption_messages(pair):
            copy.start()
    for copy in table_messages():
        copy.wait()
    publish(make_plan(tab_seq[:, 0, :], mine, tab_grp[:, 0, :], s), plan)

    for copy in loads(1):
        copy.start()

    def superstep(step, carry):
        entering = step < pairs
        working = (step >= 1) & (step <= pairs)
        leaving = step >= 2

        def following():
            for copy in loads(step + 1):
                copy.wait()
            for ty in range(2):
                first_send(0, step + 1, ty)

        @pl.when(entering)
        def _():
            pass_on(0, step)

        @pl.when(working)
        def _():
            for copy in caption_messages(step - 1):
                copy.wait()
            work(step - 1, 0)

        @pl.when(entering)
        def _():
            turn(0, step)

        @pl.when(leaving)
        def _():
            last_send(1, step - 2)

        @pl.when(working)
        def _():
            work(step - 1, 1)

        @pl.when(working)
        def _():
            pass_on(1, step - 1)

        @pl.when(entering)
        def _():
            last_send(0, step)

        @pl.when(leaving)
        def _():
            end_captions(step - 2)

        @pl.when((step >= 1) & (step + 1 < pairs))
        def _():
            for copy in loads(step + 1):
                copy.start()

        @pl.when(leaving)
        def _():
            home(step - 2)

        @pl.when(working)
        def _():
            add_captions(step - 1)

        @pl.when(step == 0)
        def _():
            following()

        @pl.when(working)
        def _():
            turn(1, step - 1)

        @pl.when((step >= 1) & (step + 1 < pairs))
        def _():
            following()

        return carry

    lax.fori_loop(0, pairs + 2, superstep, 0)
    sent(pairs - 1)
    for pair in range(pairs):
        for copy in end_messages(pair):
            copy.wait()
    for copy in caption_stores():
        copy.start()
    for copy in stores(pairs - 1):
        copy.wait()
    for copy in caption_stores():
        copy.wait()


def copy_kernel(*refs):
    count = len(refs) // 2
    for source, target in zip(refs[:count], refs[count:]):
        target[...] = source[...]


def body(
    image_queries,
    image_keys,
    image_values,
    cotangent,
    text_keys,
    text_values,
    text_lengths,
    send_owner,
    recv_source,
    tile_counts,
    caption_ids,
):
    rows, width = image_queries.shape
    peers_grp, peers_seq = lax.axis_size("grp"), lax.axis_size("seq")
    pairs = width // (2 * LANES)
    mine = jnp.concatenate(
        [send_owner[0], recv_source[0], tile_counts[0], caption_ids[0], text_lengths]
    ).astype(jnp.int32)
    mine = jnp.broadcast_to(jnp.pad(mine, (0, LANES - mine.shape[0]))[None, :], (8, LANES))
    vmem = pl.BlockSpec(memory_space=pltpu.VMEM)
    smem = pl.BlockSpec(memory_space=pltpu.SMEM)
    anywhere = pl.BlockSpec(memory_space=pl.ANY)
    bf16, f32 = jnp.bfloat16, jnp.float32
    quad = (4, TILE, LANES)
    text_rows = text_keys.shape[1]
    image = jax.ShapeDtypeStruct((rows, width), bf16)
    caption = jax.ShapeDtypeStruct(text_keys.shape, bf16)
    dma = pltpu.SemaphoreType.DMA
    scratch = [
        pltpu.VMEM((peers_seq, 8, LANES), jnp.int32),
        pltpu.VMEM((peers_grp, 8, LANES), jnp.int32),
        pltpu.VMEM((8, 2 * P_SIZE), jnp.int32),
        pltpu.SMEM((8, 2 * P_SIZE), jnp.int32),
        pltpu.SMEM((8, 2 * P_SIZE), jnp.int32),
        pltpu.VMEM((2, 2, 4, rows, LANES), bf16),
        pltpu.VMEM((pairs, peers_grp, 2, text_rows, 2 * LANES), bf16),
        pltpu.VMEM((2, peers_grp, text_rows, LANES), bf16),
        pltpu.VMEM((2, 2, 2, SLOTS) + quad, bf16),
        pltpu.VMEM((2 + pairs, 2, 2, SLOTS) + quad, bf16),
        pltpu.VMEM((2 + pairs, 2, 2, RELAY) + quad, bf16),
        pltpu.VMEM((2, 2, 2, SLOTS) + quad, bf16),
        pltpu.VMEM((4, 2, 2, SLOTS) + quad, bf16),
        pltpu.VMEM((2, 2, 2, RELAY) + quad, bf16),
        pltpu.VMEM((4, 2, 2, RELAY) + quad, bf16),
        pltpu.VMEM((POOL,) + quad, bf16),
        pltpu.VMEM((2, 2, 6) + quad, bf16),
        pltpu.VMEM((2, 4, rows, LANES), bf16),
        pltpu.VMEM((3, 4 * TILE, LANES), bf16),
        pltpu.VMEM((3, 4 * TILE, LANES), bf16),
        pltpu.VMEM((3, LANES, 4 * TILE), bf16),
        pltpu.VMEM((3, LANES, 4 * TILE), bf16),
        pltpu.VMEM((3, 3 * TILE, LANES), bf16),
        pltpu.VMEM((3, 3 * TILE, LANES), bf16),
        pltpu.VMEM((6, 2, 4, TILE, TILE), bf16),
        pltpu.VMEM((6, 2, 4, TILE, TILE), bf16),
        pltpu.VMEM((3, 2, TILE, LANES), f32),
        pltpu.VMEM((2, 2, text_rows, LANES), f32),
        pltpu.VMEM((2, peers_grp, 2, text_rows, LANES), bf16),
        pltpu.VMEM((2, 2, peers_grp - 1, 2, text_rows, LANES), bf16),
        pltpu.VMEM((2 * text_rows, 2 * LANES), f32),
        pltpu.VMEM((2, 2 * text_rows, 2 * LANES), bf16),
        pltpu.VMEM((2, peers_seq - 1, 2 * text_rows // peers_seq, 2 * LANES), bf16),
        pltpu.VMEM((pairs, 2 * text_rows // peers_seq, 2 * LANES), bf16),
        pltpu.VMEM((pairs, 2 * text_rows, 2 * LANES), bf16),
        dma((4 * (2 + pairs) * KINDS,)),
        dma((4 * (2 + pairs) * KINDS,)),
        dma((peers_seq + peers_grp - 2,)),
        dma((peers_seq + peers_grp - 2,)),
        dma((pairs * 2 * (peers_grp - 1),)),
        dma((pairs * 2 * (peers_grp - 1),)),
        dma((4 * (peers_grp - 1),)),
        dma((4 * (peers_grp - 1),)),
        dma((2 * (peers_seq - 1),)),
        dma((2 * (peers_seq - 1),)),
        dma((pairs * (peers_seq - 1),)),
        dma((pairs * (peers_seq - 1),)),
        dma((8 + 2 * pairs,)),
        dma((8 + 2 * pairs,)),
        dma,
    ]
    results = pl.pallas_call(
        functools.partial(main_kernel, peers_grp, peers_seq, pairs),
        out_shape=(image, image, image, image, caption, caption),
        in_specs=[smem, vmem] + [anywhere] * 6,
        out_specs=(anywhere,) * 6,
        scratch_shapes=scratch,
        compiler_params=pltpu.CompilerParams(
            collective_id=0, has_side_effects=True, vmem_limit_bytes=63 * 2**20
        ),
        name="attend",
    )(mine, mine, image_queries, image_keys, image_values, cotangent, text_keys, text_values)
    steps = 2
    blocks = [
        pl.BlockSpec((rows // steps, width), lambda i: (i, 0)),
        pl.BlockSpec((1, text_rows // steps, width), lambda i: (0, i, 0)),
    ]
    specs = [blocks[0]] * 4 + [blocks[1]] * 2
    return pl.pallas_call(
        copy_kernel,
        grid=(steps,),
        out_shape=(image, image, image, image, caption, caption),
        in_specs=specs,
        out_specs=tuple(specs),
        name="results",
    )(*results)


def solution(mesh):
    tokens = P(("grp", "seq"), None)
    captions = P("grp", None, None)
    return jax.shard_map(
        body,
        mesh=mesh,
        in_specs=(tokens,) * 4 + (captions, captions, P("grp")) + (tokens,) * 4,
        out_specs=(tokens,) * 4 + (captions, captions),
        check_vma=False,
    )
```

```python
import functools

import jax
import jax.numpy as jnp
from jax import lax
from jax.experimental import pallas as pl
from jax.experimental.pallas import tpu as pltpu
from jax.sharding import PartitionSpec as P

HEAD_DIM = 64
LANES = 128
TILE = 128
MESH = pl.DeviceIdType.MESH

RING = 4
SLOTS = 4
RELAY = 2

OWN = 0
DIRECT = 6
FORWARD = 14
FINAL = 18
PASSING = 26
POOL = 30

P_SEND = 0
P_MID = 8
P_LATE = 16
P_IMAGE = 20
P_BACK = 32
P_BACK_MID = 40
P_BACK_LATE = 48
P_HOME = 52
P_LENGTH = 58
P_SIZE = 64

T_RECV, T_COUNT, T_CAPTION, T_LENGTH = 6, 12, 15, 18

SEND, SEND_NEAR, PASS, MID, MID_NEAR, LATE = range(6)
KINDS = 6


def make_plan(tab, row_ref, lengths, me):
    peers = tab.shape[0]
    src = lax.broadcasted_iota(jnp.int32, (peers, LANES), 0)
    own = lax.broadcasted_iota(jnp.int32, (peers, LANES), 1)
    sends = jnp.zeros((peers, LANES), jnp.int32)
    place = jnp.zeros((peers, LANES), jnp.int32)
    for j in range(6):
        hit = (tab[:, j : j + 1] == own).astype(jnp.int32)
        sends += hit
        place += hit * j
    first = row_ref[0, T_COUNT]
    second = first + row_ref[0, T_COUNT + 1]
    result = jnp.zeros((peers, LANES), jnp.int32)
    for r in range(6):
        result += jnp.where(src == row_ref[0, T_RECV + r], r, 0)

    lower = (
        lax.broadcasted_iota(jnp.int32, (peers, peers), 1)
        < lax.broadcasted_iota(jnp.int32, (peers, peers), 0)
    ).astype(jnp.float32)
    upper = (
        lax.broadcasted_iota(jnp.int32, (LANES, LANES), 0)
        < lax.broadcasted_iota(jnp.int32, (LANES, LANES), 1)
    ).astype(jnp.float32)
    live = sends > 0
    coord = {"y": lambda t: lax.rem(t, RING), "z": lambda t: lax.div(t, RING) % RING}

    def slots(step, axis):
        count, rank = [], []
        for d in (1, 2, 3):
            picked = jnp.where(live & (step == d), 1.0, 0.0)
            if axis == 1:
                before = jnp.dot(picked, upper, preferred_element_type=jnp.float32)
            else:
                before = jnp.dot(lower, picked, preferred_element_type=jnp.float32)
            rank.append(before.astype(jnp.int32))
            count.append(jnp.sum(picked, axis=axis, keepdims=True).astype(jnp.int32))
        plus = jnp.minimum(jnp.minimum(RELAY, SLOTS - count[0]), count[1])
        code = jnp.where(
            step == 0,
            0,
            jnp.where(
                step == 1, 1, jnp.where(step == 3, 2, jnp.where(rank[1] < plus, 3, 4))
            ),
        )
        slot = jnp.where(
            code == 1,
            SLOTS - 1 - rank[0],
            jnp.where(
                code == 2,
                SLOTS - 1 - rank[2],
                jnp.where(code == 3, rank[1], rank[1] - plus),
            ),
        )
        return code, slot

    def arrived(code, slot, stay, flip):
        base = (DIRECT + SLOTS, DIRECT, FORWARD + RELAY, FORWARD) if flip else (
            DIRECT, DIRECT + SLOTS, FORWARD, FORWARD + RELAY)
        return jnp.where(
            code == 0,
            stay,
            slot
            + jnp.where(
                code == 1,
                base[0],
                jnp.where(code == 2, base[1], jnp.where(code == 3, base[2], base[3])),
            ),
        )

    def settled(code, slot, stay, flip):
        odd = (code == 1) | (code == 3)
        near, far = (FINAL + SLOTS, FINAL) if flip else (FINAL, FINAL + SLOTS)
        return jnp.where(code == 0, stay, slot + jnp.where(odd, near, far))

    zero_row = jnp.zeros((1, LANES), jnp.float32)
    rows = []
    for ring_a, ring_b in (("y", "z"), ("z", "y")):
        at_a, at_b = coord[ring_a], coord[ring_b]
        src_a, src_b, own_a, own_b = at_a(src), at_b(src), at_a(own), at_b(own)
        me_a, me_b = at_a(me), at_b(me)
        code_a, slot_a = slots(lax.rem(own_a - src_a + RING, RING), 1)
        code_b, slot_b = slots(lax.rem(own_b - src_b + RING, RING), 0)
        there = arrived(code_a, slot_a, place, False)
        there_end = settled(code_b, slot_b, there, False)
        back = arrived(code_b, slot_b, result, True)
        back_end = settled(code_a, slot_a, back, True)
        mine_src = live & (src == me)
        mine_own = live & (own == me)
        crossing = live & (own_a == me_a) & (src_b == me_b)
        part = {}

        def put(entry, condition, value):
            row = jnp.sum(
                jnp.where(condition, value, 0).astype(jnp.float32), axis=0, keepdims=True
            )
            part[entry] = part[entry] + row if entry in part else row

        def channel(code, sign, flip):
            sign = 1 - sign if flip else sign
            return (code == 1 + sign), (code == 3 + sign)

        for sign in (0, 1):
            ahead = 1 if sign == 0 else RING - 1
            near, far = channel(code_a, sign, False)
            for k in range(SLOTS):
                put(P_SEND + sign * SLOTS + k, mine_src & (near | far) & (slot_a == k), place)
            near, far = channel(code_b, sign, False)
            passing = live & (own_a == me_a) & far & (lax.rem(own_b - me_b + RING, RING) == ahead)
            for k in range(RELAY):
                put(P_MID + sign * SLOTS + k, crossing & far & (slot_b == k), there)
                put(P_LATE + sign * RELAY + k, crossing & near & (slot_b == k), there)
                put(P_LATE + sign * RELAY + k, passing & (slot_b == k), PASSING + sign * RELAY + k)
            for k in range(RELAY, SLOTS):
                put(P_MID + sign * SLOTS + k, crossing & near & (slot_b == k), there)
            near, far = channel(code_b, sign, True)
            for k in range(SLOTS):
                put(P_BACK + sign * SLOTS + k, mine_own & (near | far) & (slot_b == k), result)
            near, far = channel(code_a, sign, True)
            passing = live & (src_b == me_b) & far & (lax.rem(src_a - me_a + RING, RING) == ahead)
            for k in range(RELAY):
                put(P_BACK_MID + sign * SLOTS + k, crossing & far & (slot_a == k), back)
                put(P_BACK_LATE + sign * RELAY + k, crossing & near & (slot_a == k), back)
                put(P_BACK_LATE + sign * RELAY + k, passing & (slot_a == k), PASSING + sign * RELAY + k)
            for k in range(RELAY, SLOTS):
                put(P_BACK_MID + sign * SLOTS + k, crossing & near & (slot_a == k), back)
        begins = (0, first, second)
        for i in range(3):
            for j in range(3):
                r = jnp.minimum(begins[i] + j, 5)
                put(P_IMAGE + i * 3 + j, mine_own & (src == row_ref[0, T_RECV + r]), there_end)
        for j in range(6):
            put(P_HOME + j, mine_src & (place == j), back_end)
        if lengths is not None:
            captions = lax.broadcasted_iota(jnp.int32, lengths.shape, 0)
            column = lax.broadcasted_iota(jnp.int32, lengths.shape, 1) == T_LENGTH
            for i in range(3):
                put(P_LENGTH + i, column & (captions == row_ref[0, T_CAPTION + i]), lengths)
        rows.extend(part.get(entry, zero_row) for entry in range(P_SIZE))
    matrix = jnp.concatenate(rows, axis=0)
    ones = jnp.ones((8, LANES), jnp.float32)
    out = lax.dot_general(ones, matrix, (((1,), (1,)), ((), ())), preferred_element_type=jnp.float32)
    out = out.astype(jnp.int32)
    entry = lax.broadcasted_iota(jnp.int32, out.shape, 1) % P_SIZE
    return jnp.where(entry < P_LENGTH, jnp.clip(out, 0, POOL - 1), out)


def main_kernel(
    peers_grp,
    peers_seq,
    pairs,
    mine,
    mine_rows,
    queries,
    keys,
    values,
    grads,
    cap_keys,
    cap_values,
    out_rows,
    out_queries,
    out_keys,
    out_values,
    out_cap_keys,
    out_cap_values,
    tab_seq,
    tab_grp,
    plan_rows,
    plan_own,
    plan,
    inb,
    caps,
    txt,
    send_a,
    recv_a,
    recv_p,
    send_m,
    recv_m,
    send_l,
    recv_l,
    pool,
    res,
    stage,
    kk,
    vv,
    kt,
    vt,
    qm,
    dm,
    ps,
    ds,
    tgrad,
    tself,
    tsend,
    trecv,
    tsum,
    ttot,
    tpart,
    tdone,
    tall,
    ssem,
    rsem,
    tabssem,
    tabrsem,
    capssem,
    caprsem,
    tssem,
    trsem,
    sumssem,
    sumrsem,
    endssem,
    endrsem,
    insem,
    outsem,
    plansem,
):
    g = lax.axis_index("grp")
    s = lax.axis_index("seq")
    z, y = lax.div(s, RING), lax.rem(s, RING)
    sources = (queries, keys, values, grads)
    outs = (out_rows, out_queries, out_keys, out_values)

    def neighbour(ring, sign):
        step = 1 if sign == 0 else RING - 1
        if ring == "y":
            return (g, z * RING + lax.rem(y + step, RING))
        return (g, lax.rem(z + step, RING) * RING + y)

    def group_peer(k):
        return lax.rem(g + k, peers_grp)

    def seq_peer(k):
        return lax.rem(s + k, peers_seq)

    barrier = pltpu.get_barrier_semaphore()
    for k in range(1, peers_seq):
        pl.semaphore_signal(barrier, inc=1, device_id=(g, seq_peer(k)), device_id_type=MESH)
    for k in range(1, peers_grp):
        pl.semaphore_signal(barrier, inc=1, device_id=(group_peer(k), s), device_id_type=MESH)

    def first_ring(io, pair):
        return 2 + pair if io else lax.rem(pair, 2)

    def second_ring(io, pair):
        return io * 2 + lax.rem(pair, 2)

    def message(io, pair, ty, sign, kind):
        ring = "y" if (ty + io + (1 if kind >= MID else 0)) % 2 == 0 else "z"
        far, near = pl.ds(0, RELAY), pl.ds(RELAY, SLOTS - RELAY)
        one, two = first_ring(io, pair), second_ring(io, pair)
        if kind in (SEND, SEND_NEAR):
            at = far if kind == SEND else near
            src, dst = send_a.at[io, ty, sign, at], recv_a.at[one, ty, sign, at]
        elif kind == PASS:
            src, dst = recv_a.at[one, ty, sign, far], recv_p.at[one, ty, sign]
        elif kind in (MID, MID_NEAR):
            at = far if kind == MID else near
            src, dst = send_m.at[io, ty, sign, at], recv_m.at[two, ty, sign, at]
        else:
            src, dst = send_l.at[io, ty, sign], recv_l.at[two, ty, sign]
        index = ((one * 2 + ty) * 2 + sign) * KINDS + kind
        return pltpu.make_async_remote_copy(
            src_ref=src,
            dst_ref=dst,
            send_sem=ssem.at[index],
            recv_sem=rsem.at[index],
            device_id=neighbour(ring, sign),
            device_id_type=MESH,
        )

    def text_message(par, ty, k):
        index = (par * 2 + ty) * (peers_grp - 1) + k - 1
        target = group_peer(k)
        return pltpu.make_async_remote_copy(
            src_ref=tsend.at[ty, target],
            dst_ref=trecv.at[par, ty, k - 1],
            send_sem=tssem.at[index],
            recv_sem=trsem.at[index],
            device_id=(target, s),
            device_id_type=MESH,
        )

    def table_messages():
        copies = []
        for k in range(1, peers_seq + peers_grp - 1):
            seq = k < peers_seq
            copies.append(
                pltpu.make_async_remote_copy(
                    src_ref=mine_rows,
                    dst_ref=tab_seq.at[s] if seq else tab_grp.at[g],
                    send_sem=tabssem.at[k - 1],
                    recv_sem=tabrsem.at[k - 1],
                    device_id=(g, seq_peer(k)) if seq else (group_peer(k - peers_seq + 1), s),
                    device_id_type=MESH,
                )
            )
        return copies

    def caption_messages(pair):
        copies = []
        for a, cap in enumerate((cap_keys, cap_values)):
            src = cap.at[0, :, wide(pair)]
            dst = caps.at[pair, g, a]
            for k in range(1, peers_grp):
                index = (pair * 2 + a) * (peers_grp - 1) + k - 1
                copies.append(
                    pltpu.make_async_remote_copy(
                        src_ref=src,
                        dst_ref=dst,
                        send_sem=capssem.at[index],
                        recv_sem=caprsem.at[index],
                        device_id=(group_peer(k), s),
                        device_id_type=MESH,
                    )
                )
            copies.append(pltpu.make_async_copy(src, dst, insem.at[8 + pair * 2 + a]))
        return copies

    share = 16

    def sum_messages(par):
        copies = []
        for k in range(1, peers_seq):
            target = seq_peer(k)
            index = par * (peers_seq - 1) + k - 1
            copies.append(
                pltpu.make_async_remote_copy(
                    src_ref=ttot.at[par, pl.ds(pl.multiple_of(target * share, share), share)],
                    dst_ref=tpart.at[par, k - 1],
                    send_sem=sumssem.at[index],
                    recv_sem=sumrsem.at[index],
                    device_id=(g, target),
                    device_id_type=MESH,
                )
            )
        return copies

    def end_messages(pair):
        copies = []
        at = pl.ds(pl.multiple_of(s * share, share), share)
        for k in range(1, peers_seq):
            index = pair * (peers_seq - 1) + k - 1
            copies.append(
                pltpu.make_async_remote_copy(
                    src_ref=tdone.at[pair],
                    dst_ref=tall.at[pair, at],
                    send_sem=endssem.at[index],
                    recv_sem=endrsem.at[index],
                    device_id=(g, seq_peer(k)),
                    device_id_type=MESH,
                )
            )
        return copies

    def wide(pair):
        return pl.ds(pl.multiple_of(pair * (2 * LANES), 2 * LANES), 2 * LANES)

    def columns(pair, ty):
        return pl.ds(pl.multiple_of((pair * 2 + ty) * LANES, LANES), LANES)

    def loads(pair):
        par = lax.rem(pair, 2)
        copies = []
        for ty in range(2):
            for a in range(4):
                copies.append(
                    pltpu.make_async_copy(
                        sources[a].at[:, columns(pair, ty)], inb.at[par, ty, a], insem.at[ty * 4 + a]
                    )
                )
        return copies

    def stores(pair):
        copies = []
        for ty in range(2):
            for a in range(4):
                copies.append(
                    pltpu.make_async_copy(
                        stage.at[ty, a], outs[a].at[:, columns(pair, ty)], outsem.at[ty * 4 + a]
                    )
                )
        return copies

    def caption_stores():
        rows = tall.shape[1] // 2
        copies = []
        for pair in range(pairs):
            for a, out in enumerate((out_cap_keys, out_cap_values)):
                copies.append(
                    pltpu.make_async_copy(
                        tall.at[pair, pl.ds(a * rows, rows)],
                        out.at[0, :, wide(pair)],
                        outsem.at[8 + pair * 2 + a],
                    )
                )
        return copies

    def fill(base, count, read):
        def step(k, carry):
            pool[base + 2 * k] = read(2 * k)
            pool[base + 2 * k + 1] = read(2 * k + 1)
            return carry

        lax.fori_loop(0, count // 2, step, 0)

    def fill_own(io, pair, ty):
        par = lax.rem(pair, 2)
        if io:
            fill(OWN, 6, lambda k: res[par, ty, k])
            return

        def step(j, carry):
            at = pl.ds(pl.multiple_of(j * TILE, TILE), TILE)
            for a in range(4):
                pool[OWN + j, a] = inb[par, ty, a, at, :]
            return carry

        lax.fori_loop(0, 6, step, 0)

    def fill_arrived(io, pair, ty):
        one = first_ring(io, pair)
        for sign in range(2):
            fill(DIRECT + sign * SLOTS, SLOTS, lambda k: recv_a[one, ty, sign, k])
            fill(FORWARD + sign * RELAY, RELAY, lambda k: recv_p[one, ty, sign, k])

    def fill_passing(io, pair, ty):
        two = second_ring(io, pair)
        for sign in range(2):
            fill(PASSING + sign * RELAY, RELAY, lambda k: recv_m[two, ty, sign, k])

    def fill_final(io, pair, ty):
        two = second_ring(io, pair)
        for sign in range(2):
            fill(FINAL + sign * SLOTS, RELAY, lambda k: recv_l[two, ty, sign, k])
            fill(
                FINAL + sign * SLOTS + RELAY,
                SLOTS - RELAY,
                lambda k: recv_m[two, ty, sign, RELAY + k],
            )

    def choose(ref, io, ty, entry, count, first, last, table=plan):
        for sign in range(2):

            def step(k, carry):
                ref[io, ty, sign, k] = pool[table[0, ty * P_SIZE + entry + sign * count + k]]
                return carry

            lax.fori_loop(first, last, step, 0)

    def begin(io, pair, ty, kind):
        for sign in range(2):
            message(io, pair, ty, sign, kind).start()

    def finish(io, pair, ty, kind):
        for sign in range(2):
            message(io, pair, ty, sign, kind).wait()

    def first_send(io, pair, ty, table=plan):
        fill_own(io, pair, ty)
        entry = P_BACK if io else P_SEND
        choose(send_a, io, ty, entry, SLOTS, 0, RELAY, table)
        begin(io, pair, ty, SEND)
        choose(send_a, io, ty, entry, SLOTS, RELAY, SLOTS, table)
        begin(io, pair, ty, SEND_NEAR)

    def pass_on(io, pair):
        for ty in range(2):
            finish(io, pair, ty, SEND)
            begin(io, pair, ty, PASS)

    def turn(io, pair):
        for ty in range(2):
            finish(io, pair, ty, SEND_NEAR)
            finish(io, pair, ty, PASS)
            if io == 0 and ty == 1:
                @pl.when(pair > 0)
                def _():
                    sent(pair - 1)

            fill_own(io, pair, ty)
            fill_arrived(io, pair, ty)
            entry = P_BACK_MID if io else P_MID
            choose(send_m, io, ty, entry, SLOTS, 0, RELAY)
            begin(io, pair, ty, MID)
            choose(send_m, io, ty, entry, SLOTS, RELAY, SLOTS)
            begin(io, pair, ty, MID_NEAR)

    def last_send(io, pair):
        for ty in range(2):
            finish(io, pair, ty, MID)
            fill_own(io, pair, ty)
            fill_arrived(io, pair, ty)
            fill_passing(io, pair, ty)
            choose(send_l, io, ty, P_BACK_LATE if io else P_LATE, RELAY, 0, RELAY)
            begin(io, pair, ty, LATE)

    def sent(pair):
        for sign in range(2):
            message(0, pair, 1, sign, MID_NEAR).wait_send()

    def final(io, pair, ty):
        if io == 0 and ty == 1:
            for sign in range(2):
                message(io, pair, ty, sign, MID_NEAR).wait_recv()
        else:
            finish(io, pair, ty, MID_NEAR)
        finish(io, pair, ty, LATE)
        fill_own(io, pair, ty)
        fill_arrived(io, pair, ty)
        fill_final(io, pair, ty)

    def compute(pair, ty):
        par = lax.rem(pair, 2)
        bf16, f32 = jnp.bfloat16, jnp.float32
        scale = HEAD_DIM**-0.5
        lane = lax.broadcasted_iota(jnp.int32, (TILE, LANES), 1) < HEAD_DIM
        text_row = lax.broadcasted_iota(jnp.int32, (TILE, LANES), 0)
        contract_lanes = (((1,), (1,)), ((), ()))
        first = mine[0, T_COUNT]
        second = first + mine[0, T_COUNT + 1]
        text = 3 * TILE

        def begin_of(i):
            return jnp.where(i == 0, 0, jnp.where(i == 1, first, second))

        def half(tile, h):
            return jnp.where(lane if h == 0 else jnp.logical_not(lane), tile, jnp.zeros_like(tile))

        def prepare(i, carry):
            tiles = mine[0, T_COUNT + i]
            caption = mine[0, T_CAPTION + i]
            for j in range(4):
                at = slice(j * TILE, (j + 1) * TILE)
                if j < 3:
                    place = plan[0, ty * P_SIZE + P_IMAGE + i * 3 + j]
                    k, v = pool[place, 1], pool[place, 2]
                    live = jnp.where(j < tiles, 1.0, 0.0)
                    qm[i, at, :] = (pool[place, 0].astype(f32) * (live * scale)).astype(bf16)
                    dm[i, at, :] = (pool[place, 3].astype(f32) * live).astype(bf16)
                else:
                    k, v = txt[0, caption], txt[1, caption]
                kk[i, at, :] = k
                vv[i, at, :] = v
                kt[i, :, at] = k.T
                vt[i, :, at] = v.T
            return carry

        lax.fori_loop(0, 3, prepare, 0)

        def query(r, carry):
            i = jnp.where(r >= first, 1, 0) + jnp.where(r >= second, 1, 0)
            j = jnp.minimum(r - begin_of(i), 2)
            tiles = mine[0, T_COUNT + i]
            length = plan[0, P_LENGTH + i]
            place = plan[0, ty * P_SIZE + P_IMAGE + i * 3 + j]
            q = pool[place, 0] * jnp.asarray(scale, bf16)
            do = pool[place, 3]
            k, v = kk[i], vv[i]
            hide = [0.0] + [jnp.where(n < tiles, 0.0, -1e30) for n in (1, 2)]
            hide.append(jnp.where(text_row < length, 0.0, -1e30))
            o_parts, dq_parts = [], []
            for h in range(2):
                scores = lax.dot_general(k, half(q, h), contract_lanes, preferred_element_type=f32)
                scores = jnp.concatenate(
                    [scores[n * TILE : (n + 1) * TILE] + hide[n] for n in range(4)], axis=0
                )
                weights = jnp.exp(scores - jnp.max(scores, axis=0, keepdims=True))
                probs = weights * (1.0 / jnp.sum(weights, axis=0, keepdims=True))
                dprobs = lax.dot_general(v, half(do, h), contract_lanes, preferred_element_type=f32)
                total = jnp.sum(probs * dprobs, axis=0, keepdims=True)
                dscores = (probs * (dprobs - total)).astype(bf16)
                low = probs.astype(bf16)
                for n in range(4):
                    ps[r, h, n] = low[n * TILE : (n + 1) * TILE]
                    ds[r, h, n] = dscores[n * TILE : (n + 1) * TILE]
                span = slice(h * HEAD_DIM, (h + 1) * HEAD_DIM)
                o_parts.append(jnp.dot(vt[i, span, :], low, preferred_element_type=f32))
                dq_parts.append(jnp.dot(kt[i, span, :], dscores, preferred_element_type=f32))
            o = jnp.concatenate(o_parts, axis=0).T
            dq = jnp.concatenate(dq_parts, axis=0).T * scale
            res[par, ty, r, 0] = o.astype(bf16)
            res[par, ty, r, 1] = dq.astype(bf16)
            return carry

        def query_three(r, carry):
            query(3 * r, carry)
            query(3 * r + 1, carry)
            return query(3 * r + 2, carry)

        lax.fori_loop(0, 2, query_three, 0)

        def key_grads(i, block):
            begin_i = begin_of(i)
            rows = [jnp.minimum(begin_i + n, 5) for n in range(3)]
            q, do = qm[i], dm[i]
            dk, dv = [], []
            for h in range(2):
                low = jnp.concatenate([ps[r, h, block] for r in rows], axis=1)
                dscores = jnp.concatenate([ds[r, h, block] for r in rows], axis=1)
                dk.append(jnp.dot(dscores, q, preferred_element_type=f32))
                dv.append(jnp.dot(low, do, preferred_element_type=f32))
            return jnp.where(lane, dk[0], dk[1]), jnp.where(lane, dv[0], dv[1])

        def key(r, carry):
            i = jnp.where(r >= first, 1, 0) + jnp.where(r >= second, 1, 0)
            dk, dv = key_grads(i, jnp.minimum(r - begin_of(i), 2))
            res[par, ty, r, 2] = dk.astype(bf16)
            res[par, ty, r, 3] = dv.astype(bf16)
            return carry

        def key_two(r, carry):
            key(2 * r, carry)
            return key(2 * r + 1, carry)

        lax.fori_loop(0, 3, key_two, 0)

        def caption_key(i, carry):
            dk, dv = key_grads(i, 3)
            tgrad[i, 0] = dk
            tgrad[i, 1] = dv
            return carry

        lax.fori_loop(0, 3, caption_key, 0)

        def spread(c, a):
            hits = [jnp.where(mine[0, T_CAPTION + i] == c, 1.0, 0.0) for i in range(3)]
            return tgrad[0, a] * hits[0] + tgrad[1, a] * hits[1] + tgrad[2, a] * hits[2]

        def settle(c, carry):
            for a in range(2):
                tsend[ty, c, a] = spread(c, a).astype(bf16)
            return carry

        lax.fori_loop(0, peers_grp, settle, 0)
        for a in range(2):
            tself[ty, a] = spread(g, a)

    def captions_in(pair, ty):
        def current(c, carry):
            for a in range(2):
                txt[a, c] = caps[pair, c, a, :, ty * LANES : (ty + 1) * LANES]
            return carry

        lax.fori_loop(0, peers_grp, current, 0)

    def work(pair, ty):
        final(0, pair, ty)
        captions_in(pair, ty)
        compute(pair, ty)
        first_send(1, pair, ty)
        for k in range(1, peers_grp):
            text_message(lax.rem(pair, 2), ty, k).start()

    def home(pair):
        @pl.when(pair > 0)
        def _():
            for copy in stores(pair - 1):
                copy.wait()

        for ty in range(2):
            final(1, pair, ty)

            def place(j, carry):
                at = pl.ds(pl.multiple_of(j * TILE, TILE), TILE)
                for a in range(4):
                    stage[ty, a, at, :] = pool[plan[0, ty * P_SIZE + P_HOME + j], a]
                return carry

            lax.fori_loop(0, 6, place, 0)
        for copy in stores(pair):
            copy.start()

    def add_captions(pair):
        par = lax.rem(pair, 2)
        for ty in range(2):
            for k in range(1, peers_grp):
                text_message(par, ty, k).wait()
            at = slice(ty * LANES, (ty + 1) * LANES)
            for a in range(2):
                total = tself[ty, a]
                for k in range(1, peers_grp):
                    total = total + trecv[par, ty, k - 1, a].astype(jnp.float32)
                tsum[a * TILE : (a + 1) * TILE, at] = total
                ttot[par, a * TILE : (a + 1) * TILE, at] = total.astype(ttot.dtype)
        for copy in sum_messages(par):
            copy.start()

    def end_captions(pair):
        par = lax.rem(pair, 2)
        for copy in sum_messages(par):
            copy.wait()
        at = pl.ds(pl.multiple_of(s * share, share), share)
        total = tsum[at, :]
        for k in range(1, peers_seq):
            total = total + tpart[par, k - 1].astype(jnp.float32)
        done = total.astype(tdone.dtype)
        tdone[pair] = done
        tall[pair, at, :] = done
        for copy in end_messages(pair):
            copy.start()

    for copy in loads(0):
        copy.start()
    own_rows = mine_rows[...]
    tab_seq[s] = own_rows
    tab_grp[g] = own_rows

    def publish(values, place):
        plan_rows[...] = values
        copy = pltpu.make_async_copy(plan_rows, place, plansem)
        copy.start()
        copy.wait()

    source = lax.broadcasted_iota(jnp.int32, (peers_seq, LANES), 0)
    alone = jnp.where(source == s, jnp.concatenate([own_rows] * (peers_seq // 8), axis=0), -1)
    publish(make_plan(alone, mine, None, s), plan_own)
    pl.semaphore_wait(barrier, peers_seq + peers_grp - 2)
    for copy in table_messages():
        copy.start()
    for copy in loads(0):
        copy.wait()
    for ty in range(2):
        first_send(0, jnp.int32(0), ty, plan_own)
    for pair in range(pairs):
        for copy in caption_messages(pair):
            copy.start()
    for copy in table_messages():
        copy.wait()
    publish(make_plan(tab_seq[:, 0, :], mine, tab_grp[:, 0, :], s), plan)

    for copy in loads(1):
        copy.start()

    def superstep(step, carry):
        entering = step < pairs
        working = (step >= 1) & (step <= pairs)
        leaving = step >= 2

        def following():
            for copy in loads(step + 1):
                copy.wait()
            for ty in range(2):
                first_send(0, step + 1, ty)

        @pl.when(step > pairs)
        def _():
            end_captions(pairs - 1)

        @pl.when(entering)
        def _():
            pass_on(0, step)

        @pl.when(working)
        def _():
            for copy in caption_messages(step - 1):
                copy.wait()
            work(step - 1, 0)

        @pl.when(entering)
        def _():
            turn(0, step)

        @pl.when(leaving)
        def _():
            last_send(1, step - 2)

        @pl.when(working)
        def _():
            work(step - 1, 1)

        @pl.when(working)
        def _():
            pass_on(1, step - 1)

        @pl.when(entering)
        def _():
            last_send(0, step)

        @pl.when(leaving & (step <= pairs))
        def _():
            end_captions(step - 2)

        @pl.when((step >= 1) & (step + 1 < pairs))
        def _():
            for copy in loads(step + 1):
                copy.start()

        @pl.when(leaving)
        def _():
            home(step - 2)

        @pl.when(working)
        def _():
            add_captions(step - 1)

        @pl.when(step == 0)
        def _():
            following()

        @pl.when(working)
        def _():
            turn(1, step - 1)

        @pl.when((step >= 1) & (step + 1 < pairs))
        def _():
            following()

        return carry

    lax.fori_loop(0, pairs + 2, superstep, 0)
    sent(pairs - 1)
    for pair in range(pairs):
        for copy in end_messages(pair):
            copy.wait()
    for copy in caption_stores():
        copy.start()
    for copy in stores(pairs - 1):
        copy.wait()
    for copy in caption_stores():
        copy.wait()


def copy_kernel(*refs):
    count = len(refs) // 2
    for source, target in zip(refs[:count], refs[count:]):
        target[...] = source[...]


def body(
    image_queries,
    image_keys,
    image_values,
    cotangent,
    text_keys,
    text_values,
    text_lengths,
    send_owner,
    recv_source,
    tile_counts,
    caption_ids,
):
    rows, width = image_queries.shape
    peers_grp, peers_seq = lax.axis_size("grp"), lax.axis_size("seq")
    pairs = width // (2 * LANES)
    mine = jnp.concatenate(
        [send_owner[0], recv_source[0], tile_counts[0], caption_ids[0], text_lengths]
    ).astype(jnp.int32)
    mine = jnp.broadcast_to(jnp.pad(mine, (0, LANES - mine.shape[0]))[None, :], (8, LANES))
    vmem = pl.BlockSpec(memory_space=pltpu.VMEM)
    smem = pl.BlockSpec(memory_space=pltpu.SMEM)
    anywhere = pl.BlockSpec(memory_space=pl.ANY)
    bf16, f32 = jnp.bfloat16, jnp.float32
    quad = (4, TILE, LANES)
    text_rows = text_keys.shape[1]
    image = jax.ShapeDtypeStruct((rows, width), bf16)
    caption = jax.ShapeDtypeStruct(text_keys.shape, bf16)
    dma = pltpu.SemaphoreType.DMA
    scratch = [
        pltpu.VMEM((peers_seq, 8, LANES), jnp.int32),
        pltpu.VMEM((peers_grp, 8, LANES), jnp.int32),
        pltpu.VMEM((8, 2 * P_SIZE), jnp.int32),
        pltpu.SMEM((8, 2 * P_SIZE), jnp.int32),
        pltpu.SMEM((8, 2 * P_SIZE), jnp.int32),
        pltpu.VMEM((2, 2, 4, rows, LANES), bf16),
        pltpu.VMEM((pairs, peers_grp, 2, text_rows, 2 * LANES), bf16),
        pltpu.VMEM((2, peers_grp, text_rows, LANES), bf16),
        pltpu.VMEM((2, 2, 2, SLOTS) + quad, bf16),
        pltpu.VMEM((2 + pairs, 2, 2, SLOTS) + quad, bf16),
        pltpu.VMEM((2 + pairs, 2, 2, RELAY) + quad, bf16),
        pltpu.VMEM((2, 2, 2, SLOTS) + quad, bf16),
        pltpu.VMEM((4, 2, 2, SLOTS) + quad, bf16),
        pltpu.VMEM((2, 2, 2, RELAY) + quad, bf16),
        pltpu.VMEM((4, 2, 2, RELAY) + quad, bf16),
        pltpu.VMEM((POOL,) + quad, bf16),
        pltpu.VMEM((2, 2, 6) + quad, bf16),
        pltpu.VMEM((2, 4, rows, LANES), bf16),
        pltpu.VMEM((3, 4 * TILE, LANES), bf16),
        pltpu.VMEM((3, 4 * TILE, LANES), bf16),
        pltpu.VMEM((3, LANES, 4 * TILE), bf16),
        pltpu.VMEM((3, LANES, 4 * TILE), bf16),
        pltpu.VMEM((3, 3 * TILE, LANES), bf16),
        pltpu.VMEM((3, 3 * TILE, LANES), bf16),
        pltpu.VMEM((6, 2, 4, TILE, TILE), bf16),
        pltpu.VMEM((6, 2, 4, TILE, TILE), bf16),
        pltpu.VMEM((3, 2, TILE, LANES), f32),
        pltpu.VMEM((2, 2, text_rows, LANES), f32),
        pltpu.VMEM((2, peers_grp, 2, text_rows, LANES), bf16),
        pltpu.VMEM((2, 2, peers_grp - 1, 2, text_rows, LANES), bf16),
        pltpu.VMEM((2 * text_rows, 2 * LANES), f32),
        pltpu.VMEM((2, 2 * text_rows, 2 * LANES), bf16),
        pltpu.VMEM((2, peers_seq - 1, 2 * text_rows // peers_seq, 2 * LANES), bf16),
        pltpu.VMEM((pairs, 2 * text_rows // peers_seq, 2 * LANES), bf16),
        pltpu.VMEM((pairs, 2 * text_rows, 2 * LANES), bf16),
        dma((4 * (2 + pairs) * KINDS,)),
        dma((4 * (2 + pairs) * KINDS,)),
        dma((peers_seq + peers_grp - 2,)),
        dma((peers_seq + peers_grp - 2,)),
        dma((pairs * 2 * (peers_grp - 1),)),
        dma((pairs * 2 * (peers_grp - 1),)),
        dma((4 * (peers_grp - 1),)),
        dma((4 * (peers_grp - 1),)),
        dma((2 * (peers_seq - 1),)),
        dma((2 * (peers_seq - 1),)),
        dma((pairs * (peers_seq - 1),)),
        dma((pairs * (peers_seq - 1),)),
        dma((8 + 2 * pairs,)),
        dma((8 + 2 * pairs,)),
        dma,
    ]
    results = pl.pallas_call(
        functools.partial(main_kernel, peers_grp, peers_seq, pairs),
        out_shape=(image, image, image, image, caption, caption),
        in_specs=[smem, vmem] + [anywhere] * 6,
        out_specs=(anywhere,) * 6,
        scratch_shapes=scratch,
        compiler_params=pltpu.CompilerParams(
            collective_id=0, has_side_effects=True, vmem_limit_bytes=63 * 2**20
        ),
        name="attend",
    )(mine, mine, image_queries, image_keys, image_values, cotangent, text_keys, text_values)
    steps = 2
    blocks = [
        pl.BlockSpec((rows // steps, width), lambda i: (i, 0)),
        pl.BlockSpec((1, text_rows // steps, width), lambda i: (0, i, 0)),
    ]
    specs = [blocks[0]] * 4 + [blocks[1]] * 2
    return pl.pallas_call(
        copy_kernel,
        grid=(steps,),
        out_shape=(image, image, image, image, caption, caption),
        in_specs=specs,
        out_specs=tuple(specs),
        name="results",
    )(*results)


def solution(mesh):
    tokens = P(("grp", "seq"), None)
    captions = P("grp", None, None)
    return jax.shard_map(
        body,
        mesh=mesh,
        in_specs=(tokens,) * 4 + (captions, captions, P("grp")) + (tokens,) * 4,
        out_specs=(tokens,) * 4 + (captions, captions),
        check_vma=False,
    )
```
